32 devices in a mesh: replica: 2 (over y), tp: 16 (over z, x, core).
Axes of the slice: x: 2, y: 2, z: 4, core: 2. Of those that a mesh axis runs over, the one named last changes fastest.
Arguments:
- residual: bfloat16 [256, 16384], P('replica', 'tp'), parts along dimension 0, may hold values from -0.59765625 to 0.59765625
- attn_gain: bfloat16 [16384], replicated, may hold values from 0.25 to 1.75
- ffn_gain: bfloat16 [16384], replicated, may hold values from 0.099609375 to 1.8984375
- q_weight: bfloat16 [16384, 2048], P(None, 'tp'), may hold values from -0.046875 to 0.046875
- kv_weight: bfloat16 [16384, 2048], P(None, 'tp'), may hold values from -0.046875 to 0.046875
- o_weight: bfloat16 [2048, 16384], P('tp'), may hold values from -0.1875 to 0.1875
- key_cache: bfloat16 [4, 1024, 1024], P('replica', 'tp'), parts along dimension 0, may hold values from -260 to 260
- value_cache: bfloat16 [4, 1024, 1024], P('replica', 'tp'), parts along dimension 0, may hold values from -12 to 12
- prefix: int32 [4], P('replica'), parts along dimension 0, may hold values from 256 to 1024, as said below
Outputs:
- ffn_input: bfloat16 [256, 16384], P('replica'), parts along dimension 0
The draws below stay inside these ranges and needn't reach their ends.
There are 2 independent parts, one for each index of `replica`. The reference program is written for one: setup_inputs(seed, part) draws one part's arguments, and reference() takes and returns one part's arrays. A program takes and returns all parts, laid end to end along the dimension named above; an argument that names none is the same for every part. Nothing has to cross between parts.
Inputs may be any that keep to these rules, and one draw needn't show every extreme that they name: `prefix`: the first sequence's cache is full, 1024; the others hold 256 to 1024 positions.
All inputs are finite; a program needn't handle non-finite values.
Results may differ from the reference program's by a relative error of at most 0.012.
The reference program's roundings to bfloat16 on the way count: a program that leaves them out, or rounds other values in their place, can miss the bound.
Values may be sent and summed in bfloat16 or wider, within the bound.
No kernel may reach another device: no remote copies, remote signals or barrier semaphores. Data moves between devices by JAX's collectives and lax.ppermute only.
A program may use at most 128 MiB of HBM per device.

```python
import jax
import jax.numpy as jnp
from jax import lax

D = 16384
HD = 128
KVH = 8
SPAN = 64
SEQS = 2
HQ = 16
CTX = 1024
TOKENS = 128


def draw_key_cache(key, part):
    key = jax.random.fold_in(key, 11)
    base_draw = jax.random.normal(jax.random.fold_in(key, 1), (SEQS, CTX, KVH * HD), jnp.float32)
    return base_draw.astype(jnp.bfloat16)


def draw_prefix(key, part):
    key = jax.random.fold_in(key, 5)
    lengths = jax.random.randint(key, (SEQS,), CTX // 4, CTX + 1, dtype=jnp.int32)
    return lengths.at[0].set(CTX)


def strengthened(values, rng, source, target, shards_of, factor):
    owner, partner = [(jnp.arange(values.shape[axis_at]) // (values.shape[axis_at] // shards_of)).reshape([-1 if axis == axis_at else 1 for axis in range(values.ndim)]) for axis_at in (source, target)]
    chosen = jax.random.permutation(rng, shards_of)[partner]
    strong = (owner == chosen) | (owner == (partner + shards_of // 2) % shards_of)
    return jnp.where(strong, factor * values, values)


def block_scale(own_key, dims, pieces, least, largest):
    def one(position, blocks):
        draws = jax.random.uniform(jax.random.fold_in(jax.random.fold_in(own_key, 6), position), (blocks,), jnp.float32, least / len(pieces), largest / len(pieces))
        return jnp.repeat(jnp.exp(draws), dims[position] // blocks).reshape((-1,) + (1,) * (len(dims) - position - 1))

    level = one(*pieces[0])
    for cut in pieces[1:]:
        level = level * one(*cut)
    return level


def centred(own_key, extent, width, most, pieces=(), kind=jnp.bfloat16):
    level = block_scale(own_key, extent, pieces, -0.22, 0.18) if pieces else 1.0
    result = jax.random.normal(own_key, extent, jnp.float32) * width * level
    return jnp.minimum(jnp.maximum(result, -most), most).astype(kind)


def bell_draw_with(rng, extent, deviation, bound, shards, heavy, kind=jnp.bfloat16):
    array = deviation * jax.random.normal(rng, extent, jnp.float32)
    if shards:
        array = array * block_scale(rng, extent, shards, -0.22, 0.18)
    return jnp.clip(strengthened(array, jax.random.fold_in(rng, 3), *heavy), -bound, bound).astype(kind)


def setup_inputs(seed: int = 0, part: int = 0) -> dict:
    streams_of = jax.random.split(jax.random.key(seed), 10)
    part_keys = jax.random.split(jax.random.fold_in(streams_of[9], part), 10)
    residual = centred(part_keys[0], (TOKENS, D), 0.1, 0.59765625, ((1, 16),))
    attn_gain = jnp.clip(1.0 + 0.15 * jax.random.normal(streams_of[1], (D,), jnp.float32), 0.25, 1.75).astype(jnp.bfloat16)
    ffn_gain = jnp.clip(1.0 + 0.18 * jax.random.normal(streams_of[2], (D,), jnp.float32), 0.099609375, 1.8984375).astype(jnp.bfloat16)
    q_weight = centred(streams_of[3], (D, HQ * HD), D ** -0.5, 0.046875, ((1, 16),))
    kv_weight = centred(streams_of[4], (D, 2 * KVH * HD), D ** -0.5, 0.046875, ((1, 16),))
    o_weight = bell_draw_with(streams_of[5], (HQ * HD, D), (HQ * HD) ** -0.5, 0.1875, ((0, 16),), (0, 1, 16, 2.0))
    key_cache = draw_key_cache(jax.random.fold_in(jax.random.fold_in(streams_of[9], part), 71), part)
    value_cache = centred(part_keys[7], (SEQS, CTX, KVH * HD), 3.0, 12.0, ((1, 16),))
    prefix = draw_prefix(jax.random.fold_in(jax.random.fold_in(streams_of[9], part), 71), part)
    return dict(residual=residual, attn_gain=attn_gain, ffn_gain=ffn_gain, q_weight=q_weight, kv_weight=kv_weight, o_weight=o_weight, key_cache=key_cache, value_cache=value_cache, prefix=prefix)


epsilon = 1e-05

def rms_rows(rows, gain):
    values_f = rows.astype(jnp.float32)
    factor = lax.rsqrt(lax.optimization_barrier(jnp.mean(values_f * values_f, axis=-1, keepdims=True)) + epsilon)
    return values_f * factor * gain.astype(jnp.float32)

def rotate(vectors, positions):
    half_width = vectors.shape[-1] // 2
    frequency = 500000.0 ** (-jnp.arange(half_width, dtype=jnp.float32) / half_width)
    angles = positions.astype(jnp.float32)[:, None] * frequency[None, :]
    cosine = jnp.cos(angles)[:, None, :]
    sine = jnp.sin(angles)[:, None, :]
    first_half = vectors[..., :half_width]
    second_half = vectors[..., half_width:]
    return jnp.concatenate([first_half * cosine - second_half * sine, second_half * cosine + first_half * sine], axis=-1)

def reference(residual, attn_gain, ffn_gain, q_weight, kv_weight, o_weight, key_cache, value_cache, prefix):
    normed = rms_rows(residual, attn_gain).astype(jnp.bfloat16)
    positions = (prefix[:, None] + jnp.arange(SPAN, dtype=jnp.int32)[None, :]).reshape(-1)
    queries = jnp.dot(normed, q_weight, preferred_element_type=jnp.float32).reshape(TOKENS, HQ, HD)
    queries = rotate(queries, positions).astype(jnp.bfloat16).reshape(SEQS, SPAN, HQ, HD)
    kv_new = jnp.dot(normed, kv_weight, preferred_element_type=jnp.float32)
    new_keys = rotate(kv_new[:, :KVH * HD].reshape(TOKENS, KVH, HD), positions).astype(jnp.bfloat16)
    new_keys = new_keys.reshape(SEQS, SPAN, KVH, HD)
    new_values = kv_new[:, KVH * HD:].astype(jnp.bfloat16).reshape(SEQS, SPAN, KVH, HD)
    cache_keys = key_cache.reshape(SEQS, CTX, KVH, HD)
    cache_values = value_cache.reshape(SEQS, CTX, KVH, HD)
    score_scale = HD ** (-0.5)
    is_valid = jnp.arange(CTX, dtype=jnp.int32)[None, None, :] < prefix[:, None, None]
    causal = jnp.arange(SPAN)[:, None] >= jnp.arange(SPAN)[None, :]
    group_size = HQ // KVH

    def one_head(head_index):
        kv_index = head_index // group_size
        query_head = lax.dynamic_index_in_dim(queries, head_index, axis=2, keepdims=False).astype(jnp.float32)
        keys_old = lax.dynamic_index_in_dim(cache_keys, kv_index, axis=2, keepdims=False).astype(jnp.float32)
        values_old = lax.dynamic_index_in_dim(cache_values, kv_index, axis=2, keepdims=False).astype(jnp.float32)
        keys_fresh = lax.dynamic_index_in_dim(new_keys, kv_index, axis=2, keepdims=False).astype(jnp.float32)
        values_fresh = lax.dynamic_index_in_dim(new_values, kv_index, axis=2, keepdims=False).astype(jnp.float32)
        old_scores = jnp.einsum('scd,sjd->scj', query_head, keys_old, precision=lax.Precision.HIGHEST) * score_scale
        fresh_scores = jnp.einsum('scd,sjd->scj', query_head, keys_fresh, precision=lax.Precision.HIGHEST) * score_scale
        old_scores = jnp.where(is_valid, old_scores, -1e+30)
        fresh_scores = jnp.where(causal[None], fresh_scores, -1e+30)
        running_max = jnp.maximum(old_scores.max(-1), fresh_scores.max(-1))
        old_weights = jnp.where(is_valid, jnp.exp(old_scores - running_max[..., None]), 0.0)
        fresh_weights = jnp.where(causal[None], jnp.exp(fresh_scores - running_max[..., None]), 0.0)
        totals = old_weights.sum(-1) + fresh_weights.sum(-1)
        old_rounded = old_weights.astype(jnp.bfloat16).astype(jnp.float32)
        fresh_rounded = fresh_weights.astype(jnp.bfloat16).astype(jnp.float32)
        summed = jnp.einsum('scj,sjd->scd', old_rounded, values_old, precision=lax.Precision.HIGHEST)
        summed = summed + jnp.einsum('scj,sjd->scd', fresh_rounded, values_fresh, precision=lax.Precision.HIGHEST)
        return (summed / totals[..., None]).astype(jnp.bfloat16)
    per_head = lax.map(one_head, jnp.arange(HQ, dtype=jnp.int32))
    attn = jnp.transpose(per_head, (1, 2, 0, 3)).reshape(TOKENS, HQ * HD)
    projected = jnp.dot(attn, o_weight, preferred_element_type=jnp.float32)
    hidden = (residual.astype(jnp.float32) + projected).astype(jnp.bfloat16)
    return rms_rows(hidden, ffn_gain).astype(jnp.bfloat16)
```

```python
import jax
import jax.numpy as jnp
from jax import lax
from jax.experimental import pallas as pl
from jax.experimental.pallas import tpu as pltpu
from jax.sharding import PartitionSpec as P

HD = 128
KVH = 8
HQ_DEV = 1
SPAN = 64
SEQS = 2
CTX_DEV = 64
TOKENS = SEQS * SPAN
MIB = 1024 * 1024

epsilon = 1e-05


def rms_rows(rows, gain):
    values_f = rows.astype(jnp.float32)
    factor = lax.rsqrt(jnp.mean(values_f * values_f, axis=-1, keepdims=True) + epsilon)
    return values_f * factor * gain.astype(jnp.float32)


def rope_tables(positions):
    half_width = HD // 2
    frequency = 500000.0 ** (-jnp.arange(half_width, dtype=jnp.float32) / half_width)
    angles = positions.astype(jnp.float32)[:, None] * frequency[None, :]
    return jnp.cos(angles), jnp.sin(angles)


def rotate(vectors, positions):
    half_width = vectors.shape[-1] // 2
    cosine, sine = rope_tables(positions)
    cosine, sine = cosine[:, None, :], sine[:, None, :]
    first_half = vectors[..., :half_width]
    second_half = vectors[..., half_width:]
    return jnp.concatenate(
        [first_half * cosine - second_half * sine, second_half * cosine + first_half * sine],
        axis=-1,
    )


CHIPS = 8
RING = (0, 2, 4, 6, 7, 5, 3, 1)
FORTH = [(2 * RING[i] + c, 2 * RING[(i + 1) % CHIPS] + c) for i in range(CHIPS) for c in range(2)]
BACK = [(b, a) for a, b in FORTH]
SWAP = [(t, t ^ 1) for t in range(2 * CHIPS)]
STRAIGHT = [(k, 2 * k) for k in range(KVH)] + [(KVH + k, 2 * k + 1) for k in range(KVH)]
CROSSED = [(k, 2 * k + 1) for k in range(KVH)] + [(KVH + k, 2 * k) for k in range(KVH)]


def ring_place(rank):
    chip = rank // 2
    return jnp.where(chip % 2 == 0, chip // 2, CHIPS - 1 - chip // 2)


def chip_at(place):
    place = place % CHIPS
    return jnp.where(place < CHIPS // 2, 2 * place, 2 * CHIPS - 1 - 2 * place)


def send(array, pairs):
    return lax.ppermute(array, "tp", pairs)


OFFSETS = (0, -1, 1, -2, 2, -3, 3, 4)


def ring_gather(halves):
    forth, back = list(halves), list(halves)
    got = [{0: halves[0]}, {0: halves[1]}]
    for step in range(1, 5):
        for h in range(2):
            if step < 4 or h == 0:
                forth[h] = send(forth[h], FORTH)
                got[h][-step if step < 4 else 4] = forth[h]
            if step < 4 or h == 1:
                back[h] = send(back[h], BACK)
                got[h][step] = back[h]
    out = []
    for offset in OFFSETS:
        own = [got[h][offset] for h in range(2)]
        other = [send(a, SWAP) for a in own]
        out += [own, other]
    return out


def block_ids(rank):
    place, core = ring_place(rank), rank % 2
    ids = []
    for offset in OFFSETS:
        chip = chip_at(place + offset)
        ids += [2 * chip + core, 2 * chip + 1 - core]
    return jnp.stack(ids).astype(jnp.int32)


def scatter_add(parts):
    narrow = lambda a: a.astype(jnp.bfloat16)
    totals = []
    for h in range(2):
        forth_len, back_len = (4, 3) if h == 0 else (3, 4)
        sums = []
        for length, pairs, sign in ((forth_len, FORTH, 1), (back_len, BACK, -1)):
            running = send(narrow(parts[sign * length if length < 4 else 4][h]), pairs)
            for distance in range(length - 1, 0, -1):
                mine = parts[sign * distance][h]
                running = send(narrow(running.astype(jnp.float32) + mine), pairs)
            sums.append(running.astype(jnp.float32))
        totals.append(sums[0] + sums[1])
    return totals


def project_kernel(ids, *refs):
    blocks = refs[:32]
    gain, cosine, sine, kv_cos, kv_sin, wq, wkv = refs[32:39]
    q_out, kv_out = refs[39:41]
    wq_buf, wkv_buf, sems = refs[41:]
    width = blocks[0].shape[1]
    copies = []
    for i in range(16):
        rows = pl.ds(pl.multiple_of(ids[i] * width, width), width)
        pair = (
            pltpu.make_async_copy(wq.at[rows, :], wq_buf.at[i], sems.at[0, i]),
            pltpu.make_async_copy(wkv.at[rows, :], wkv_buf.at[i], sems.at[1, i]),
        )
        for copy in pair:
            copy.start()
        copies.append(pair)
    factors = []
    for h in range(2):
        squares = jnp.zeros((SPAN, 128), jnp.float32)
        for i in range(16):
            for j in range(width // 128):
                v = blocks[2 * i + h][:, j * 128 : (j + 1) * 128].astype(jnp.float32)
                squares = squares + v * v
        mean = jnp.sum(squares, axis=1, keepdims=True) * (1.0 / (16 * width))
        factors.append(lax.rsqrt(mean + epsilon))
    total = jnp.zeros((TOKENS, 2 * HD), jnp.float32)
    for i in range(16):
        gain_row = gain[ids[i]]
        rows = [
            (blocks[2 * i + h][...].astype(jnp.float32) * factors[h] * gain_row).astype(jnp.bfloat16)
            for h in range(2)
        ]
        for copy in copies[i]:
            copy.wait()
        weights = jnp.concatenate([wq_buf[i], wkv_buf[i]], axis=1)
        total = total + jnp.dot(
            jnp.concatenate(rows, axis=0), weights, preferred_element_type=jnp.float32
        )
    q, kv = total[:, :HD], total[:, HD:]
    q_out[...] = (q * cosine[...] + pltpu.roll(q, HD // 2, 1) * sine[...]).astype(jnp.bfloat16)
    kv_out[...] = (kv * kv_cos[...] + pltpu.roll(kv, HD // 2, 1) * kv_sin[...]).astype(jnp.bfloat16)


def project(ids, blocks, gain, tables, q_weight, kv_weight):
    width = blocks[0].shape[1]
    vmem = pl.BlockSpec(memory_space=pltpu.VMEM)
    return pl.pallas_call(
        project_kernel,
        out_shape=[jax.ShapeDtypeStruct((TOKENS, HD), jnp.bfloat16)] * 2,
        in_specs=[pl.BlockSpec(memory_space=pltpu.SMEM)]
        + [vmem] * 37
        + [pl.BlockSpec(memory_space=pl.ANY)] * 2,
        out_specs=[vmem] * 2,
        scratch_shapes=[
            pltpu.VMEM((16, width, HD), jnp.bfloat16),
            pltpu.VMEM((16, width, HD), jnp.bfloat16),
            pltpu.SemaphoreType.DMA((2, 16)),
        ],
        compiler_params=pltpu.CompilerParams(vmem_limit_bytes=32 * MIB),
        name="norm_project",
    )(ids, *blocks, gain, *tables, q_weight, kv_weight)


def attend_kernel(info, q, first, second, keys, values, out):
    even = info[2] == 0
    fresh_keys = jnp.where(even, first[...], second[...])
    fresh_values = jnp.where(even, second[...], first[...])
    scale = HD ** (-0.5)
    context = keys.shape[0] * keys.shape[2]
    contract = (((1,), (1,)), ((), ()))
    for s in range(SEQS):
        rows = slice(s * SPAN, (s + 1) * SPAN)
        queries = q[rows, :]
        old_keys = keys[:, s].reshape(context, HD)
        old_values = values[:, s].reshape(context, HD)
        old = lax.dot_general(queries, old_keys, contract, preferred_element_type=jnp.float32) * scale
        fresh = (
            lax.dot_general(queries, fresh_keys[rows], contract, preferred_element_type=jnp.float32)
            * scale
        )
        valid = lax.broadcasted_iota(jnp.int32, old.shape, 1) < info[s]
        causal = lax.broadcasted_iota(jnp.int32, fresh.shape, 0) >= lax.broadcasted_iota(
            jnp.int32, fresh.shape, 1
        )
        old = jnp.where(valid, old, -1e30)
        fresh = jnp.where(causal, fresh, -1e30)
        most = jnp.maximum(
            jnp.max(old, axis=1, keepdims=True), jnp.max(fresh, axis=1, keepdims=True)
        )
        old_weights = jnp.where(valid, jnp.exp(old - most), 0.0)
        fresh_weights = jnp.where(causal, jnp.exp(fresh - most), 0.0)
        totals = jnp.sum(old_weights, axis=1, keepdims=True) + jnp.sum(
            fresh_weights, axis=1, keepdims=True
        )
        summed = jnp.dot(
            old_weights.astype(jnp.bfloat16), old_values, preferred_element_type=jnp.float32
        ) + jnp.dot(
            fresh_weights.astype(jnp.bfloat16), fresh_values[rows], preferred_element_type=jnp.float32
        )
        out[rows, :] = (summed / totals).astype(jnp.bfloat16)


def attend(info, q, first, second, keys, values):
    vmem = pl.BlockSpec(memory_space=pltpu.VMEM)
    return pl.pallas_call(
        attend_kernel,
        out_shape=jax.ShapeDtypeStruct((TOKENS, HD), jnp.bfloat16),
        in_specs=[pl.BlockSpec(memory_space=pltpu.SMEM)] + [vmem] * 5,
        out_specs=vmem,
        compiler_params=pltpu.CompilerParams(vmem_limit_bytes=24 * MIB),
        name="attend",
    )(info, q, first, second, keys, values)


def output_kernel(chips, attn, other, weight, other_weight, out):
    left = jnp.concatenate([attn[...], other[...]], axis=1)
    right = jnp.concatenate([weight[0], other_weight[0]], axis=0)
    out[0] = jnp.dot(left, right, preferred_element_type=jnp.float32)


def output_shares(chips, attn, other, weight, other_weight):
    width = weight.shape[2]
    whole = pl.BlockSpec((TOKENS, HD), lambda i, chips: (0, 0))
    block = pl.BlockSpec((1, HD, width), lambda i, chips: (chips[i], 0, 0))
    return pl.pallas_call(
        output_kernel,
        out_shape=jax.ShapeDtypeStruct((CHIPS, TOKENS, width), jnp.float32),
        grid_spec=pltpu.PrefetchScalarGridSpec(
            num_scalar_prefetch=1,
            grid=(CHIPS,),
            in_specs=[whole, whole, block, block],
            out_specs=pl.BlockSpec((1, TOKENS, width), lambda i, chips: (i, 0, 0)),
        ),
        compiler_params=pltpu.CompilerParams(vmem_limit_bytes=24 * MIB),
        name="output_shares",
    )(chips, attn, other, weight, other_weight)


def final_kernel(ids, *refs):
    blocks, gain, out = refs[:32], refs[32], refs[33]
    staged, sems = refs[34:]
    width = blocks[0].shape[1]
    factors = []
    for h in range(2):
        squares = jnp.zeros((SPAN, 128), jnp.float32)
        for i in range(16):
            for j in range(width // 128):
                v = blocks[2 * i + h][:, j * 128 : (j + 1) * 128].astype(jnp.float32)
                squares = squares + v * v
        mean = jnp.sum(squares, axis=1, keepdims=True) * (1.0 / (16 * width))
        factors.append(lax.rsqrt(mean + epsilon))
    copies = []
    for i in range(16):
        gain_row = gain[ids[i]]
        for h in range(2):
            staged[i, h * SPAN : (h + 1) * SPAN, :] = (
                blocks[2 * i + h][...].astype(jnp.float32) * factors[h] * gain_row
            ).astype(jnp.bfloat16)
        copy = pltpu.make_async_copy(
            staged.at[i],
            out.at[:, pl.ds(pl.multiple_of(ids[i] * width, width), width)],
            sems.at[i],
        )
        copy.start()
        copies.append(copy)
    for copy in copies:
        copy.wait()


def final_norm(ids, blocks, gain):
    width = blocks[0].shape[1]
    vmem = pl.BlockSpec(memory_space=pltpu.VMEM)
    return pl.pallas_call(
        final_kernel,
        out_shape=jax.ShapeDtypeStruct((TOKENS, 16 * width), jnp.bfloat16),
        in_specs=[pl.BlockSpec(memory_space=pltpu.SMEM)] + [vmem] * 33,
        out_specs=pl.BlockSpec(memory_space=pl.ANY),
        scratch_shapes=[
            pltpu.VMEM((16, TOKENS, width), jnp.bfloat16),
            pltpu.SemaphoreType.DMA((16,)),
        ],
        compiler_params=pltpu.CompilerParams(vmem_limit_bytes=32 * MIB),
        name="final_norm",
    )(ids, *blocks, gain)


def per_device_ring(
    residual, attn_gain, ffn_gain, q_weight, kv_weight, o_weight, key_cache, value_cache, prefix
):
    rank = lax.axis_index("tp")
    core = rank % 2
    width = residual.shape[1]
    ids = block_ids(rank)

    by_head = lambda cache: jnp.transpose(cache.reshape(SEQS, CTX_DEV, KVH, HD), (2, 0, 1, 3))
    pieces = jnp.stack([by_head(key_cache), by_head(value_cache)], axis=1)
    pieces = pieces.reshape(2 * KVH, SEQS, CTX_DEV, HD)
    mine = lax.all_to_all(pieces, "tp", split_axis=0, concat_axis=0, tiled=True)
    theirs = send(mine, SWAP)
    keys = jnp.where(core == 0, mine, theirs)
    values = jnp.where(core == 0, theirs, mine)

    columns = o_weight.reshape(HD, CHIPS, 2, width)
    o_mine = jnp.transpose(lax.dynamic_index_in_dim(columns, core, 2, keepdims=False), (1, 0, 2))
    o_sent = jnp.transpose(lax.dynamic_index_in_dim(columns, 1 - core, 2, keepdims=False), (1, 0, 2))
    o_other = send(o_sent, SWAP)

    positions = (prefix[:, None] + jnp.arange(SPAN, dtype=jnp.int32)[None, :]).reshape(-1)
    cosine, sine = rope_tables(positions)
    cosine = jnp.concatenate([cosine, cosine], axis=1)
    sine = jnp.concatenate([-sine, sine], axis=1)
    holds_keys = rank < KVH
    tables = (cosine, sine, jnp.where(holds_keys, cosine, 1.0), jnp.where(holds_keys, sine, 0.0))

    blocks = [a for pair in ring_gather([residual[:SPAN], residual[SPAN:]]) for a in pair]
    queries, fresh = project(
        ids, blocks, attn_gain.reshape(16, 1, width).astype(jnp.float32), tables, q_weight, kv_weight
    )
    first, second = send(fresh, STRAIGHT), send(fresh, CROSSED)
    info = jnp.concatenate([prefix, core[None].astype(jnp.int32)])
    attn = attend(info, queries, first, second, keys, values)

    chips = jnp.stack([chip_at(ring_place(rank) + o) for o in OFFSETS]).astype(jnp.int32)
    shares = output_shares(chips, attn, send(attn, SWAP), o_mine, o_other)
    parts = {
        o: [shares[i, :SPAN], shares[i, SPAN:]] for i, o in enumerate(OFFSETS)
    }
    others = scatter_add(parts)
    hidden = [
        (residual[h * SPAN : (h + 1) * SPAN].astype(jnp.float32) + (parts[0][h] + others[h])).astype(
            jnp.bfloat16
        )
        for h in range(2)
    ]
    blocks = [a for pair in ring_gather(hidden) for a in pair]
    return final_norm(ids, blocks, ffn_gain.reshape(16, 1, width).astype(jnp.float32))


def per_device(
    residual, attn_gain, ffn_gain, q_weight, kv_weight, o_weight, key_cache, value_cache, prefix
):
    tp_count = lax.axis_size("tp")
    tp_rank = lax.axis_index("tp")
    heads_all = HQ_DEV * tp_count
    group_size = heads_all // KVH
    token_count = SEQS * SPAN
    score_scale = HD ** (-0.5)
    whole_rows = lax.all_gather(residual, "tp", axis=1, tiled=True)
    normed = rms_rows(whole_rows, attn_gain).astype(jnp.bfloat16)
    positions = (prefix[:, None] + jnp.arange(SPAN, dtype=jnp.int32)[None, :]).reshape(-1)
    queries = jnp.dot(normed, q_weight, preferred_element_type=jnp.float32).reshape(
        token_count, HQ_DEV, HD
    )
    queries = rotate(queries, positions).astype(jnp.bfloat16)
    kv_part = jnp.dot(normed, kv_weight, preferred_element_type=jnp.float32)
    kv_whole = lax.all_gather(kv_part, "tp", axis=1, tiled=True)
    new_keys = rotate(kv_whole[:, : KVH * HD].reshape(token_count, KVH, HD), positions).astype(
        jnp.bfloat16
    )
    new_values = kv_whole[:, KVH * HD :].reshape(token_count, KVH, HD).astype(jnp.bfloat16)
    head_ids = tp_rank * HQ_DEV + jnp.arange(HQ_DEV, dtype=jnp.int32)
    own_kv = head_ids // group_size
    own_keys = jnp.take(new_keys, own_kv, axis=1).reshape(SEQS, SPAN, HQ_DEV, HD)
    own_values = jnp.take(new_values, own_kv, axis=1).reshape(SEQS, SPAN, HQ_DEV, HD)
    own_queries = queries.reshape(SEQS, SPAN, HQ_DEV, HD)
    causal = (jnp.arange(SPAN)[:, None] >= jnp.arange(SPAN)[None, :])[None, None]
    fresh_scores = (
        jnp.einsum("schd,skhd->shck", own_queries, own_keys, preferred_element_type=jnp.float32)
        * score_scale
    )
    fresh_scores = jnp.where(causal, fresh_scores, -1e30)
    fresh_max = fresh_scores.max(-1)
    gathered = lax.all_gather(queries.reshape(token_count, HQ_DEV * HD), "tp", axis=1, tiled=True)
    queries_all = gathered.reshape(SEQS, SPAN, KVH, group_size, HD)
    keys_local = key_cache.reshape(SEQS, CTX_DEV, KVH, HD)
    values_local = value_cache.reshape(SEQS, CTX_DEV, KVH, HD)
    local_scores = (
        jnp.einsum("sckgd,sjkd->skgcj", queries_all, keys_local, preferred_element_type=jnp.float32)
        * score_scale
    )
    first_slot = tp_rank * CTX_DEV
    is_valid = ((first_slot + jnp.arange(CTX_DEV, dtype=jnp.int32))[None, :] < prefix[:, None])[
        :, None, None, None, :
    ]
    local_scores = jnp.where(is_valid, local_scores, -1e30)
    local_max = local_scores.max(-1)
    local_weights = jnp.where(is_valid, jnp.exp(local_scores - local_max[..., None]), 0.0)
    local_total = local_weights.sum(-1)
    local_sum = jnp.einsum(
        "skgcj,sjkd->skgcd",
        local_weights.astype(jnp.bfloat16),
        values_local,
        preferred_element_type=jnp.float32,
    )
    sums_in, maxes_in, totals_in = (
        lax.all_to_all(
            local_sum.reshape(1, SEQS, heads_all, SPAN, HD),
            "tp",
            split_axis=2,
            concat_axis=0,
            tiled=True,
        ),
        lax.all_to_all(
            local_max.reshape(1, SEQS, heads_all, SPAN),
            "tp",
            split_axis=2,
            concat_axis=0,
            tiled=True,
        ),
        lax.all_to_all(
            local_total.reshape(1, SEQS, heads_all, SPAN),
            "tp",
            split_axis=2,
            concat_axis=0,
            tiled=True,
        ),
    )
    running_max = jnp.maximum(maxes_in.max(0), fresh_max)
    factors = jnp.exp(maxes_in - running_max[None])
    fresh_weights = jnp.where(causal, jnp.exp(fresh_scores - running_max[..., None]), 0.0)
    totals = (factors * totals_in).sum(0) + fresh_weights.sum(-1)
    summed = (factors[..., None] * sums_in).sum(0)
    summed = summed + jnp.einsum(
        "shck,skhd->shcd",
        fresh_weights.astype(jnp.bfloat16),
        own_values,
        preferred_element_type=jnp.float32,
    )
    attn = (summed / totals[..., None]).astype(jnp.bfloat16)
    attn = jnp.transpose(attn, (0, 2, 1, 3)).reshape(token_count, HQ_DEV * HD)
    share_part = lax.psum_scatter(
        lax.dot_general(
            o_weight, attn, (((0,), (1,)), ((), ())), preferred_element_type=jnp.float32
        ),
        "tp",
        scatter_dimension=0,
        tiled=True,
    )
    hidden = (residual.astype(jnp.float32) + share_part.T).astype(jnp.bfloat16)
    stream = lax.all_gather(hidden, "tp", axis=1, tiled=True)
    return rms_rows(stream, ffn_gain).astype(jnp.bfloat16)


def solution(mesh):
    return jax.shard_map(
        per_device_ring if mesh.shape["tp"] == 2 * CHIPS else per_device,
        mesh=mesh,
        in_specs=(
            P("replica", "tp"),
            P(),
            P(),
            P(None, "tp"),
            P(None, "tp"),
            P("tp", None),
            P("replica", "tp", None),
            P("replica", "tp", None),
            P("replica"),
        ),
        out_specs=P("replica", None),
        check_vma=False,
    )
```

```python
import jax
import jax.numpy as jnp
from jax import lax
from jax.experimental import pallas as pl
from jax.experimental.pallas import tpu as pltpu
from jax.sharding import PartitionSpec as P

HD = 128
KVH = 8
HQ_DEV = 1
SPAN = 64
SEQS = 2
CTX_DEV = 64
TOKENS = SEQS * SPAN
MIB = 1024 * 1024

epsilon = 1e-05


def rms_rows(rows, gain):
    values_f = rows.astype(jnp.float32)
    factor = lax.rsqrt(jnp.mean(values_f * values_f, axis=-1, keepdims=True) + epsilon)
    return values_f * factor * gain.astype(jnp.float32)


def rope_tables(positions):
    half_width = HD // 2
    frequency = 500000.0 ** (-jnp.arange(half_width, dtype=jnp.float32) / half_width)
    angles = positions.astype(jnp.float32)[:, None] * frequency[None, :]
    return jnp.cos(angles), jnp.sin(angles)


def rotate(vectors, positions):
    half_width = vectors.shape[-1] // 2
    cosine, sine = rope_tables(positions)
    cosine, sine = cosine[:, None, :], sine[:, None, :]
    first_half = vectors[..., :half_width]
    second_half = vectors[..., half_width:]
    return jnp.concatenate(
        [first_half * cosine - second_half * sine, second_half * cosine + first_half * sine],
        axis=-1,
    )


CHIPS = 8
RING = (0, 2, 4, 6, 7, 5, 3, 1)
ONWARD = [(2 * RING[i], 2 * RING[(i + 1) % CHIPS]) for i in range(CHIPS)] + [
    (2 * RING[i] + 1, 2 * RING[i - 1] + 1) for i in range(CHIPS)
]
SWAP = [(t, t ^ 1) for t in range(2 * CHIPS)]
STRAIGHT = [(k, 2 * k) for k in range(KVH)] + [(KVH + k, 2 * k + 1) for k in range(KVH)]
CROSSED = [(k, 2 * k + 1) for k in range(KVH)] + [(KVH + k, 2 * k) for k in range(KVH)]
VMEM = pl.BlockSpec(memory_space=pltpu.VMEM)
SMEM = pl.BlockSpec(memory_space=pltpu.SMEM)
HBM = pl.BlockSpec(memory_space=pltpu.HBM)


def ring_place(rank):
    chip = rank // 2
    return jnp.where(chip % 2 == 0, chip // 2, CHIPS - 1 - chip // 2)


def chip_at(place):
    place = place % CHIPS
    return jnp.where(place < CHIPS // 2, 2 * place, 2 * CHIPS - 1 - 2 * place)


def send(array, pairs):
    return lax.ppermute(array, "tp", pairs)


def ring_gather(own):
    straight, crossed = own, send(own, SWAP)
    blocks = [straight, crossed]
    for step in range(1, 5):
        straight = send(straight, ONWARD)
        blocks += [straight, send(straight, SWAP)]
        if step < 4:
            crossed = send(crossed, ONWARD)
            blocks += [crossed, send(crossed, SWAP)]
    return blocks


def gathered_ids(rank):
    place, core = ring_place(rank), rank % 2
    ahead = 2 * core - 1
    ids = [rank, rank ^ 1]
    for step in range(1, 5):
        near, far = 2 * chip_at(place + ahead * step), 2 * chip_at(place - ahead * step)
        ids += [near + core, far + 1 - core]
        if step < 4:
            ids += [near + 1 - core, far + core]
    return jnp.stack(ids).astype(jnp.int32)


SHARES = ((4, 0), (3, 1), (3, 0), (2, 1), (2, 0), (1, 1), (1, 0), (0, 0))


def share_ids(rank):
    place, core = ring_place(rank), rank % 2
    return jnp.stack(
        [2 * chip_at(place + (1 - 2 * core) * d) + (core + other) % 2 for d, other in SHARES]
    ).astype(jnp.int32)


def ring_sum(shares):
    running = {0: shares[4, 0], 1: shares[3, 1]}
    for step in range(4, 0, -1):
        for other in range(2):
            if step == 4 and other == 1:
                continue
            if (step, other) not in ((4, 0), (3, 1)):
                running[other] = (
                    running[other].astype(jnp.float32) + shares[step, other]
                ).astype(jnp.bfloat16)
            running[other] = send(running[other], ONWARD)
    return running[0], send(running[1], SWAP)


def row_factors(blocks):
    width = blocks[0].shape[1]
    squares = jnp.zeros((TOKENS, 128), jnp.float32)
    for block in blocks:
        for j in range(width // 128):
            v = block[:, j * 128 : (j + 1) * 128].astype(jnp.float32)
            squares = squares + v * v
    mean = jnp.sum(squares, axis=1, keepdims=True) * (1.0 / (len(blocks) * width))
    return lax.rsqrt(mean + epsilon)


def project_kernel(ids, *refs):
    blocks = refs[:16]
    gain, cosine, sine, kv_cos, kv_sin, wq, wkv = refs[16:23]
    q_keep, q_send, kv_straight, kv_crossed = refs[23:27]
    wq_buf, wkv_buf, kv_buf, q_buf, sems = refs[27:]
    width = blocks[0].shape[1]
    copies = []
    for i in range(16):
        rows = pl.ds(pl.multiple_of(ids[i] * width, width), width)
        pair = (
            pltpu.make_async_copy(wq.at[rows, :], wq_buf.at[i], sems.at[0, i]),
            pltpu.make_async_copy(wkv.at[rows, :], wkv_buf.at[i], sems.at[1, i]),
        )
        for copy in pair:
            copy.start()
        copies.append(pair)
    factor = row_factors(blocks)
    total = jnp.zeros((TOKENS, 2 * HD), jnp.float32)
    for i in range(16):
        normed = (blocks[i][...].astype(jnp.float32) * factor * gain[ids[i]]).astype(jnp.bfloat16)
        for copy in copies[i]:
            copy.wait()
        weights = jnp.concatenate([wq_buf[i], wkv_buf[i]], axis=1)
        total = total + jnp.dot(normed, weights, preferred_element_type=jnp.float32)
    q, kv = total[:, :HD], total[:, HD:]
    q_buf[...] = (q * cosine[...] + pltpu.roll(q, HD // 2, 1) * sine[...]).astype(jnp.bfloat16)
    kv_buf[...] = (kv * kv_cos[...] + pltpu.roll(kv, HD // 2, 1) * kv_sin[...]).astype(jnp.bfloat16)
    core_one = ids[0] % 2 == 1
    holds_keys = ids[0] < KVH
    first, second = slice(0, SPAN), slice(SPAN, TOKENS)
    q_keep[...] = jnp.where(core_one, q_buf[second, :], q_buf[first, :])
    q_send[...] = jnp.where(core_one, q_buf[first, :], q_buf[second, :])
    kv_straight[...] = jnp.where(holds_keys, kv_buf[first, :], kv_buf[second, :])
    kv_crossed[...] = jnp.where(holds_keys, kv_buf[second, :], kv_buf[first, :])


def project(ids, blocks, gain, tables, q_weight, kv_weight):
    width = blocks[0].shape[1]
    return pl.pallas_call(
        project_kernel,
        out_shape=[jax.ShapeDtypeStruct((SPAN, HD), jnp.bfloat16)] * 4,
        in_specs=[SMEM] + [VMEM] * 21 + [HBM] * 2,
        out_specs=[VMEM] * 4,
        scratch_shapes=[
            pltpu.VMEM((16, width, HD), jnp.bfloat16),
            pltpu.VMEM((16, width, HD), jnp.bfloat16),
            pltpu.VMEM((TOKENS, HD), jnp.bfloat16),
            pltpu.VMEM((TOKENS, HD), jnp.bfloat16),
            pltpu.SemaphoreType.DMA((2, 16)),
        ],
        compiler_params=pltpu.CompilerParams(vmem_limit_bytes=32 * MIB),
        cost_estimate=pl.CostEstimate(
            flops=4 * TOKENS * 16 * width * HD, bytes_accessed=12 * MIB, transcendentals=0
        ),
        name="norm_project",
    )(ids, *blocks, gain, *tables, q_weight, kv_weight)


def attend_kernel(info, q, q_other, straight, crossed, cache, out):
    core = info[SEQS]
    fresh_keys = jnp.where(core == 0, straight[...], crossed[...])
    fresh_values = jnp.where(core == 0, crossed[...], straight[...])
    scale = HD ** (-0.5)
    context = cache.shape[0] * cache.shape[2]
    contract = (((1,), (1,)), ((), ()))
    queries = jnp.concatenate([q[...], q_other[...]], axis=0)
    old_keys = cache[:, 0].reshape(context, HD)
    old_values = cache[:, 1].reshape(context, HD)
    old = lax.dot_general(queries, old_keys, contract, preferred_element_type=jnp.float32) * scale
    fresh = (
        lax.dot_general(queries, fresh_keys, contract, preferred_element_type=jnp.float32) * scale
    )
    valid = lax.broadcasted_iota(jnp.int32, old.shape, 1) < info[core]
    place = lax.broadcasted_iota(jnp.int32, fresh.shape, 0) % SPAN
    causal = place >= lax.broadcasted_iota(jnp.int32, fresh.shape, 1)
    old = jnp.where(valid, old, -1e30)
    fresh = jnp.where(causal, fresh, -1e30)
    most = jnp.maximum(jnp.max(old, axis=1, keepdims=True), jnp.max(fresh, axis=1, keepdims=True))
    old_weights = jnp.where(valid, jnp.exp(old - most), 0.0)
    fresh_weights = jnp.where(causal, jnp.exp(fresh - most), 0.0)
    totals = jnp.sum(old_weights, axis=1, keepdims=True) + jnp.sum(
        fresh_weights, axis=1, keepdims=True
    )
    summed = jnp.dot(
        old_weights.astype(jnp.bfloat16), old_values, preferred_element_type=jnp.float32
    ) + jnp.dot(
        fresh_weights.astype(jnp.bfloat16), fresh_values, preferred_element_type=jnp.float32
    )
    attn = (summed / totals).astype(jnp.bfloat16)
    out[:, :HD] = attn[:SPAN]
    out[:, HD:] = attn[SPAN:]


def attend(info, q, q_other, straight, crossed, cache):
    return pl.pallas_call(
        attend_kernel,
        out_shape=jax.ShapeDtypeStruct((SPAN, 2 * HD), jnp.bfloat16),
        in_specs=[SMEM] + [VMEM] * 5,
        out_specs=VMEM,
        compiler_params=pltpu.CompilerParams(vmem_limit_bytes=24 * MIB),
        cost_estimate=pl.CostEstimate(
            flops=80 * MIB, bytes_accessed=MIB, transcendentals=TOKENS * 1088
        ),
        name="attend",
    )(info, q, q_other, straight, crossed, cache)


def output_kernel(ids, attn, attn_other, weight, weight_other, *refs):
    count = len(refs) - 2
    outs, (weights, sems) = refs[:count], refs[count:]
    width = weights.shape[2]
    copies = []
    for i in range(count):
        columns = pl.ds(pl.multiple_of(ids[i] * width, width), width)
        pair = (
            pltpu.make_async_copy(weight.at[:, columns], weights.at[i, :HD], sems.at[0, i]),
            pltpu.make_async_copy(weight_other.at[:, columns], weights.at[i, HD:], sems.at[1, i]),
        )
        for copy in pair:
            copy.start()
        copies.append(pair)
    mine = attn[...]
    theirs = jnp.concatenate([attn_other[:, HD:], attn_other[:, :HD]], axis=1)
    core_one = ids[count] == 1
    rows = jnp.concatenate(
        [jnp.where(core_one, theirs, mine), jnp.where(core_one, mine, theirs)], axis=0
    )
    for i in range(count):
        for copy in copies[i]:
            copy.wait()
        outs[i][...] = jnp.dot(
            rows, weights[i], preferred_element_type=jnp.float32
        ).astype(outs[i].dtype)


def output_shares(ids, core, attn, attn_other, weight, weight_other, width, dtype):
    count = ids.shape[0]
    return pl.pallas_call(
        output_kernel,
        out_shape=[jax.ShapeDtypeStruct((TOKENS, width), dtype)] * count,
        in_specs=[SMEM, VMEM, VMEM, HBM, HBM],
        out_specs=[VMEM] * count,
        scratch_shapes=[
            pltpu.VMEM((count, 2 * HD, width), jnp.bfloat16),
            pltpu.SemaphoreType.DMA((2, count)),
        ],
        compiler_params=pltpu.CompilerParams(vmem_limit_bytes=24 * MIB),
        cost_estimate=pl.CostEstimate(
            flops=4 * TOKENS * HD * width * count,
            bytes_accessed=count * MIB,
            transcendentals=0,
        ),
        name="output_shares_%d" % count,
    )(jnp.concatenate([ids, core[None].astype(jnp.int32)]), attn, attn_other, weight, weight_other)


def final_kernel(ids, *refs):
    blocks, gain, out = refs[:16], refs[16], refs[17]
    staged, sems = refs[18:]
    width = blocks[0].shape[1]
    factor = row_factors(blocks)
    copies = []
    for i in range(16):
        staged[i] = (blocks[i][...].astype(jnp.float32) * factor * gain[ids[i]]).astype(jnp.bfloat16)
        copy = pltpu.make_async_copy(
            staged.at[i],
            out.at[:, pl.ds(pl.multiple_of(ids[i] * width, width), width)],
            sems.at[i],
        )
        copy.start()
        copies.append(copy)
    for copy in copies:
        copy.wait()


def final_norm(ids, blocks, gain):
    width = blocks[0].shape[1]
    return pl.pallas_call(
        final_kernel,
        out_shape=jax.ShapeDtypeStruct((TOKENS, 16 * width), jnp.bfloat16),
        in_specs=[SMEM] + [VMEM] * 17,
        out_specs=HBM,
        scratch_shapes=[
            pltpu.VMEM((16, TOKENS, width), jnp.bfloat16),
            pltpu.SemaphoreType.DMA((16,)),
        ],
        compiler_params=pltpu.CompilerParams(vmem_limit_bytes=32 * MIB),
        name="final_norm",
    )(ids, *blocks, gain)


def per_device_ring(
    residual, attn_gain, ffn_gain, q_weight, kv_weight, o_weight, key_cache, value_cache, prefix
):
    rank = lax.axis_index("tp")
    core = rank % 2
    width = residual.shape[1]
    ids = gathered_ids(rank)

    blocks = ring_gather(residual)

    by_head = lambda cache: jnp.transpose(cache.reshape(SEQS, CTX_DEV, KVH, HD), (2, 0, 1, 3))
    pieces = jnp.stack([by_head(key_cache), by_head(value_cache)], axis=2)
    pieces = pieces.reshape(2 * KVH, 2, CTX_DEV, HD)
    pieces, _ = lax.optimization_barrier((pieces, blocks[-4]))
    cache = lax.all_to_all(pieces, "tp", split_axis=0, concat_axis=0, tiled=True)

    held, _ = lax.optimization_barrier((o_weight, blocks[2]))
    weight_other = send(held, SWAP)

    positions = (prefix[:, None] + jnp.arange(SPAN, dtype=jnp.int32)[None, :]).reshape(-1)
    cosine, sine = rope_tables(positions)
    cosine = jnp.concatenate([cosine, cosine], axis=1)
    sine = jnp.concatenate([-sine, sine], axis=1)
    holds_keys = rank < KVH
    tables = (cosine, sine, jnp.where(holds_keys, cosine, 1.0), jnp.where(holds_keys, sine, 0.0))

    q_keep, q_send, straight, crossed = project(
        ids, blocks, attn_gain.reshape(16, 1, width).astype(jnp.float32), tables, q_weight, kv_weight
    )
    info = jnp.concatenate([prefix, core[None].astype(jnp.int32)])
    attn = attend(
        info, q_keep, send(q_send, SWAP), send(straight, STRAIGHT), send(crossed, CROSSED), cache
    )

    to = share_ids(rank)
    inputs = (core, attn, send(attn, SWAP), o_weight, weight_other, width)
    shares = output_shares(to[:2], *inputs, jnp.bfloat16)
    shares += output_shares(to[2:], *inputs, jnp.float32)
    shares = dict(zip(SHARES, shares))
    one_way, other_way = ring_sum(shares)
    projected = shares[0, 0] + one_way.astype(jnp.float32) + other_way.astype(jnp.float32)
    hidden = (residual.astype(jnp.float32) + projected).astype(jnp.bfloat16)
    return final_norm(
        ids, ring_gather(hidden), ffn_gain.reshape(16, 1, width).astype(jnp.float32)
    )


def per_device(
    residual, attn_gain, ffn_gain, q_weight, kv_weight, o_weight, key_cache, value_cache, prefix
):
    tp_count = lax.axis_size("tp")
    tp_rank = lax.axis_index("tp")
    heads_all = HQ_DEV * tp_count
    group_size = heads_all // KVH
    token_count = SEQS * SPAN
    score_scale = HD ** (-0.5)
    whole_rows = lax.all_gather(residual, "tp", axis=1, tiled=True)
    normed = rms_rows(whole_rows, attn_gain).astype(jnp.bfloat16)
    positions = (prefix[:, None] + jnp.arange(SPAN, dtype=jnp.int32)[None, :]).reshape(-1)
    queries = jnp.dot(normed, q_weight, preferred_element_type=jnp.float32).reshape(
        token_count, HQ_DEV, HD
    )
    queries = rotate(queries, positions).astype(jnp.bfloat16)
    kv_part = jnp.dot(normed, kv_weight, preferred_element_type=jnp.float32)
    kv_whole = lax.all_gather(kv_part, "tp", axis=1, tiled=True)
    new_keys = rotate(kv_whole[:, : KVH * HD].reshape(token_count, KVH, HD), positions).astype(
        jnp.bfloat16
    )
    new_values = kv_whole[:, KVH * HD :].reshape(token_count, KVH, HD).astype(jnp.bfloat16)
    head_ids = tp_rank * HQ_DEV + jnp.arange(HQ_DEV, dtype=jnp.int32)
    own_kv = head_ids // group_size
    own_keys = jnp.take(new_keys, own_kv, axis=1).reshape(SEQS, SPAN, HQ_DEV, HD)
    own_values = jnp.take(new_values, own_kv, axis=1).reshape(SEQS, SPAN, HQ_DEV, HD)
    own_queries = queries.reshape(SEQS, SPAN, HQ_DEV, HD)
    causal = (jnp.arange(SPAN)[:, None] >= jnp.arange(SPAN)[None, :])[None, None]
    fresh_scores = (
        jnp.einsum("schd,skhd->shck", own_queries, own_keys, preferred_element_type=jnp.float32)
        * score_scale
    )
    fresh_scores = jnp.where(causal, fresh_scores, -1e30)
    fresh_max = fresh_scores.max(-1)
    gathered = lax.all_gather(queries.reshape(token_count, HQ_DEV * HD), "tp", axis=1, tiled=True)
    queries_all = gathered.reshape(SEQS, SPAN, KVH, group_size, HD)
    keys_local = key_cache.reshape(SEQS, CTX_DEV, KVH, HD)
    values_local = value_cache.reshape(SEQS, CTX_DEV, KVH, HD)
    local_scores = (
        jnp.einsum("sckgd,sjkd->skgcj", queries_all, keys_local, preferred_element_type=jnp.float32)
        * score_scale
    )
    first_slot = tp_rank * CTX_DEV
    is_valid = ((first_slot + jnp.arange(CTX_DEV, dtype=jnp.int32))[None, :] < prefix[:, None])[
        :, None, None, None, :
    ]
    local_scores = jnp.where(is_valid, local_scores, -1e30)
    local_max = local_scores.max(-1)
    local_weights = jnp.where(is_valid, jnp.exp(local_scores - local_max[..., None]), 0.0)
    local_total = local_weights.sum(-1)
    local_sum = jnp.einsum(
        "skgcj,sjkd->skgcd",
        local_weights.astype(jnp.bfloat16),
        values_local,
        preferred_element_type=jnp.float32,
    )
    sums_in, maxes_in, totals_in = (
        lax.all_to_all(
            local_sum.reshape(1, SEQS, heads_all, SPAN, HD),
            "tp",
            split_axis=2,
            concat_axis=0,
            tiled=True,
        ),
        lax.all_to_all(
            local_max.reshape(1, SEQS, heads_all, SPAN),
            "tp",
            split_axis=2,
            concat_axis=0,
            tiled=True,
        ),
        lax.all_to_all(
            local_total.reshape(1, SEQS, heads_all, SPAN),
            "tp",
            split_axis=2,
            concat_axis=0,
            tiled=True,
        ),
    )
    running_max = jnp.maximum(maxes_in.max(0), fresh_max)
    factors = jnp.exp(maxes_in - running_max[None])
    fresh_weights = jnp.where(causal, jnp.exp(fresh_scores - running_max[..., None]), 0.0)
    totals = (factors * totals_in).sum(0) + fresh_weights.sum(-1)
    summed = (factors[..., None] * sums_in).sum(0)
    summed = summed + jnp.einsum(
        "shck,skhd->shcd",
        fresh_weights.astype(jnp.bfloat16),
        own_values,
        preferred_element_type=jnp.float32,
    )
    attn = (summed / totals[..., None]).astype(jnp.bfloat16)
    attn = jnp.transpose(attn, (0, 2, 1, 3)).reshape(token_count, HQ_DEV * HD)
    share_part = lax.psum_scatter(
        lax.dot_general(
            o_weight, attn, (((0,), (1,)), ((), ())), preferred_element_type=jnp.float32
        ),
        "tp",
        scatter_dimension=0,
        tiled=True,
    )
    hidden = (residual.astype(jnp.float32) + share_part.T).astype(jnp.bfloat16)
    stream = lax.all_gather(hidden, "tp", axis=1, tiled=True)
    return rms_rows(stream, ffn_gain).astype(jnp.bfloat16)


def solution(mesh):
    return jax.shard_map(
        per_device_ring if mesh.shape["tp"] == 2 * CHIPS else per_device,
        mesh=mesh,
        in_specs=(
            P("replica", "tp"),
            P(),
            P(),
            P(None, "tp"),
            P(None, "tp"),
            P("tp", None),
            P("replica", "tp", None),
            P("replica", "tp", None),
            P("replica"),
        ),
        out_specs=P("replica", None),
        check_vma=False,
    )
```

```python
import functools

import jax
import jax.numpy as jnp
from jax import lax
from jax.experimental import pallas as pl
from jax.experimental.pallas import tpu as pltpu
from jax.sharding import PartitionSpec as P

HD = 128
KVH = 8
HQ_DEV = 1
SPAN = 64
SEQS = 2
CTX_DEV = 64
TOKENS = SEQS * SPAN
MIB = 1024 * 1024

epsilon = 1e-05


def rms_rows(rows, gain):
    values_f = rows.astype(jnp.float32)
    factor = lax.rsqrt(jnp.mean(values_f * values_f, axis=-1, keepdims=True) + epsilon)
    return values_f * factor * gain.astype(jnp.float32)


def rope_tables(positions):
    half_width = HD // 2
    frequency = 500000.0 ** (-jnp.arange(half_width, dtype=jnp.float32) / half_width)
    angles = positions.astype(jnp.float32)[:, None] * frequency[None, :]
    return jnp.cos(angles), jnp.sin(angles)


def rotate(vectors, positions):
    half_width = vectors.shape[-1] // 2
    cosine, sine = rope_tables(positions)
    cosine, sine = cosine[:, None, :], sine[:, None, :]
    first_half = vectors[..., :half_width]
    second_half = vectors[..., half_width:]
    return jnp.concatenate(
        [first_half * cosine - second_half * sine, second_half * cosine + first_half * sine],
        axis=-1,
    )


CHIPS = 8
RING = (0, 2, 4, 6, 7, 5, 3, 1)
ONWARD = [(2 * RING[i], 2 * RING[(i + 1) % CHIPS]) for i in range(CHIPS)] + [
    (2 * RING[i] + 1, 2 * RING[i - 1] + 1) for i in range(CHIPS)
]
ENTER = [(2 * RING[i], 2 * RING[i - 1] + 1) for i in range(CHIPS)] + [
    (2 * RING[i] + 1, 2 * RING[(i + 1) % CHIPS]) for i in range(CHIPS)
]
LEAVE = [(2 * RING[i], 2 * RING[(i + 1) % CHIPS] + 1) for i in range(CHIPS)] + [
    (2 * RING[i] + 1, 2 * RING[i - 1]) for i in range(CHIPS)
]
SWAP = [(t, t ^ 1) for t in range(2 * CHIPS)]
STRAIGHT = [(k, 2 * k) for k in range(KVH)] + [(KVH + k, 2 * k + 1) for k in range(KVH)]
CROSSED = [(k, 2 * k + 1) for k in range(KVH)] + [(KVH + k, 2 * k) for k in range(KVH)]
VMEM = pl.BlockSpec(memory_space=pltpu.VMEM)
SMEM = pl.BlockSpec(memory_space=pltpu.SMEM)
HBM = pl.BlockSpec(memory_space=pltpu.HBM)


def ring_place(rank):
    chip = rank // 2
    return jnp.where(chip % 2 == 0, chip // 2, CHIPS - 1 - chip // 2)


def chip_at(place):
    place = place % CHIPS
    return jnp.where(place < CHIPS // 2, 2 * place, 2 * CHIPS - 1 - 2 * place)


def send(array, pairs):
    return lax.ppermute(array, "tp", pairs)


def ring_gather(own):
    straight, crossed = own, own
    blocks = [own, send(own, SWAP)]
    values_f = own.astype(jnp.float32)
    squares = jnp.sum(values_f * values_f, axis=1)
    for step in range(1, 5):
        if step > 1:
            straight, squares = lax.optimization_barrier((straight, squares))
        straight = send(straight, ONWARD)
        blocks.append(straight)
        if step < 4:
            blocks.append(send(straight, SWAP))
            squares = squares + send(squares, [(t, t ^ 2**step) for t in range(2 * CHIPS)])
            crossed = send(crossed, ENTER if step == 1 else ONWARD)
            blocks += [crossed, send(crossed, SWAP)]
    squares = squares + send(squares, SWAP)
    return blocks, squares[None, :]


def last_block(block, work):
    block, work = lax.optimization_barrier((block, work))
    return [block, send(block, SWAP)], work


def gathered_ids(rank):
    place, core = ring_place(rank), rank % 2
    ahead = 2 * core - 1
    ids = [rank, rank ^ 1]
    for step in range(1, 5):
        near, far = 2 * chip_at(place + ahead * step), 2 * chip_at(place - ahead * step)
        ids += [near + core, far + 1 - core]
        if step < 4:
            ids += [near + 1 - core, far + core]
    return jnp.stack(ids).astype(jnp.int32)


SHARES = ((4, 0), (3, 1), (3, 0), (2, 1), (2, 0), (1, 1), (1, 0), (0, 0))


def share_ids(rank):
    place, core = ring_place(rank), rank % 2
    return jnp.stack(
        [2 * chip_at(place + (1 - 2 * core) * d) + (core + other) % 2 for d, other in SHARES]
    ).astype(jnp.int32)


def ring_sum(shares):
    running = {0: shares[4, 0], 1: shares[3, 1]}
    for step in range(4, 0, -1):
        for other in range(2):
            if step == 4 and other == 1:
                continue
            if (step, other) not in ((4, 0), (3, 1)):
                running[other] = (
                    running[other].astype(jnp.float32) + shares[step, other]
                ).astype(jnp.bfloat16)
            running[other] = send(running[other], LEAVE if (step, other) == (1, 1) else ONWARD)
    return running[0], running[1]


def row_factors(squares, features):
    factor = lax.rsqrt(squares[...] * (1.0 / features) + epsilon)
    return jnp.transpose(jnp.broadcast_to(factor, (TOKENS, TOKENS)))


def normed_block(block, factors, gain_row):
    return jnp.concatenate(
        [
            (block[:, j : j + 128].astype(jnp.float32) * factors * gain_row[:, j : j + 128]).astype(
                jnp.bfloat16
            )
            for j in range(0, block.shape[1], 128)
        ],
        axis=1,
    )


def in_hbm(array):
    return pltpu.with_memory_space_constraint(array, pltpu.HBM)


def weight_copies(ids, first, wq, wkv, out, sems):
    count, width, _ = out.shape
    copies = []
    for i in range(count):
        rows = pl.ds(pl.multiple_of(ids[first + i] * width, width), width)
        pair = [
            pltpu.make_async_copy(weight.at[rows, :], out.at[i, :, pl.ds(j * HD, HD)], sems.at[j, i])
            for j, weight in enumerate((wq, wkv))
        ]
        for copy in pair:
            copy.start()
        copies.append(pair)
    return copies


def project_kernel(start, count, ahead, with_sum, ids, *refs):
    blocks, refs = refs[:count], refs[count:]
    squares, gain, wq, wkv = refs[:4]
    before, refs = (refs[4], refs[5:]) if with_sum else (None, refs[4:])
    out, refs = refs[0], refs[1:]
    next_weights, refs = (refs[0], refs[1:]) if ahead else (None, refs)
    weights, sems = refs[:2]
    copies = weight_copies(ids, start, wq, wkv, weights, sems)
    if ahead:
        next_copies = weight_copies(ids, start + count, wq, wkv, next_weights, refs[2])
    width = blocks[0].shape[1]
    factors = row_factors(squares, 16 * width)
    total = before[...] if with_sum else jnp.zeros((TOKENS, 2 * HD), jnp.float32)
    for i in range(count):
        normed = normed_block(blocks[i], factors, gain[ids[start + i]])
        for copy in copies[i]:
            copy.wait()
        total = total + jnp.dot(normed, weights[i], preferred_element_type=jnp.float32)
    out[...] = total
    if ahead:
        for pair in next_copies:
            for copy in pair:
                copy.wait()


def project_some(ids, start, blocks, squares, gain, wq, wkv, before=None, ahead=0):
    count, width = len(blocks), blocks[0].shape[1]
    out_shape = [jax.ShapeDtypeStruct((TOKENS, 2 * HD), jnp.float32)]
    scratch = [
        pltpu.VMEM((count, width, 2 * HD), jnp.bfloat16),
        pltpu.SemaphoreType.DMA((2, count)),
    ]
    if ahead:
        out_shape.append(jax.ShapeDtypeStruct((ahead, width, 2 * HD), jnp.bfloat16))
        scratch.append(pltpu.SemaphoreType.DMA((2, ahead)))
    sums = [] if before is None else [before]
    return pl.pallas_call(
        functools.partial(project_kernel, start, count, ahead, before is not None),
        out_shape=out_shape,
        in_specs=[SMEM] + [VMEM] * (count + 2) + [HBM] * 2 + [VMEM] * len(sums),
        out_specs=[VMEM] * len(out_shape),
        scratch_shapes=scratch,
        compiler_params=pltpu.CompilerParams(vmem_limit_bytes=24 * MIB),
        cost_estimate=pl.CostEstimate(
            flops=4 * TOKENS * count * width * HD,
            bytes_accessed=(count + ahead) * width * HD * 4 + count * TOKENS * width * 2,
            transcendentals=0,
        ),
        name="project_%d" % start,
    )(ids, *blocks, squares, gain, in_hbm(wq), in_hbm(wkv), *sums)


def project_last_kernel(start, count, ids, *refs):
    blocks, refs = refs[:count], refs[count:]
    squares, gain, before, weights, cosine, sine, kv_cos, kv_sin = refs[:8]
    q_keep, q_send, kv_straight, kv_crossed = refs[8:12]
    factors = row_factors(squares, 16 * blocks[0].shape[1])
    total = before[...]
    for i in range(count):
        normed = normed_block(blocks[i], factors, gain[ids[start + i]])
        total = total + jnp.dot(normed, weights[i], preferred_element_type=jnp.float32)
    q, kv = total[:, :HD], total[:, HD:]
    q = (q * cosine[...] + pltpu.roll(q, HD // 2, 1) * sine[...]).astype(jnp.bfloat16)
    kv = (kv * kv_cos[...] + pltpu.roll(kv, HD // 2, 1) * kv_sin[...]).astype(jnp.bfloat16)
    core_one = ids[0] % 2 == 1
    holds_keys = ids[0] < KVH
    first, second = slice(0, SPAN), slice(SPAN, TOKENS)
    q_keep[...] = jnp.where(core_one, q[second], q[first])
    q_send[...] = jnp.where(core_one, q[first], q[second])
    kv_straight[...] = jnp.where(holds_keys, kv[first], kv[second])
    kv_crossed[...] = jnp.where(holds_keys, kv[second], kv[first])


def project_last(ids, start, blocks, squares, gain, before, weights, tables):
    count = len(blocks)
    return pl.pallas_call(
        functools.partial(project_last_kernel, start, count),
        out_shape=[jax.ShapeDtypeStruct((SPAN, HD), jnp.bfloat16)] * 4,
        in_specs=[SMEM] + [VMEM] * (count + 8),
        out_specs=[VMEM] * 4,
        compiler_params=pltpu.CompilerParams(vmem_limit_bytes=16 * MIB),
        cost_estimate=pl.CostEstimate(
            flops=2 * TOKENS * weights.size, bytes_accessed=2 * MIB, transcendentals=0
        ),
        name="project_last",
    )(ids, *blocks, squares, gain, before, weights, *tables)


def share_copies(to, first, weight, weight_other, out, sems):
    count, _, width = out.shape
    copies = []
    for i in range(count):
        columns = pl.ds(pl.multiple_of(to[first + i] * width, width), width)
        pair = [
            pltpu.make_async_copy(part.at[:, columns], out.at[i, pl.ds(j * HD, HD), :], sems.at[j, i])
            for j, part in enumerate((weight, weight_other))
        ]
        for copy in pair:
            copy.start()
        copies.append(pair)
    return copies


def attend_kernel(
    info, to, q, q_other, straight, crossed, cache, weight, weight_other, out, weights, sems
):
    copies = share_copies(to, 0, weight, weight_other, weights, sems)
    core = info[SEQS]
    fresh_keys = jnp.where(core == 0, straight[...], crossed[...])
    fresh_values = jnp.where(core == 0, crossed[...], straight[...])
    scale = HD ** (-0.5)
    context = cache.shape[0] * cache.shape[2]
    contract = (((1,), (1,)), ((), ()))
    queries = jnp.concatenate([q[...], q_other[...]], axis=0)
    old_keys = cache[:, 0].reshape(context, HD)
    old_values = cache[:, 1].reshape(context, HD)
    old = lax.dot_general(queries, old_keys, contract, preferred_element_type=jnp.float32) * scale
    fresh = (
        lax.dot_general(queries, fresh_keys, contract, preferred_element_type=jnp.float32) * scale
    )
    valid = lax.broadcasted_iota(jnp.int32, old.shape, 1) < info[core]
    place = lax.broadcasted_iota(jnp.int32, fresh.shape, 0) % SPAN
    causal = place >= lax.broadcasted_iota(jnp.int32, fresh.shape, 1)
    old = jnp.where(valid, old, -1e30)
    fresh = jnp.where(causal, fresh, -1e30)
    most = jnp.maximum(jnp.max(old, axis=1, keepdims=True), jnp.max(fresh, axis=1, keepdims=True))
    old_weights = jnp.where(valid, jnp.exp(old - most), 0.0)
    fresh_weights = jnp.where(causal, jnp.exp(fresh - most), 0.0)
    totals = jnp.sum(old_weights, axis=1, keepdims=True) + jnp.sum(
        fresh_weights, axis=1, keepdims=True
    )
    summed = jnp.dot(
        old_weights.astype(jnp.bfloat16), old_values, preferred_element_type=jnp.float32
    ) + jnp.dot(
        fresh_weights.astype(jnp.bfloat16), fresh_values, preferred_element_type=jnp.float32
    )
    attn = (summed / totals).astype(jnp.bfloat16)
    out[:, :HD] = attn[:SPAN]
    out[:, HD:] = attn[SPAN:]
    for pair in copies:
        for copy in pair:
            copy.wait()


def attend(info, to, q, q_other, straight, crossed, cache, weight, weight_other, ahead):
    width = weight.shape[1] // 16
    return pl.pallas_call(
        attend_kernel,
        out_shape=[
            jax.ShapeDtypeStruct((SPAN, 2 * HD), jnp.bfloat16),
            jax.ShapeDtypeStruct((ahead, 2 * HD, width), jnp.bfloat16),
        ],
        in_specs=[SMEM] * 2 + [VMEM] * 5 + [HBM] * 2,
        out_specs=[VMEM] * 2,
        scratch_shapes=[pltpu.SemaphoreType.DMA((2, ahead))],
        compiler_params=pltpu.CompilerParams(vmem_limit_bytes=16 * MIB),
        cost_estimate=pl.CostEstimate(
            flops=80 * MIB, bytes_accessed=3 * MIB, transcendentals=TOKENS * 1088
        ),
        name="attend",
    )(info, to, q, q_other, straight, crossed, cache, in_hbm(weight), weight_other)


def both_heads(core, attn, attn_other):
    mine = attn[...]
    theirs = jnp.concatenate([attn_other[:, HD:], attn_other[:, :HD]], axis=1)
    core_one = core[0] == 1
    return jnp.concatenate(
        [jnp.where(core_one, theirs, mine), jnp.where(core_one, mine, theirs)], axis=0
    )


def first_shares_kernel(core, attn, attn_other, weights, *outs):
    rows = both_heads(core, attn, attn_other)
    for i, out in enumerate(outs):
        out[...] = jnp.dot(rows, weights[i], preferred_element_type=jnp.float32).astype(out.dtype)


def first_shares(core, attn, attn_other, weights):
    count, _, width = weights.shape
    return pl.pallas_call(
        first_shares_kernel,
        out_shape=[jax.ShapeDtypeStruct((TOKENS, width), jnp.bfloat16)] * count,
        in_specs=[SMEM] + [VMEM] * 3,
        out_specs=[VMEM] * count,
        compiler_params=pltpu.CompilerParams(vmem_limit_bytes=16 * MIB),
        cost_estimate=pl.CostEstimate(
            flops=2 * TOKENS * weights.size, bytes_accessed=count * MIB, transcendentals=0
        ),
        name="first_shares",
    )(core, attn, attn_other, weights)


def more_shares_kernel(first, core, to, attn, attn_other, weight, weight_other, *refs):
    outs, (weights, sems) = refs[:-2], refs[-2:]
    copies = share_copies(to, first, weight, weight_other, weights, sems)
    rows = both_heads(core, attn, attn_other)
    for i, out in enumerate(outs):
        for copy in copies[i]:
            copy.wait()
        out[...] = jnp.dot(rows, weights[i], preferred_element_type=jnp.float32)


def more_shares(core, to, attn, attn_other, weight, weight_other, first):
    count, width = len(SHARES) - first, weight.shape[1] // 16
    return pl.pallas_call(
        functools.partial(more_shares_kernel, first),
        out_shape=[jax.ShapeDtypeStruct((TOKENS, width), jnp.float32)] * count,
        in_specs=[SMEM] * 2 + [VMEM] * 2 + [HBM] * 2,
        out_specs=[VMEM] * count,
        scratch_shapes=[
            pltpu.VMEM((count, 2 * HD, width), jnp.bfloat16),
            pltpu.SemaphoreType.DMA((2, count)),
        ],
        compiler_params=pltpu.CompilerParams(vmem_limit_bytes=16 * MIB),
        cost_estimate=pl.CostEstimate(
            flops=4 * TOKENS * HD * width * count,
            bytes_accessed=count * MIB,
            transcendentals=0,
        ),
        name="more_shares",
    )(core, to, attn, attn_other, in_hbm(weight), weight_other)


def final_kernel(start, count, features, ids, *refs):
    blocks, squares, gain = refs[:count], refs[count], refs[count + 1]
    out, staged, sems = refs[-3:]
    width = blocks[0].shape[1]
    factors = row_factors(squares, features)
    copies = []
    for i in range(count):
        staged[i] = normed_block(blocks[i], factors, gain[ids[start + i]])
        copy = pltpu.make_async_copy(
            staged.at[i],
            out.at[:, pl.ds(pl.multiple_of(ids[start + i] * width, width), width)],
            sems.at[i],
        )
        copy.start()
        copies.append(copy)
    for copy in copies:
        copy.wait()


def final_some(ids, start, blocks, squares, gain, before=None):
    count, width = len(blocks), blocks[0].shape[1]
    features = 16 * width
    kept = [] if before is None else [before]
    return pl.pallas_call(
        functools.partial(final_kernel, start, count, features),
        out_shape=jax.ShapeDtypeStruct((TOKENS, features), jnp.bfloat16),
        in_specs=[SMEM] + [VMEM] * (count + 2) + [HBM] * len(kept),
        out_specs=HBM,
        input_output_aliases={count + 3: 0} if kept else {},
        scratch_shapes=[
            pltpu.VMEM((count, TOKENS, width), jnp.bfloat16),
            pltpu.SemaphoreType.DMA((count,)),
        ],
        compiler_params=pltpu.CompilerParams(vmem_limit_bytes=16 * MIB),
        cost_estimate=pl.CostEstimate(
            flops=4 * TOKENS * width * count,
            bytes_accessed=4 * TOKENS * width * count,
            transcendentals=0,
        ),
        name="final_%d" % start,
    )(ids, *blocks, squares, gain, *kept)


def per_device_ring(
    residual, attn_gain, ffn_gain, q_weight, kv_weight, o_weight, key_cache, value_cache, prefix
):
    rank = lax.axis_index("tp")
    core = rank % 2
    width = residual.shape[1]
    ids = gathered_ids(rank)
    to = share_ids(rank)
    core_id = core[None].astype(jnp.int32)
    info = jnp.concatenate([prefix, core_id])

    blocks, squares = ring_gather(residual)
    weight_other = send(o_weight, SWAP)

    by_head = lambda cache: jnp.transpose(cache.reshape(SEQS, CTX_DEV, KVH, HD), (2, 0, 1, 3))
    pieces = jnp.stack([by_head(key_cache), by_head(value_cache)], axis=2)
    pieces = pieces.reshape(2 * KVH, 2, CTX_DEV, HD)
    cache = lax.all_to_all(pieces, "tp", split_axis=0, concat_axis=0, tiled=True)

    positions = (prefix[:, None] + jnp.arange(SPAN, dtype=jnp.int32)[None, :]).reshape(-1)
    cosine, sine = rope_tables(positions)
    cosine = jnp.concatenate([cosine, cosine], axis=1)
    sine = jnp.concatenate([-sine, sine], axis=1)
    holds_keys = rank < KVH
    tables = (cosine, sine, jnp.where(holds_keys, cosine, 1.0), jnp.where(holds_keys, sine, 0.0))

    gain = attn_gain.reshape(16, 1, width).astype(jnp.float32)
    shared = (squares, gain, q_weight, kv_weight)
    (total,) = project_some(ids, 0, blocks[:10], *shared)
    last, total = last_block(blocks[14], total)
    total, last_weights = project_some(ids, 10, blocks[10:14], *shared, before=total, ahead=2)
    q_keep, q_send, straight, crossed = project_last(
        ids, 14, last, squares, gain, total, last_weights, tables
    )
    attn, first_weights = attend(
        info,
        to,
        q_keep,
        send(q_send, SWAP),
        send(straight, STRAIGHT),
        send(crossed, CROSSED),
        cache,
        o_weight,
        weight_other,
        2,
    )
    attn_other = send(attn, SWAP)
    shares = list(first_shares(core_id, attn, attn_other, first_weights))
    shares += more_shares(core_id, to, attn, attn_other, o_weight, weight_other, 2)
    one_way, other_way = ring_sum(dict(zip(SHARES, shares)))
    projected = shares[-1] + one_way.astype(jnp.float32) + other_way.astype(jnp.float32)
    hidden = (residual.astype(jnp.float32) + projected).astype(jnp.bfloat16)

    blocks, squares = ring_gather(hidden)
    gain = ffn_gain.reshape(16, 1, width).astype(jnp.float32)
    out = final_some(ids, 0, blocks[:10], squares, gain)
    last, out = last_block(blocks[14], out)
    out = final_some(ids, 10, blocks[10:14], squares, gain, out)
    return final_some(ids, 14, last, squares, gain, out)


def per_device(
    residual, attn_gain, ffn_gain, q_weight, kv_weight, o_weight, key_cache, value_cache, prefix
):
    tp_count = lax.axis_size("tp")
    tp_rank = lax.axis_index("tp")
    heads_all = HQ_DEV * tp_count
    group_size = heads_all // KVH
    token_count = SEQS * SPAN
    score_scale = HD ** (-0.5)
    whole_rows = lax.all_gather(residual, "tp", axis=1, tiled=True)
    normed = rms_rows(whole_rows, attn_gain).astype(jnp.bfloat16)
    positions = (prefix[:, None] + jnp.arange(SPAN, dtype=jnp.int32)[None, :]).reshape(-1)
    queries = jnp.dot(normed, q_weight, preferred_element_type=jnp.float32).reshape(
        token_count, HQ_DEV, HD
    )
    queries = rotate(queries, positions).astype(jnp.bfloat16)
    kv_part = jnp.dot(normed, kv_weight, preferred_element_type=jnp.float32)
    kv_whole = lax.all_gather(kv_part, "tp", axis=1, tiled=True)
    new_keys = rotate(kv_whole[:, : KVH * HD].reshape(token_count, KVH, HD), positions).astype(
        jnp.bfloat16
    )
    new_values = kv_whole[:, KVH * HD :].reshape(token_count, KVH, HD).astype(jnp.bfloat16)
    head_ids = tp_rank * HQ_DEV + jnp.arange(HQ_DEV, dtype=jnp.int32)
    own_kv = head_ids // group_size
    own_keys = jnp.take(new_keys, own_kv, axis=1).reshape(SEQS, SPAN, HQ_DEV, HD)
    own_values = jnp.take(new_values, own_kv, axis=1).reshape(SEQS, SPAN, HQ_DEV, HD)
    own_queries = queries.reshape(SEQS, SPAN, HQ_DEV, HD)
    causal = (jnp.arange(SPAN)[:, None] >= jnp.arange(SPAN)[None, :])[None, None]
    fresh_scores = (
        jnp.einsum("schd,skhd->shck", own_queries, own_keys, preferred_element_type=jnp.float32)
        * score_scale
    )
    fresh_scores = jnp.where(causal, fresh_scores, -1e30)
    fresh_max = fresh_scores.max(-1)
    gathered = lax.all_gather(queries.reshape(token_count, HQ_DEV * HD), "tp", axis=1, tiled=True)
    queries_all = gathered.reshape(SEQS, SPAN, KVH, group_size, HD)
    keys_local = key_cache.reshape(SEQS, CTX_DEV, KVH, HD)
    values_local = value_cache.reshape(SEQS, CTX_DEV, KVH, HD)
    local_scores = (
        jnp.einsum("sckgd,sjkd->skgcj", queries_all, keys_local, preferred_element_type=jnp.float32)
        * score_scale
    )
    first_slot = tp_rank * CTX_DEV
    is_valid = ((first_slot + jnp.arange(CTX_DEV, dtype=jnp.int32))[None, :] < prefix[:, None])[
        :, None, None, None, :
    ]
    local_scores = jnp.where(is_valid, local_scores, -1e30)
    local_max = local_scores.max(-1)
    local_weights = jnp.where(is_valid, jnp.exp(local_scores - local_max[..., None]), 0.0)
    local_total = local_weights.sum(-1)
    local_sum = jnp.einsum(
        "skgcj,sjkd->skgcd",
        local_weights.astype(jnp.bfloat16),
        values_local,
        preferred_element_type=jnp.float32,
    )
    sums_in, maxes_in, totals_in = (
        lax.all_to_all(
            local_sum.reshape(1, SEQS, heads_all, SPAN, HD),
            "tp",
            split_axis=2,
            concat_axis=0,
            tiled=True,
        ),
        lax.all_to_all(
            local_max.reshape(1, SEQS, heads_all, SPAN),
            "tp",
            split_axis=2,
            concat_axis=0,
            tiled=True,
        ),
        lax.all_to_all(
            local_total.reshape(1, SEQS, heads_all, SPAN),
            "tp",
            split_axis=2,
            concat_axis=0,
            tiled=True,
        ),
    )
    running_max = jnp.maximum(maxes_in.max(0), fresh_max)
    factors = jnp.exp(maxes_in - running_max[None])
    fresh_weights = jnp.where(causal, jnp.exp(fresh_scores - running_max[..., None]), 0.0)
    totals = (factors * totals_in).sum(0) + fresh_weights.sum(-1)
    summed = (factors[..., None] * sums_in).sum(0)
    summed = summed + jnp.einsum(
        "shck,skhd->shcd",
        fresh_weights.astype(jnp.bfloat16),
        own_values,
        preferred_element_type=jnp.float32,
    )
    attn = (summed / totals[..., None]).astype(jnp.bfloat16)
    attn = jnp.transpose(attn, (0, 2, 1, 3)).reshape(token_count, HQ_DEV * HD)
    share_part = lax.psum_scatter(
        lax.dot_general(
            o_weight, attn, (((0,), (1,)), ((), ())), preferred_element_type=jnp.float32
        ),
        "tp",
        scatter_dimension=0,
        tiled=True,
    )
    hidden = (residual.astype(jnp.float32) + share_part.T).astype(jnp.bfloat16)
    stream = lax.all_gather(hidden, "tp", axis=1, tiled=True)
    return rms_rows(stream, ffn_gain).astype(jnp.bfloat16)


def solution(mesh):
    return jax.shard_map(
        per_device_ring if mesh.shape["tp"] == 2 * CHIPS else per_device,
        mesh=mesh,
        in_specs=(
            P("replica", "tp"),
            P(),
            P(),
            P(None, "tp"),
            P(None, "tp"),
            P("tp", None),
            P("replica", "tp", None),
            P("replica", "tp", None),
            P("replica"),
        ),
        out_specs=P("replica", None),
        check_vma=False,
    )
```

```python
import functools

import jax
import jax.numpy as jnp
from jax import lax
from jax.experimental import pallas as pl
from jax.experimental.pallas import tpu as pltpu
from jax.sharding import PartitionSpec as P

HD = 128
KVH = 8
HQ_DEV = 1
SPAN = 64
SEQS = 2
CTX_DEV = 64
TOKENS = SEQS * SPAN
MIB = 1024 * 1024

epsilon = 1e-05


def rms_rows(rows, gain):
    values_f = rows.astype(jnp.float32)
    factor = lax.rsqrt(jnp.mean(values_f * values_f, axis=-1, keepdims=True) + epsilon)
    return values_f * factor * gain.astype(jnp.float32)


def rope_tables(positions):
    half_width = HD // 2
    frequency = 500000.0 ** (-jnp.arange(half_width, dtype=jnp.float32) / half_width)
    angles = positions.astype(jnp.float32)[:, None] * frequency[None, :]
    return jnp.cos(angles), jnp.sin(angles)


def rotate(vectors, positions):
    half_width = vectors.shape[-1] // 2
    cosine, sine = rope_tables(positions)
    cosine, sine = cosine[:, None, :], sine[:, None, :]
    first_half = vectors[..., :half_width]
    second_half = vectors[..., half_width:]
    return jnp.concatenate(
        [first_half * cosine - second_half * sine, second_half * cosine + first_half * sine],
        axis=-1,
    )


CHIPS = 8
RING = (0, 2, 4, 6, 7, 5, 3, 1)
ONWARD = [(2 * RING[i], 2 * RING[(i + 1) % CHIPS]) for i in range(CHIPS)] + [
    (2 * RING[i] + 1, 2 * RING[i - 1] + 1) for i in range(CHIPS)
]
ENTER = [(2 * RING[i], 2 * RING[i - 1] + 1) for i in range(CHIPS)] + [
    (2 * RING[i] + 1, 2 * RING[(i + 1) % CHIPS]) for i in range(CHIPS)
]
LEAVE = [(2 * RING[i], 2 * RING[(i + 1) % CHIPS] + 1) for i in range(CHIPS)] + [
    (2 * RING[i] + 1, 2 * RING[i - 1]) for i in range(CHIPS)
]
SWAP = [(t, t ^ 1) for t in range(2 * CHIPS)]
STRAIGHT = [(k, 2 * k) for k in range(KVH)] + [(KVH + k, 2 * k + 1) for k in range(KVH)]
CROSSED = [(k, 2 * k + 1) for k in range(KVH)] + [(KVH + k, 2 * k) for k in range(KVH)]
VMEM = pl.BlockSpec(memory_space=pltpu.VMEM)
SMEM = pl.BlockSpec(memory_space=pltpu.SMEM)
HBM = pl.BlockSpec(memory_space=pltpu.HBM)


def ring_place(rank):
    chip = rank // 2
    return jnp.where(chip % 2 == 0, chip // 2, CHIPS - 1 - chip // 2)


def chip_at(place):
    place = place % CHIPS
    return jnp.where(place < CHIPS // 2, 2 * place, 2 * CHIPS - 1 - 2 * place)


def send(array, pairs):
    return lax.ppermute(array, "tp", pairs)


def xor(bits):
    return [(t, t ^ bits) for t in range(2 * CHIPS)]


def ring_gather(halves, own, work=None):
    straight, crossed = list(halves), own
    came = [(own,)]
    for step in range(1, 5):
        straight = [send(half, ONWARD) for half in straight]
        came.append(tuple(straight))
        if step < 4:
            if step == 3 and work is not None:
                crossed, work = lax.optimization_barrier((crossed, work))
            crossed = send(crossed, ENTER if step == 1 else ONWARD)
            came.append((crossed,))
    early, _ = lax.optimization_barrier((came[:5], came[5]))
    blocks = []
    for block in early + came[5:]:
        blocks += [block, tuple(send(piece, SWAP) for piece in block)]
    return blocks, work


def gathered_ids(rank):
    place, core = ring_place(rank), rank % 2
    ahead = 2 * core - 1
    ids = [rank, rank ^ 1]
    for step in range(1, 5):
        near, far = 2 * chip_at(place + ahead * step), 2 * chip_at(place - ahead * step)
        ids += [near + core, far + 1 - core]
        if step < 4:
            ids += [near + 1 - core, far + core]
    return jnp.stack(ids).astype(jnp.int32)


SHARES = ((4, 0), (3, 1), (3, 0), (2, 1), (2, 0), (1, 1), (1, 0), (0, 0))


def share_ids(rank):
    place, core = ring_place(rank), rank % 2
    return jnp.stack(
        [2 * chip_at(place + (1 - 2 * core) * d) + (core + other) % 2 for d, other in SHARES]
    ).astype(jnp.int32)


def ring_sum(shares):
    running = {0: shares[4, 0], 1: shares[3, 1]}
    for step in range(4, 0, -1):
        for other in range(2):
            if step == 4 and other == 1:
                continue
            if (step, other) not in ((4, 0), (3, 1)):
                running[other] = [
                    (part.astype(jnp.float32) + share).astype(jnp.bfloat16)
                    for part, share in zip(running[other], shares[step, other])
                ]
            pairs = LEAVE if (step, other) == (1, 1) else ONWARD
            running[other] = [send(part, pairs) for part in running[other]]
    return running[0], running[1][0]


def move_cache(key_cache, value_cache, rank, rank_id, after):
    core = rank % 2
    give = jnp.stack(
        [lax.dynamic_index_in_dim(c, 1 - core, 0, keepdims=False) for c in (key_cache, value_cache)]
    )
    keep, give = pack(rank_id, key_cache, value_cache, send(give, SWAP))
    came = send(give, xor(2))
    pieces = [jnp.stack([keep[m], came[m]]) for m in range(1, 4)]
    pieces, _ = lax.optimization_barrier((pieces, after))
    return [keep, came] + [send(piece, xor(4 * m)) for m, piece in zip(range(1, 4), pieces)]


def pack_kernel(rank, keys, values, theirs, keep, give):
    me = rank[0]
    for m in range(4):
        for j, out in enumerate((keep, give)):
            chip = (me ^ (4 * m + 2 * j)) // 2
            head = pl.ds(pl.multiple_of(chip * HD, HD), HD)
            out[m, 0, 0] = keys[me % 2, :, head]
            out[m, 0, 1] = values[me % 2, :, head]
            out[m, 1, 0] = theirs[0, :, head]
            out[m, 1, 1] = theirs[1, :, head]


def pack(rank_id, key_cache, value_cache, theirs):
    return pl.pallas_call(
        pack_kernel,
        out_shape=[jax.ShapeDtypeStruct((4, 2, 2, CTX_DEV, HD), jnp.bfloat16)] * 2,
        in_specs=[SMEM] + [VMEM] * 3,
        out_specs=[VMEM] * 2,
        compiler_params=pltpu.CompilerParams(vmem_limit_bytes=8 * MIB),
        cost_estimate=pl.CostEstimate(flops=0, bytes_accessed=MIB, transcendentals=0),
        name="pack_cache",
    )(rank_id, key_cache, value_cache, theirs)


def flat(blocks):
    return [piece for block in blocks for piece in block]


def grouped(refs, counts):
    blocks, at = [], 0
    for count in counts:
        blocks.append(refs[at : at + count])
        at += count
    return blocks


def lanes(block, j):
    parts = [piece[:, 128 * j : 128 * j + 128] for piece in block]
    return (parts[0] if len(parts) == 1 else jnp.concatenate(parts, axis=0)).astype(jnp.float32)


def square_sums(blocks, total):
    for block in blocks:
        for j in range(block[0].shape[1] // 128):
            v = lanes(block, j)
            total = total + v * v
    return total


def row_factors(squares, features):
    mean = jnp.sum(squares, axis=1, keepdims=True) * (1.0 / features)
    return lax.rsqrt(mean + epsilon)


def normed_block(block, factors, gain_row):
    return jnp.concatenate(
        [
            (lanes(block, j) * factors * gain_row[:, 128 * j : 128 * j + 128]).astype(jnp.bfloat16)
            for j in range(block[0].shape[1] // 128)
        ],
        axis=1,
    )


def squares_kernel(counts, *refs):
    out = refs[-1]
    out[...] = square_sums(grouped(refs[:-1], counts), jnp.zeros((TOKENS, 128), jnp.float32))


def squares_of(blocks):
    pieces = flat(blocks)
    return pl.pallas_call(
        functools.partial(squares_kernel, [len(block) for block in blocks]),
        out_shape=jax.ShapeDtypeStruct((TOKENS, 128), jnp.float32),
        in_specs=[VMEM] * len(pieces),
        out_specs=VMEM,
        compiler_params=pltpu.CompilerParams(vmem_limit_bytes=16 * MIB),
        cost_estimate=pl.CostEstimate(
            flops=4 * MIB, bytes_accessed=len(blocks) * MIB // 4, transcendentals=0
        ),
        name="squares",
    )(*pieces)


def in_hbm(array):
    return pltpu.with_memory_space_constraint(array, pltpu.HBM)


def load_kernel(ids, wq, wkv, out, sems):
    count, width, _ = out.shape
    copies = []
    for i in range(count):
        rows = pl.ds(pl.multiple_of(ids[i] * width, width), width)
        for j, weight in enumerate((wq, wkv)):
            copies.append(
                pltpu.make_async_copy(
                    weight.at[rows, :], out.at[i, :, pl.ds(j * HD, HD)], sems.at[j, i]
                )
            )
            copies[-1].start()
    for copy in copies:
        copy.wait()


def load_weights(ids, wq, wkv, width):
    return pl.pallas_call(
        load_kernel,
        out_shape=jax.ShapeDtypeStruct((16, width, 2 * HD), jnp.bfloat16),
        in_specs=[SMEM] + [HBM] * 2,
        out_specs=VMEM,
        scratch_shapes=[pltpu.SemaphoreType.DMA((2, 16))],
        compiler_params=pltpu.CompilerParams(vmem_limit_bytes=16 * MIB),
        cost_estimate=pl.CostEstimate(flops=0, bytes_accessed=16 * MIB, transcendentals=0),
        name="load_weights",
    )(ids, in_hbm(wq), in_hbm(wkv))


def project_kernel(counts, ids, *refs):
    blocks, refs = grouped(refs, counts), refs[sum(counts) :]
    squares, gain, weights, cosine, sine, kv_cos, kv_sin = refs[:7]
    q_keep, q_send, kv_straight, kv_crossed = refs[7:11]
    features = 16 * blocks[0][0].shape[1]
    factors = row_factors(square_sums(blocks[14:15] + blocks[1::2], squares[...]), features)
    total = jnp.zeros((TOKENS, 2 * HD), jnp.float32)
    for i in range(16):
        normed = normed_block(blocks[i], factors, gain[ids[i]])
        total = total + jnp.dot(normed, weights[i], preferred_element_type=jnp.float32)
    q, kv = total[:, :HD], total[:, HD:]
    q = (q * cosine[...] + pltpu.roll(q, HD // 2, 1) * sine[...]).astype(jnp.bfloat16)
    kv = (kv * kv_cos[...] + pltpu.roll(kv, HD // 2, 1) * kv_sin[...]).astype(jnp.bfloat16)
    core_one = ids[0] % 2 == 1
    holds_keys = ids[0] < KVH
    first, second = slice(0, SPAN), slice(SPAN, TOKENS)
    q_keep[...] = jnp.where(core_one, q[second], q[first])
    q_send[...] = jnp.where(core_one, q[first], q[second])
    kv_straight[...] = jnp.where(holds_keys, kv[first], kv[second])
    kv_crossed[...] = jnp.where(holds_keys, kv[second], kv[first])


def project(ids, blocks, squares, gain, weights, tables):
    pieces = flat(blocks)
    return pl.pallas_call(
        functools.partial(project_kernel, [len(block) for block in blocks]),
        out_shape=[jax.ShapeDtypeStruct((SPAN, HD), jnp.bfloat16)] * 4,
        in_specs=[SMEM] + [VMEM] * (len(pieces) + 7),
        out_specs=[VMEM] * 4,
        compiler_params=pltpu.CompilerParams(vmem_limit_bytes=24 * MIB),
        cost_estimate=pl.CostEstimate(
            flops=2 * TOKENS * weights.size, bytes_accessed=12 * MIB, transcendentals=0
        ),
        name="norm_project",
    )(ids, *pieces, squares, gain, weights, *tables)


def share_copies(to, first, weight, weight_other, out, sems):
    count, _, width = out.shape
    copies = []
    for i in range(count):
        columns = pl.ds(pl.multiple_of(to[first + i] * width, width), width)
        pair = [
            pltpu.make_async_copy(part.at[:, columns], out.at[i, pl.ds(j * HD, HD), :], sems.at[j, i])
            for j, part in enumerate((weight, weight_other))
        ]
        for copy in pair:
            copy.start()
        copies.append(pair)
    return copies


def cache_rows(cache, which):
    keep, came, rest = cache[0], cache[1], cache[2:]
    groups = [part[0, c, which] for part in (keep, came) for c in range(2)]
    groups += [part[x, c, which] for part in rest for x in range(2) for c in range(2)]
    return jnp.concatenate(groups, axis=0)


CONTRACT = (((1,), (1,)), ((), ()))


def scores_kernel(info, to, q, q_other, *refs):
    cache, weight, weight_other, scores, weights, sems = refs[:5], *refs[5:]
    copies = share_copies(to, 0, weight, weight_other, weights, sems)
    core, rank = info[SEQS], info[SEQS + 1]
    queries = jnp.concatenate([q[...], q_other[...]], axis=0)
    old = lax.dot_general(
        queries, cache_rows(cache, 0), CONTRACT, preferred_element_type=jnp.float32
    )
    lane = lax.broadcasted_iota(jnp.int32, old.shape, 1)
    position = (rank ^ (lane // CTX_DEV)) * CTX_DEV + lane % CTX_DEV
    scores[...] = jnp.where(position < info[core], old * HD ** (-0.5), -1e30)
    for pair in copies:
        for copy in pair:
            copy.wait()


def cache_scores(info, to, q, q_other, cache, weight, weight_other, ahead):
    width = weight.shape[1] // 16
    return pl.pallas_call(
        scores_kernel,
        out_shape=[
            jax.ShapeDtypeStruct((TOKENS, 16 * CTX_DEV), jnp.float32),
            jax.ShapeDtypeStruct((ahead, 2 * HD, width), jnp.bfloat16),
        ],
        in_specs=[SMEM] * 2 + [VMEM] * 7 + [HBM] * 2,
        out_specs=[VMEM] * 2,
        scratch_shapes=[pltpu.SemaphoreType.DMA((2, ahead))],
        compiler_params=pltpu.CompilerParams(vmem_limit_bytes=16 * MIB),
        cost_estimate=pl.CostEstimate(
            flops=32 * MIB, bytes_accessed=3 * MIB, transcendentals=0
        ),
        name="cache_scores",
    )(info, to, q, q_other, *cache, in_hbm(weight), weight_other)


def attend_kernel(info, q, q_other, straight, crossed, scores, *refs):
    cache, out = refs[:5], refs[5]
    core = info[SEQS]
    fresh_keys = jnp.where(core == 0, straight[...], crossed[...])
    fresh_values = jnp.where(core == 0, crossed[...], straight[...])
    queries = jnp.concatenate([q[...], q_other[...]], axis=0)
    old = scores[...]
    valid = old > -1e29
    fresh = lax.dot_general(
        queries, fresh_keys, CONTRACT, preferred_element_type=jnp.float32
    ) * HD ** (-0.5)
    place = lax.broadcasted_iota(jnp.int32, fresh.shape, 0) % SPAN
    causal = place >= lax.broadcasted_iota(jnp.int32, fresh.shape, 1)
    fresh = jnp.where(causal, fresh, -1e30)
    most = jnp.maximum(jnp.max(old, axis=1, keepdims=True), jnp.max(fresh, axis=1, keepdims=True))
    old_weights = jnp.where(valid, jnp.exp(old - most), 0.0)
    fresh_weights = jnp.where(causal, jnp.exp(fresh - most), 0.0)
    totals = jnp.sum(old_weights, axis=1, keepdims=True) + jnp.sum(
        fresh_weights, axis=1, keepdims=True
    )
    summed = jnp.dot(
        old_weights.astype(jnp.bfloat16), cache_rows(cache, 1), preferred_element_type=jnp.float32
    ) + jnp.dot(
        fresh_weights.astype(jnp.bfloat16), fresh_values, preferred_element_type=jnp.float32
    )
    attn = (summed / totals).astype(jnp.bfloat16)
    out[:, :HD] = attn[:SPAN]
    out[:, HD:] = attn[SPAN:]


def attend(info, q, q_other, straight, crossed, scores, cache):
    return pl.pallas_call(
        attend_kernel,
        out_shape=jax.ShapeDtypeStruct((SPAN, 2 * HD), jnp.bfloat16),
        in_specs=[SMEM] + [VMEM] * 10,
        out_specs=VMEM,
        compiler_params=pltpu.CompilerParams(vmem_limit_bytes=16 * MIB),
        cost_estimate=pl.CostEstimate(
            flops=48 * MIB, bytes_accessed=2 * MIB, transcendentals=TOKENS * 1088
        ),
        name="attend",
    )(info, q, q_other, straight, crossed, scores, *cache)


def both_heads(core, attn, attn_other):
    mine = attn[...]
    theirs = jnp.concatenate([attn_other[:, HD:], attn_other[:, :HD]], axis=1)
    core_one = core[0] == 1
    return jnp.concatenate(
        [jnp.where(core_one, theirs, mine), jnp.where(core_one, mine, theirs)], axis=0
    )


def share_shapes(shares, width, dtype):
    half, whole = [((SPAN, width), dtype)] * 2, [((TOKENS, width), dtype)]
    return [jax.ShapeDtypeStruct(*s) for _, other in shares for s in (whole if other else half)]


def share_lists(shares, arrays):
    arrays = list(arrays)
    return {key: [arrays.pop(0) for _ in range(2 - key[1])] for key in shares}


def write_share(value, outs):
    rows = TOKENS // len(outs)
    for i, out in enumerate(outs):
        out[...] = value[i * rows : (i + 1) * rows].astype(out.dtype)


def first_shares_kernel(shares, core, attn, attn_other, weights, *outs):
    rows = both_heads(core, attn, attn_other)
    for i, refs in enumerate(share_lists(shares, outs).values()):
        write_share(jnp.dot(rows, weights[i], preferred_element_type=jnp.float32), refs)


def first_shares(shares, core, attn, attn_other, weights):
    count, _, width = weights.shape
    out_shape = share_shapes(shares, width, jnp.bfloat16)
    arrays = pl.pallas_call(
        functools.partial(first_shares_kernel, shares),
        out_shape=out_shape,
        in_specs=[SMEM] + [VMEM] * 3,
        out_specs=[VMEM] * len(out_shape),
        compiler_params=pltpu.CompilerParams(vmem_limit_bytes=16 * MIB),
        cost_estimate=pl.CostEstimate(
            flops=2 * TOKENS * weights.size, bytes_accessed=count * MIB, transcendentals=0
        ),
        name="first_shares",
    )(core, attn, attn_other, weights)
    return share_lists(shares, arrays)


def more_shares_kernel(first, core, to, attn, attn_other, weight, weight_other, *refs):
    outs, (weights, sems) = refs[:-2], refs[-2:]
    copies = share_copies(to, first, weight, weight_other, weights, sems)
    rows = both_heads(core, attn, attn_other)
    for i, out in enumerate(share_lists(SHARES[first:], outs).values()):
        for copy in copies[i]:
            copy.wait()
        write_share(jnp.dot(rows, weights[i], preferred_element_type=jnp.float32), out)


def more_shares(core, to, attn, attn_other, weight, weight_other, first):
    count, width = len(SHARES) - first, weight.shape[1] // 16
    out_shape = share_shapes(SHARES[first:], width, jnp.float32)
    arrays = pl.pallas_call(
        functools.partial(more_shares_kernel, first),
        out_shape=out_shape,
        in_specs=[SMEM] * 2 + [VMEM] * 2 + [HBM] * 2,
        out_specs=[VMEM] * len(out_shape),
        scratch_shapes=[
            pltpu.VMEM((count, 2 * HD, width), jnp.bfloat16),
            pltpu.SemaphoreType.DMA((2, count)),
        ],
        compiler_params=pltpu.CompilerParams(vmem_limit_bytes=16 * MIB),
        cost_estimate=pl.CostEstimate(
            flops=4 * TOKENS * HD * width * count,
            bytes_accessed=count * MIB,
            transcendentals=0,
        ),
        name="more_shares",
    )(core, to, attn, attn_other, in_hbm(weight), weight_other)
    return share_lists(SHARES[first:], arrays)


def final_kernel(counts, ids, *refs):
    blocks, refs = grouped(refs, counts), refs[sum(counts) :]
    squares, gain, out, staged, sems = refs
    width = blocks[0][0].shape[1]
    factors = row_factors(square_sums(blocks[14:15] + blocks[1::2], squares[...]), 16 * width)
    copies = []
    for i in range(16):
        staged[i] = normed_block(blocks[i], factors, gain[ids[i]])
        copy = pltpu.make_async_copy(
            staged.at[i],
            out.at[:, pl.ds(pl.multiple_of(ids[i] * width, width), width)],
            sems.at[i],
        )
        copy.start()
        copies.append(copy)
    for copy in copies:
        copy.wait()


def final_norm(ids, blocks, squares, gain):
    pieces = flat(blocks)
    width = pieces[0].shape[1]
    return pl.pallas_call(
        functools.partial(final_kernel, [len(block) for block in blocks]),
        out_shape=jax.ShapeDtypeStruct((TOKENS, 16 * width), jnp.bfloat16),
        in_specs=[SMEM] + [VMEM] * (len(pieces) + 2),
        out_specs=HBM,
        scratch_shapes=[
            pltpu.VMEM((16, TOKENS, width), jnp.bfloat16),
            pltpu.SemaphoreType.DMA((16,)),
        ],
        compiler_params=pltpu.CompilerParams(vmem_limit_bytes=24 * MIB),
        cost_estimate=pl.CostEstimate(
            flops=16 * MIB, bytes_accessed=12 * MIB, transcendentals=0
        ),
        name="final_norm",
    )(ids, *pieces, squares, gain)


def per_device_ring(
    residual, attn_gain, ffn_gain, q_weight, kv_weight, o_weight, key_cache, value_cache, prefix
):
    rank = lax.axis_index("tp")
    core = rank % 2
    width = residual.shape[1]
    ids = gathered_ids(rank)
    to = share_ids(rank)
    core_id, rank_id = core[None].astype(jnp.int32), rank[None].astype(jnp.int32)
    info = jnp.concatenate([prefix, core_id, rank_id])

    weights = load_weights(ids, q_weight, kv_weight, width)
    residual_halves = [residual[:SPAN], residual[SPAN:]]
    blocks, weights = ring_gather(residual_halves, residual, weights)
    weight_other = send(o_weight, SWAP)
    cache = move_cache(key_cache, value_cache, rank, rank_id, blocks[12])

    positions = (prefix[:, None] + jnp.arange(SPAN, dtype=jnp.int32)[None, :]).reshape(-1)
    cosine, sine = rope_tables(positions)
    cosine = jnp.concatenate([cosine, cosine], axis=1)
    sine = jnp.concatenate([-sine, sine], axis=1)
    holds_keys = rank < KVH
    tables = (cosine, sine, jnp.where(holds_keys, cosine, 1.0), jnp.where(holds_keys, sine, 0.0))

    gain = attn_gain.reshape(16, 1, width).astype(jnp.float32)
    squares = squares_of(blocks[:14:2])
    q_keep, q_send, straight, crossed = project(
        ids, blocks, squares, gain, weights, tables
    )
    q_other = send(q_send, SWAP)
    scores, first_weights = cache_scores(
        info, to, q_keep, q_other, cache, o_weight, weight_other, 2
    )
    attn = attend(
        info, q_keep, q_other, send(straight, STRAIGHT), send(crossed, CROSSED), scores, cache
    )
    attn_other = send(attn, SWAP)

    shares = first_shares(SHARES[:2], core_id, attn, attn_other, first_weights)
    shares.update(more_shares(core_id, to, attn, attn_other, o_weight, weight_other, 2))
    one_way, other_way = ring_sum(shares)
    hidden = []
    for h, rows in enumerate((slice(0, SPAN), slice(SPAN, TOKENS))):
        projected = shares[0, 0][h] + one_way[h].astype(jnp.float32)
        projected = projected + other_way[rows].astype(jnp.float32)
        hidden.append((residual_halves[h].astype(jnp.float32) + projected).astype(jnp.bfloat16))

    blocks, _ = ring_gather(hidden, jnp.concatenate(hidden, axis=0))
    gain = ffn_gain.reshape(16, 1, width).astype(jnp.float32)
    squares = squares_of(blocks[:14:2])
    return final_norm(ids, blocks, squares, gain)


def per_device(
    residual, attn_gain, ffn_gain, q_weight, kv_weight, o_weight, key_cache, value_cache, prefix
):
    tp_count = lax.axis_size("tp")
    tp_rank = lax.axis_index("tp")
    heads_all = HQ_DEV * tp_count
    group_size = heads_all // KVH
    token_count = SEQS * SPAN
    score_scale = HD ** (-0.5)
    whole_rows = lax.all_gather(residual, "tp", axis=1, tiled=True)
    normed = rms_rows(whole_rows, attn_gain).astype(jnp.bfloat16)
    positions = (prefix[:, None] + jnp.arange(SPAN, dtype=jnp.int32)[None, :]).reshape(-1)
    queries = jnp.dot(normed, q_weight, preferred_element_type=jnp.float32).reshape(
        token_count, HQ_DEV, HD
    )
    queries = rotate(queries, positions).astype(jnp.bfloat16)
    kv_part = jnp.dot(normed, kv_weight, preferred_element_type=jnp.float32)
    kv_whole = lax.all_gather(kv_part, "tp", axis=1, tiled=True)
    new_keys = rotate(kv_whole[:, : KVH * HD].reshape(token_count, KVH, HD), positions).astype(
        jnp.bfloat16
    )
    new_values = kv_whole[:, KVH * HD :].reshape(token_count, KVH, HD).astype(jnp.bfloat16)
    head_ids = tp_rank * HQ_DEV + jnp.arange(HQ_DEV, dtype=jnp.int32)
    own_kv = head_ids // group_size
    own_keys = jnp.take(new_keys, own_kv, axis=1).reshape(SEQS, SPAN, HQ_DEV, HD)
    own_values = jnp.take(new_values, own_kv, axis=1).reshape(SEQS, SPAN, HQ_DEV, HD)
    own_queries = queries.reshape(SEQS, SPAN, HQ_DEV, HD)
    causal = (jnp.arange(SPAN)[:, None] >= jnp.arange(SPAN)[None, :])[None, None]
    fresh_scores = (
        jnp.einsum("schd,skhd->shck", own_queries, own_keys, preferred_element_type=jnp.float32)
        * score_scale
    )
    fresh_scores = jnp.where(causal, fresh_scores, -1e30)
    fresh_max = fresh_scores.max(-1)
    gathered = lax.all_gather(queries.reshape(token_count, HQ_DEV * HD), "tp", axis=1, tiled=True)
    queries_all = gathered.reshape(SEQS, SPAN, KVH, group_size, HD)
    keys_local = key_cache.reshape(SEQS, CTX_DEV, KVH, HD)
    values_local = value_cache.reshape(SEQS, CTX_DEV, KVH, HD)
    local_scores = (
        jnp.einsum("sckgd,sjkd->skgcj", queries_all, keys_local, preferred_element_type=jnp.float32)
        * score_scale
    )
    first_slot = tp_rank * CTX_DEV
    is_valid = ((first_slot + jnp.arange(CTX_DEV, dtype=jnp.int32))[None, :] < prefix[:, None])[
        :, None, None, None, :
    ]
    local_scores = jnp.where(is_valid, local_scores, -1e30)
    local_max = local_scores.max(-1)
    local_weights = jnp.where(is_valid, jnp.exp(local_scores - local_max[..., None]), 0.0)
    local_total = local_weights.sum(-1)
    local_sum = jnp.einsum(
        "skgcj,sjkd->skgcd",
        local_weights.astype(jnp.bfloat16),
        values_local,
        preferred_element_type=jnp.float32,
    )
    sums_in, maxes_in, totals_in = (
        lax.all_to_all(
            local_sum.reshape(1, SEQS, heads_all, SPAN, HD),
            "tp",
            split_axis=2,
            concat_axis=0,
            tiled=True,
        ),
        lax.all_to_all(
            local_max.reshape(1, SEQS, heads_all, SPAN),
            "tp",
            split_axis=2,
            concat_axis=0,
            tiled=True,
        ),
        lax.all_to_all(
            local_total.reshape(1, SEQS, heads_all, SPAN),
            "tp",
            split_axis=2,
            concat_axis=0,
            tiled=True,
        ),
    )
    running_max = jnp.maximum(maxes_in.max(0), fresh_max)
    factors = jnp.exp(maxes_in - running_max[None])
    fresh_weights = jnp.where(causal, jnp.exp(fresh_scores - running_max[..., None]), 0.0)
    totals = (factors * totals_in).sum(0) + fresh_weights.sum(-1)
    summed = (factors[..., None] * sums_in).sum(0)
    summed = summed + jnp.einsum(
        "shck,skhd->shcd",
        fresh_weights.astype(jnp.bfloat16),
        own_values,
        preferred_element_type=jnp.float32,
    )
    attn = (summed / totals[..., None]).astype(jnp.bfloat16)
    attn = jnp.transpose(attn, (0, 2, 1, 3)).reshape(token_count, HQ_DEV * HD)
    share_part = lax.psum_scatter(
        lax.dot_general(
            o_weight, attn, (((0,), (1,)), ((), ())), preferred_element_type=jnp.float32
        ),
        "tp",
        scatter_dimension=0,
        tiled=True,
    )
    hidden = (residual.astype(jnp.float32) + share_part.T).astype(jnp.bfloat16)
    stream = lax.all_gather(hidden, "tp", axis=1, tiled=True)
    return rms_rows(stream, ffn_gain).astype(jnp.bfloat16)


def solution(mesh):
    return jax.shard_map(
        per_device_ring if mesh.shape["tp"] == 2 * CHIPS else per_device,
        mesh=mesh,
        in_specs=(
            P("replica", "tp"),
            P(),
            P(),
            P(None, "tp"),
            P(None, "tp"),
            P("tp", None),
            P("replica", "tp", None),
            P("replica", "tp", None),
            P("replica"),
        ),
        out_specs=P("replica", None),
        check_vma=False,
    )
```

```python
import functools

import jax
import jax.numpy as jnp
from jax import lax
from jax.experimental import pallas as pl
from jax.experimental.pallas import tpu as pltpu
from jax.sharding import PartitionSpec as P

HD = 128
KVH = 8
HQ_DEV = 1
SPAN = 64
SEQS = 2
CTX_DEV = 64
TOKENS = SEQS * SPAN
MIB = 1024 * 1024

epsilon = 1e-05


def rms_rows(rows, gain):
    values_f = rows.astype(jnp.float32)
    factor = lax.rsqrt(jnp.mean(values_f * values_f, axis=-1, keepdims=True) + epsilon)
    return values_f * factor * gain.astype(jnp.float32)


def rope_tables(positions):
    half_width = HD // 2
    frequency = 500000.0 ** (-jnp.arange(half_width, dtype=jnp.float32) / half_width)
    angles = positions.astype(jnp.float32)[:, None] * frequency[None, :]
    return jnp.cos(angles), jnp.sin(angles)


def rotate(vectors, positions):
    half_width = vectors.shape[-1] // 2
    cosine, sine = rope_tables(positions)
    cosine, sine = cosine[:, None, :], sine[:, None, :]
    first_half = vectors[..., :half_width]
    second_half = vectors[..., half_width:]
    return jnp.concatenate(
        [first_half * cosine - second_half * sine, second_half * cosine + first_half * sine],
        axis=-1,
    )


CHIPS = 8
RING = (0, 2, 4, 6, 7, 5, 3, 1)
ONWARD = [(2 * RING[i], 2 * RING[(i + 1) % CHIPS]) for i in range(CHIPS)] + [
    (2 * RING[i] + 1, 2 * RING[i - 1] + 1) for i in range(CHIPS)
]
ENTER = [(2 * RING[i], 2 * RING[i - 1] + 1) for i in range(CHIPS)] + [
    (2 * RING[i] + 1, 2 * RING[(i + 1) % CHIPS]) for i in range(CHIPS)
]
LEAVE = [(2 * RING[i], 2 * RING[(i + 1) % CHIPS] + 1) for i in range(CHIPS)] + [
    (2 * RING[i] + 1, 2 * RING[i - 1]) for i in range(CHIPS)
]
SWAP = [(t, t ^ 1) for t in range(2 * CHIPS)]
FRESH = [(k, 2 * k) for k in range(KVH)] + [(KVH + k, 2 * k + 1) for k in range(KVH)]
VMEM = pl.BlockSpec(memory_space=pltpu.VMEM)
SMEM = pl.BlockSpec(memory_space=pltpu.SMEM)
HBM = pl.BlockSpec(memory_space=pltpu.HBM)


def ring_place(rank):
    chip = rank // 2
    return jnp.where(chip % 2 == 0, chip // 2, CHIPS - 1 - chip // 2)


def chip_at(place):
    place = place % CHIPS
    return jnp.where(place < CHIPS // 2, 2 * place, 2 * CHIPS - 1 - 2 * place)


def send(array, pairs):
    return lax.ppermute(array, "tp", pairs)


def xor(bits):
    return [(t, t ^ bits) for t in range(2 * CHIPS)]


def after(array, *others):
    return lax.optimization_barrier((array, others))[0]


def ring_gather(parts, own, ready=None):
    streams, crossed = list(parts), own
    came = [(own,)]
    for step in range(1, 5):
        if step == 4 and ready is not None:
            streams = after(streams, ready)
        streams = [send(part, ONWARD) for part in streams]
        came.append(tuple(streams))
        if step < 4:
            crossed = send(crossed, ENTER if step == 1 else ONWARD)
            came.append((crossed,))
    return came


def both_cores(came):
    mine = flat(came)
    return mine + [send(piece, SWAP) for piece in mine]


def block_refs(refs, parts):
    counts = (1,) + (parts, 1) * 3 + (parts,)
    return grouped(refs, counts * 2)


def gathered_ids(rank):
    place = ring_place(rank)
    ids = []
    for side in range(2):
        device = rank ^ side
        core = device % 2
        ids.append(device)
        for step in range(1, 5):
            chip = 2 * chip_at(place + (2 * core - 1) * step)
            ids += [chip + core, chip + 1 - core] if step < 4 else [chip + core]
    return jnp.stack(ids).astype(jnp.int32)


SHARES = ((4, 0), (3, 1), (3, 0), (2, 1), (2, 0), (1, 1), (1, 0), (0, 0))


def share_ids(rank):
    place, core = ring_place(rank), rank % 2
    return jnp.stack(
        [2 * chip_at(place + (1 - 2 * core) * d) + (core + other) % 2 for d, other in SHARES]
    ).astype(jnp.int32)


def ring_sum(shares, more_shares):
    streams, crossed = shares[4, 0], shares[3, 1][0]
    for step in range(1, 5):
        streams = [send(part, ONWARD) for part in streams]
        if step < 4:
            crossed = send(crossed, LEAVE if step == 3 else ONWARD)
        if step == 1:
            shares.update(more_shares(streams[0]))
        if step < 4:
            streams = [add_share(part, share) for part, share in zip(streams, shares[4 - step, 0])]
        if step < 3:
            crossed = add_share(crossed, shares[3 - step, 1][0])
    return streams, crossed


def add_share(part, share):
    return (part.astype(jnp.float32) + share).astype(jnp.bfloat16)


def split_cache(key_cache, value_cache, rank, rank_id):
    core = rank % 2
    give = jnp.stack(
        [lax.dynamic_index_in_dim(c, 1 - core, 0, keepdims=False) for c in (key_cache, value_cache)]
    )
    return pack(rank_id, key_cache, value_cache, send(give, SWAP))


def move_cache(parts, *when):
    keep, give = parts
    came = send(give, xor(2))
    pieces = [jnp.stack([keep[m], came[m]]) for m in range(1, 4)]
    return [keep, came] + [send(piece, xor(4 * m)) for m, piece in zip(range(1, 4), pieces)]


def pack_kernel(rank, keys, values, theirs, keep, give, sems):
    me = rank[0]
    copies = []
    for m in range(4):
        for j, out in enumerate((keep, give)):
            chip = (me ^ (4 * m + 2 * j)) // 2
            head = pl.ds(pl.multiple_of(chip * HD, HD), HD)
            for k, cache in enumerate((keys, values)):
                copies.append(
                    pltpu.make_async_copy(
                        cache.at[me % 2, :, head], out.at[m, 0, k], sems.at[m, j, k]
                    )
                )
                copies[-1].start()
            out[m, 1, 0] = theirs[0, :, head]
            out[m, 1, 1] = theirs[1, :, head]
    for copy in copies:
        copy.wait()


def pack(rank_id, key_cache, value_cache, theirs):
    return pl.pallas_call(
        pack_kernel,
        out_shape=[jax.ShapeDtypeStruct((4, 2, 2, CTX_DEV, HD), jnp.bfloat16)] * 2,
        in_specs=[SMEM] + [HBM] * 2 + [VMEM],
        out_specs=[VMEM] * 2,
        scratch_shapes=[pltpu.SemaphoreType.DMA((4, 2, 2))],
        compiler_params=pltpu.CompilerParams(vmem_limit_bytes=8 * MIB),
        cost_estimate=pl.CostEstimate(flops=0, bytes_accessed=MIB, transcendentals=0),
        name="pack_cache",
    )(rank_id, in_hbm(key_cache), in_hbm(value_cache), theirs)


def flat(blocks):
    return [piece for block in blocks for piece in block]


def grouped(refs, counts):
    blocks, at = [], 0
    for count in counts:
        blocks.append(refs[at : at + count])
        at += count
    return blocks


def lanes(block, j):
    parts = [piece[:, 128 * j : 128 * j + 128] for piece in block]
    return (parts[0] if len(parts) == 1 else jnp.concatenate(parts, axis=0)).astype(jnp.float32)


def square_sums(blocks, total):
    for block in blocks:
        for j in range(block[0].shape[1] // 128):
            v = lanes(block, j)
            total = total + v * v
    return total


def row_factors(squares, features):
    mean = jnp.sum(squares, axis=1, keepdims=True) * (1.0 / features)
    return lax.rsqrt(mean + epsilon)


def normed_block(block, factors, gain_row):
    return jnp.concatenate(
        [
            (lanes(block, j) * factors * gain_row[:, 128 * j : 128 * j + 128]).astype(jnp.bfloat16)
            for j in range(block[0].shape[1] // 128)
        ],
        axis=1,
    )


def in_hbm(array):
    return pltpu.with_memory_space_constraint(array, pltpu.HBM)


def load_kernel(ids, wq, wkv, out, sems):
    count, width, _ = out.shape
    copies = []
    for i in range(count):
        rows = pl.ds(pl.multiple_of(ids[i] * width, width), width)
        for j, weight in enumerate((wq, wkv)):
            copies.append(
                pltpu.make_async_copy(
                    weight.at[rows, :], out.at[i, :, pl.ds(j * HD, HD)], sems.at[j, i]
                )
            )
            copies[-1].start()
    for copy in copies:
        copy.wait()


def load_weights(ids, wq, wkv, width):
    return pl.pallas_call(
        load_kernel,
        out_shape=jax.ShapeDtypeStruct((16, width, 2 * HD), jnp.bfloat16),
        in_specs=[SMEM] + [HBM] * 2,
        out_specs=VMEM,
        scratch_shapes=[pltpu.SemaphoreType.DMA((2, 16))],
        compiler_params=pltpu.CompilerParams(vmem_limit_bytes=16 * MIB),
        cost_estimate=pl.CostEstimate(flops=0, bytes_accessed=16 * MIB, transcendentals=0),
        name="load_weights",
    )(ids, in_hbm(wq), in_hbm(wkv))


def all_factors(blocks):
    total = square_sums(blocks, jnp.zeros((TOKENS, 128), jnp.float32))
    return row_factors(total, 16 * blocks[0][0].shape[1])


def project_kernel(parts, ids, *refs):
    count = 8 * (parts + 1)
    blocks, refs = block_refs(refs[:count], parts), refs[count:]
    gain, weights, cosine, sine, kv_cos, kv_sin = refs[:6]
    q_keep, q_send, fresh = refs[6:]
    factors = all_factors(blocks)
    total = jnp.zeros((TOKENS, 2 * HD), jnp.float32)
    for i in range(16):
        normed = normed_block(blocks[i], factors, gain[ids[i]])
        total = total + jnp.dot(normed, weights[i], preferred_element_type=jnp.float32)
    q, kv = total[:, :HD], total[:, HD:]
    q = (q * cosine[...] + pltpu.roll(q, HD // 2, 1) * sine[...]).astype(jnp.bfloat16)
    kv = (kv * kv_cos[...] + pltpu.roll(kv, HD // 2, 1) * kv_sin[...]).astype(jnp.bfloat16)
    core_one = ids[0] % 2 == 1
    q_keep[...] = jnp.where(core_one, q[SPAN:], q[:SPAN])
    q_send[...] = jnp.where(core_one, q[:SPAN], q[SPAN:])
    fresh[...] = kv


def project(ids, arrays, gain, weights, tables):
    return pl.pallas_call(
        functools.partial(project_kernel, len(arrays) // 8 - 1),
        out_shape=[jax.ShapeDtypeStruct((SPAN, HD), jnp.bfloat16)] * 2
        + [jax.ShapeDtypeStruct((TOKENS, HD), jnp.bfloat16)],
        in_specs=[SMEM] + [VMEM] * (len(arrays) + 6),
        out_specs=[VMEM] * 3,
        compiler_params=pltpu.CompilerParams(vmem_limit_bytes=24 * MIB),
        cost_estimate=pl.CostEstimate(
            flops=2 * TOKENS * weights.size, bytes_accessed=12 * MIB, transcendentals=0
        ),
        name="norm_project",
    )(ids, *arrays, gain, weights, *tables)


def share_copies(to, first, weight, weight_other, out, sems):
    count, _, width = out.shape
    copies = []
    for i in range(count):
        columns = pl.ds(pl.multiple_of(to[first + i] * width, width), width)
        pair = [
            pltpu.make_async_copy(part.at[:, columns], out.at[i, pl.ds(j * HD, HD), :], sems.at[j, i])
            for j, part in enumerate((weight, weight_other))
        ]
        for copy in pair:
            copy.start()
        copies.append(pair)
    return copies


def cache_rows(cache, which):
    keep, came, rest = cache[0], cache[1], cache[2:]
    groups = [part[0, c, which] for part in (keep, came) for c in range(2)]
    groups += [part[x, c, which] for part in rest for x in range(2) for c in range(2)]
    return jnp.concatenate(groups, axis=0)


CONTRACT = (((1,), (1,)), ((), ()))


def scores_kernel(info, to, q, q_other, *refs):
    cache, weight, weight_other, scores, weights, sems = refs[:5], *refs[5:]
    copies = share_copies(to, 0, weight, weight_other, weights, sems)
    core, rank = info[SEQS], info[SEQS + 1]
    queries = jnp.concatenate([q[...], q_other[...]], axis=0)
    old = lax.dot_general(
        queries, cache_rows(cache, 0), CONTRACT, preferred_element_type=jnp.float32
    )
    lane = lax.broadcasted_iota(jnp.int32, old.shape, 1)
    position = (rank ^ (lane // CTX_DEV)) * CTX_DEV + lane % CTX_DEV
    scores[...] = jnp.where(position < info[core], old * HD ** (-0.5), -1e30)
    for pair in copies:
        for copy in pair:
            copy.wait()


def cache_scores(info, to, q, q_other, cache, weight, weight_other, ahead):
    width = weight.shape[1] // 16
    return pl.pallas_call(
        scores_kernel,
        out_shape=[
            jax.ShapeDtypeStruct((TOKENS, 16 * CTX_DEV), jnp.float32),
            jax.ShapeDtypeStruct((ahead, 2 * HD, width), jnp.bfloat16),
        ],
        in_specs=[SMEM] * 2 + [VMEM] * 7 + [HBM] * 2,
        out_specs=[VMEM] * 2,
        scratch_shapes=[pltpu.SemaphoreType.DMA((2, ahead))],
        compiler_params=pltpu.CompilerParams(vmem_limit_bytes=16 * MIB),
        cost_estimate=pl.CostEstimate(
            flops=32 * MIB, bytes_accessed=3 * MIB, transcendentals=0
        ),
        name="cache_scores",
    )(info, to, q, q_other, *cache, in_hbm(weight), weight_other)


def attend_kernel(info, q, q_other, fresh_own, fresh_other, scores, *refs):
    cache, out = refs[:5], refs[5]
    core = info[SEQS]
    came = fresh_other[...]
    fresh_keys = jnp.where(core == 0, fresh_own[:SPAN, :], came)
    fresh_values = jnp.where(core == 0, came, fresh_own[SPAN:, :])
    queries = jnp.concatenate([q[...], q_other[...]], axis=0)
    old = scores[...]
    valid = old > -1e29
    fresh = lax.dot_general(
        queries, fresh_keys, CONTRACT, preferred_element_type=jnp.float32
    ) * HD ** (-0.5)
    place = lax.broadcasted_iota(jnp.int32, fresh.shape, 0) % SPAN
    causal = place >= lax.broadcasted_iota(jnp.int32, fresh.shape, 1)
    fresh = jnp.where(causal, fresh, -1e30)
    most = jnp.maximum(jnp.max(old, axis=1, keepdims=True), jnp.max(fresh, axis=1, keepdims=True))
    old_weights = jnp.where(valid, jnp.exp(old - most), 0.0)
    fresh_weights = jnp.where(causal, jnp.exp(fresh - most), 0.0)
    totals = jnp.sum(old_weights, axis=1, keepdims=True) + jnp.sum(
        fresh_weights, axis=1, keepdims=True
    )
    summed = jnp.dot(
        old_weights.astype(jnp.bfloat16), cache_rows(cache, 1), preferred_element_type=jnp.float32
    ) + jnp.dot(
        fresh_weights.astype(jnp.bfloat16), fresh_values, preferred_element_type=jnp.float32
    )
    attn = (summed / totals).astype(jnp.bfloat16)
    out[:, :HD] = attn[:SPAN]
    out[:, HD:] = attn[SPAN:]


def attend(info, q, q_other, fresh_own, fresh_other, scores, cache):
    return pl.pallas_call(
        attend_kernel,
        out_shape=jax.ShapeDtypeStruct((SPAN, 2 * HD), jnp.bfloat16),
        in_specs=[SMEM] + [VMEM] * 10,
        out_specs=VMEM,
        compiler_params=pltpu.CompilerParams(vmem_limit_bytes=16 * MIB),
        cost_estimate=pl.CostEstimate(
            flops=48 * MIB, bytes_accessed=2 * MIB, transcendentals=TOKENS * 1088
        ),
        name="attend",
    )(info, q, q_other, fresh_own, fresh_other, scores, *cache)


def both_heads(core, attn, attn_other):
    mine = attn[...]
    theirs = jnp.concatenate([attn_other[:, HD:], attn_other[:, :HD]], axis=1)
    core_one = core[0] == 1
    return jnp.concatenate(
        [jnp.where(core_one, theirs, mine), jnp.where(core_one, mine, theirs)], axis=0
    )


def share_shapes(shares, width, dtype):
    half, whole = [((SPAN, width), dtype)] * 2, [((TOKENS, width), dtype)]
    return [jax.ShapeDtypeStruct(*s) for _, other in shares for s in (whole if other else half)]


def share_lists(shares, arrays):
    arrays = list(arrays)
    return {key: [arrays.pop(0) for _ in range(2 - key[1])] for key in shares}


def write_share(value, outs):
    rows = TOKENS // len(outs)
    for i, out in enumerate(outs):
        out[...] = value[i * rows : (i + 1) * rows].astype(out.dtype)


def first_shares_kernel(shares, core, attn, attn_other, weights, *outs):
    rows = both_heads(core, attn, attn_other)
    for i, refs in enumerate(share_lists(shares, outs).values()):
        write_share(jnp.dot(rows, weights[i], preferred_element_type=jnp.float32), refs)


def first_shares(shares, core, attn, attn_other, weights):
    count, _, width = weights.shape
    out_shape = share_shapes(shares, width, jnp.bfloat16)
    arrays = pl.pallas_call(
        functools.partial(first_shares_kernel, shares),
        out_shape=out_shape,
        in_specs=[SMEM] + [VMEM] * 3,
        out_specs=[VMEM] * len(out_shape),
        compiler_params=pltpu.CompilerParams(vmem_limit_bytes=16 * MIB),
        cost_estimate=pl.CostEstimate(
            flops=2 * TOKENS * weights.size, bytes_accessed=count * MIB, transcendentals=0
        ),
        name="first_shares",
    )(core, attn, attn_other, weights)
    return share_lists(shares, arrays)


def more_shares_kernel(first, last, core, to, attn, attn_other, weight, weight_other, *refs):
    outs, (weights, sems) = refs[:-2], refs[-2:]
    copies = share_copies(to, first, weight, weight_other, weights, sems)
    rows = both_heads(core, attn, attn_other)
    for i, out in enumerate(share_lists(SHARES[first:last], outs).values()):
        for copy in copies[i]:
            copy.wait()
        write_share(jnp.dot(rows, weights[i], preferred_element_type=jnp.float32), out)


def more_shares(core, to, attn, attn_other, weight, weight_other, first, last):
    count, width = last - first, weight.shape[1] // 16
    out_shape = share_shapes(SHARES[first:last], width, jnp.float32)
    arrays = pl.pallas_call(
        functools.partial(more_shares_kernel, first, last),
        out_shape=out_shape,
        in_specs=[SMEM] * 2 + [VMEM] * 2 + [HBM] * 2,
        out_specs=[VMEM] * len(out_shape),
        scratch_shapes=[
            pltpu.VMEM((count, 2 * HD, width), jnp.bfloat16),
            pltpu.SemaphoreType.DMA((2, count)),
        ],
        compiler_params=pltpu.CompilerParams(vmem_limit_bytes=16 * MIB),
        cost_estimate=pl.CostEstimate(
            flops=4 * TOKENS * HD * width * count,
            bytes_accessed=count * MIB,
            transcendentals=0,
        ),
        name="shares_%d" % first,
    )(core, to, attn, attn_other, in_hbm(weight), weight_other)
    return share_lists(SHARES[first:last], arrays)


def final_kernel(parts, ids, *refs):
    count = 8 * (parts + 1)
    blocks, refs = block_refs(refs[:count], parts), refs[count:]
    gain, out, staged, sems = refs
    width = staged.shape[2]
    factors = all_factors(blocks)
    copies = []
    for i in range(16):
        staged[i] = normed_block(blocks[i], factors, gain[ids[i]])
        copy = pltpu.make_async_copy(
            staged.at[i],
            out.at[:, pl.ds(pl.multiple_of(ids[i] * width, width), width)],
            sems.at[i],
        )
        copy.start()
        copies.append(copy)
    for copy in copies:
        copy.wait()


def final_norm(ids, arrays, gain):
    width = arrays[0].shape[1]
    return pl.pallas_call(
        functools.partial(final_kernel, len(arrays) // 8 - 1),
        out_shape=jax.ShapeDtypeStruct((TOKENS, 16 * width), jnp.bfloat16),
        in_specs=[SMEM] + [VMEM] * (len(arrays) + 1),
        out_specs=HBM,
        scratch_shapes=[
            pltpu.VMEM((16, TOKENS, width), jnp.bfloat16),
            pltpu.SemaphoreType.DMA((16,)),
        ],
        compiler_params=pltpu.CompilerParams(vmem_limit_bytes=24 * MIB),
        cost_estimate=pl.CostEstimate(
            flops=16 * MIB, bytes_accessed=12 * MIB, transcendentals=0
        ),
        name="final_norm",
    )(ids, *arrays, gain)


def per_device_ring(
    residual, attn_gain, ffn_gain, q_weight, kv_weight, o_weight, key_cache, value_cache, prefix
):
    rank = lax.axis_index("tp")
    core = rank % 2
    width = residual.shape[1]
    ids = gathered_ids(rank)
    to = share_ids(rank)
    core_id, rank_id = core[None].astype(jnp.int32), rank[None].astype(jnp.int32)
    info = jnp.concatenate([prefix, core_id, rank_id])

    weight_other = send(o_weight, SWAP)
    parts = split_cache(key_cache, value_cache, rank, rank_id)
    came = ring_gather([residual], residual, weight_other)
    weights = load_weights(ids, q_weight, kv_weight, width)
    cache = move_cache(parts)

    positions = (prefix[:, None] + jnp.arange(SPAN, dtype=jnp.int32)[None, :]).reshape(-1)
    cosine, sine = rope_tables(positions)
    cosine = jnp.concatenate([cosine, cosine], axis=1)
    sine = jnp.concatenate([-sine, sine], axis=1)
    holds_keys = rank < KVH
    tables = (cosine, sine, jnp.where(holds_keys, cosine, 1.0), jnp.where(holds_keys, sine, 0.0))

    gain = attn_gain.reshape(16, 1, width).astype(jnp.float32)
    arrays = both_cores(came)
    arrays[0] = after(arrays[0], cache[1])
    q_keep, q_send, fresh = project(ids, arrays, gain, weights, tables)
    q_other = send(q_send, SWAP)
    fresh_own = send(fresh, FRESH)
    fresh_other = send(jnp.where(core == 0, fresh_own[SPAN:], fresh_own[:SPAN]), SWAP)
    scores, first_weights = cache_scores(
        info, to, q_keep, q_other, cache, o_weight, weight_other, 2
    )
    attn = attend(info, q_keep, q_other, fresh_own, fresh_other, scores, cache)
    attn_other = send(attn, SWAP)

    shares = first_shares(SHARES[:2], core_id, attn, attn_other, first_weights)
    inputs = (attn, attn_other, o_weight, weight_other)
    shares.update(more_shares(core_id, to, *inputs, 2, 4))
    one_way, other_way = ring_sum(
        shares, lambda came: more_shares(core_id, after(to, came), *inputs, 4, len(SHARES))
    )
    hidden = []
    for h, rows in enumerate((slice(0, SPAN), slice(SPAN, TOKENS))):
        projected = shares[0, 0][h] + one_way[h].astype(jnp.float32)
        projected = projected + other_way[rows].astype(jnp.float32)
        hidden.append((residual[rows].astype(jnp.float32) + projected).astype(jnp.bfloat16))

    hidden = jnp.concatenate(hidden, axis=0)
    came = ring_gather([hidden], hidden)
    arrays = both_cores(came)
    gain = ffn_gain.reshape(16, 1, width).astype(jnp.float32)
    return final_norm(ids, arrays, gain)


def per_device(
    residual, attn_gain, ffn_gain, q_weight, kv_weight, o_weight, key_cache, value_cache, prefix
):
    tp_count = lax.axis_size("tp")
    tp_rank = lax.axis_index("tp")
    heads_all = HQ_DEV * tp_count
    group_size = heads_all // KVH
    token_count = SEQS * SPAN
    score_scale = HD ** (-0.5)
    whole_rows = lax.all_gather(residual, "tp", axis=1, tiled=True)
    normed = rms_rows(whole_rows, attn_gain).astype(jnp.bfloat16)
    positions = (prefix[:, None] + jnp.arange(SPAN, dtype=jnp.int32)[None, :]).reshape(-1)
    queries = jnp.dot(normed, q_weight, preferred_element_type=jnp.float32).reshape(
        token_count, HQ_DEV, HD
    )
    queries = rotate(queries, positions).astype(jnp.bfloat16)
    kv_part = jnp.dot(normed, kv_weight, preferred_element_type=jnp.float32)
    kv_whole = lax.all_gather(kv_part, "tp", axis=1, tiled=True)
    new_keys = rotate(kv_whole[:, : KVH * HD].reshape(token_count, KVH, HD), positions).astype(
        jnp.bfloat16
    )
    new_values = kv_whole[:, KVH * HD :].reshape(token_count, KVH, HD).astype(jnp.bfloat16)
    head_ids = tp_rank * HQ_DEV + jnp.arange(HQ_DEV, dtype=jnp.int32)
    own_kv = head_ids // group_size
    own_keys = jnp.take(new_keys, own_kv, axis=1).reshape(SEQS, SPAN, HQ_DEV, HD)
    own_values = jnp.take(new_values, own_kv, axis=1).reshape(SEQS, SPAN, HQ_DEV, HD)
    own_queries = queries.reshape(SEQS, SPAN, HQ_DEV, HD)
    causal = (jnp.arange(SPAN)[:, None] >= jnp.arange(SPAN)[None, :])[None, None]
    fresh_scores = (
        jnp.einsum("schd,skhd->shck", own_queries, own_keys, preferred_element_type=jnp.float32)
        * score_scale
    )
    fresh_scores = jnp.where(causal, fresh_scores, -1e30)
    fresh_max = fresh_scores.max(-1)
    gathered = lax.all_gather(queries.reshape(token_count, HQ_DEV * HD), "tp", axis=1, tiled=True)
    queries_all = gathered.reshape(SEQS, SPAN, KVH, group_size, HD)
    keys_local = key_cache.reshape(SEQS, CTX_DEV, KVH, HD)
    values_local = value_cache.reshape(SEQS, CTX_DEV, KVH, HD)
    local_scores = (
        jnp.einsum("sckgd,sjkd->skgcj", queries_all, keys_local, preferred_element_type=jnp.float32)
        * score_scale
    )
    first_slot = tp_rank * CTX_DEV
    is_valid = ((first_slot + jnp.arange(CTX_DEV, dtype=jnp.int32))[None, :] < prefix[:, None])[
        :, None, None, None, :
    ]
    local_scores = jnp.where(is_valid, local_scores, -1e30)
    local_max = local_scores.max(-1)
    local_weights = jnp.where(is_valid, jnp.exp(local_scores - local_max[..., None]), 0.0)
    local_total = local_weights.sum(-1)
    local_sum = jnp.einsum(
        "skgcj,sjkd->skgcd",
        local_weights.astype(jnp.bfloat16),
        values_local,
        preferred_element_type=jnp.float32,
    )
    sums_in, maxes_in, totals_in = (
        lax.all_to_all(
            local_sum.reshape(1, SEQS, heads_all, SPAN, HD),
            "tp",
            split_axis=2,
            concat_axis=0,
            tiled=True,
        ),
        lax.all_to_all(
            local_max.reshape(1, SEQS, heads_all, SPAN),
            "tp",
            split_axis=2,
            concat_axis=0,
            tiled=True,
        ),
        lax.all_to_all(
            local_total.reshape(1, SEQS, heads_all, SPAN),
            "tp",
            split_axis=2,
            concat_axis=0,
            tiled=True,
        ),
    )
    running_max = jnp.maximum(maxes_in.max(0), fresh_max)
    factors = jnp.exp(maxes_in - running_max[None])
    fresh_weights = jnp.where(causal, jnp.exp(fresh_scores - running_max[..., None]), 0.0)
    totals = (factors * totals_in).sum(0) + fresh_weights.sum(-1)
    summed = (factors[..., None] * sums_in).sum(0)
    summed = summed + jnp.einsum(
        "shck,skhd->shcd",
        fresh_weights.astype(jnp.bfloat16),
        own_values,
        preferred_element_type=jnp.float32,
    )
    attn = (summed / totals[..., None]).astype(jnp.bfloat16)
    attn = jnp.transpose(attn, (0, 2, 1, 3)).reshape(token_count, HQ_DEV * HD)
    share_part = lax.psum_scatter(
        lax.dot_general(
            o_weight, attn, (((0,), (1,)), ((), ())), preferred_element_type=jnp.float32
        ),
        "tp",
        scatter_dimension=0,
        tiled=True,
    )
    hidden = (residual.astype(jnp.float32) + share_part.T).astype(jnp.bfloat16)
    stream = lax.all_gather(hidden, "tp", axis=1, tiled=True)
    return rms_rows(stream, ffn_gain).astype(jnp.bfloat16)


def solution(mesh):
    return jax.shard_map(
        per_device_ring if mesh.shape["tp"] == 2 * CHIPS else per_device,
        mesh=mesh,
        in_specs=(
            P("replica", "tp"),
            P(),
            P(),
            P(None, "tp"),
            P(None, "tp"),
            P("tp", None),
            P("replica", "tp", None),
            P("replica", "tp", None),
            P("replica"),
        ),
        out_specs=P("replica", None),
        check_vma=False,
    )
```

```python
import functools

import jax
import jax.numpy as jnp
from jax import lax
from jax.experimental import pallas as pl
from jax.experimental.pallas import tpu as pltpu
from jax.sharding import PartitionSpec as P

HD = 128
KVH = 8
HQ_DEV = 1
SPAN = 64
SEQS = 2
CTX_DEV = 64
TOKENS = SEQS * SPAN
MIB = 1024 * 1024

epsilon = 1e-05


def rms_rows(rows, gain):
    values_f = rows.astype(jnp.float32)
    factor = lax.rsqrt(jnp.mean(values_f * values_f, axis=-1, keepdims=True) + epsilon)
    return values_f * factor * gain.astype(jnp.float32)


def rope_tables(positions):
    half_width = HD // 2
    frequency = 500000.0 ** (-jnp.arange(half_width, dtype=jnp.float32) / half_width)
    angles = positions.astype(jnp.float32)[:, None] * frequency[None, :]
    return jnp.cos(angles), jnp.sin(angles)


def rotate(vectors, positions):
    half_width = vectors.shape[-1] // 2
    cosine, sine = rope_tables(positions)
    cosine, sine = cosine[:, None, :], sine[:, None, :]
    first_half = vectors[..., :half_width]
    second_half = vectors[..., half_width:]
    return jnp.concatenate(
        [first_half * cosine - second_half * sine, second_half * cosine + first_half * sine],
        axis=-1,
    )


CHIPS = 8
RING = (0, 2, 4, 6, 7, 5, 3, 1)
ONWARD = [(2 * RING[i], 2 * RING[(i + 1) % CHIPS]) for i in range(CHIPS)] + [
    (2 * RING[i] + 1, 2 * RING[i - 1] + 1) for i in range(CHIPS)
]
ENTER = [(2 * RING[i], 2 * RING[i - 1] + 1) for i in range(CHIPS)] + [
    (2 * RING[i] + 1, 2 * RING[(i + 1) % CHIPS]) for i in range(CHIPS)
]
LEAVE = [(2 * RING[i], 2 * RING[(i + 1) % CHIPS] + 1) for i in range(CHIPS)] + [
    (2 * RING[i] + 1, 2 * RING[i - 1]) for i in range(CHIPS)
]
SWAP = [(t, t ^ 1) for t in range(2 * CHIPS)]
FRESH = [(k, 2 * k) for k in range(KVH)] + [(KVH + k, 2 * k + 1) for k in range(KVH)]
VMEM = pl.BlockSpec(memory_space=pltpu.VMEM)
SMEM = pl.BlockSpec(memory_space=pltpu.SMEM)
HBM = pl.BlockSpec(memory_space=pltpu.HBM)


def ring_place(rank):
    chip = rank // 2
    return jnp.where(chip % 2 == 0, chip // 2, CHIPS - 1 - chip // 2)


def chip_at(place):
    place = place % CHIPS
    return jnp.where(place < CHIPS // 2, 2 * place, 2 * CHIPS - 1 - 2 * place)


def send(array, pairs):
    return lax.ppermute(array, "tp", pairs)


def xor(bits):
    return [(t, t ^ bits) for t in range(2 * CHIPS)]


def after(array, *others):
    return lax.optimization_barrier((array, others))[0]


def ring_gather(own, ready=None, direct=False):
    straight, swapped = own, send(own, SWAP)
    crossed = own if direct else swapped
    mine, theirs = [own], [swapped]
    for step in range(1, 5):
        if step == 4 and ready is not None:
            straight = after(straight, ready)
        straight = send(straight, ONWARD)
        mine.append(straight)
        theirs.append(send(straight, SWAP))
        if step < 4:
            crossed = send(crossed, ENTER if direct and step == 1 else ONWARD)
            mine.append(crossed)
            theirs.append(send(crossed, SWAP))
    return mine, theirs


def gathered_ids(rank):
    place = ring_place(rank)
    ids = []
    for side in range(2):
        device = rank ^ side
        core = device % 2
        ids.append(device)
        for step in range(1, 5):
            chip = 2 * chip_at(place + (2 * core - 1) * step)
            ids += [chip + core, chip + 1 - core] if step < 4 else [chip + core]
    return jnp.stack(ids).astype(jnp.int32)


SHARES = ((4, 0), (3, 1), (3, 0), (2, 1), (2, 0), (1, 1), (1, 0), (0, 0))


def share_ids(rank):
    place, core = ring_place(rank), rank % 2
    return jnp.stack(
        [2 * chip_at(place + (1 - 2 * core) * d) + (core + other) % 2 for d, other in SHARES]
    ).astype(jnp.int32)


def ring_sum(shares):
    streams, crossed = shares[4, 0], shares[3, 1][0]
    for step in range(1, 5):
        streams = [send(part, ONWARD) for part in streams]
        if step < 4:
            crossed = send(crossed, LEAVE if step == 3 else ONWARD)
        if step < 4:
            streams = [add_share(part, share) for part, share in zip(streams, shares[4 - step, 0])]
        if step < 3:
            crossed = add_share(crossed, shares[3 - step, 1][0])
    return streams, crossed


def add_share(part, share):
    return (part.astype(jnp.float32) + share).astype(jnp.bfloat16)


def split_cache(key_cache, value_cache, rank, rank_id):
    core = rank % 2
    give = jnp.stack(
        [lax.dynamic_index_in_dim(c, 1 - core, 0, keepdims=False) for c in (key_cache, value_cache)]
    )
    theirs = send(give, SWAP)
    return pack(rank_id, key_cache, value_cache, theirs)


def move_cache(parts):
    keep, give = parts
    came = send(give, xor(2))
    pieces = stack_pieces(keep, came)
    return [keep, came] + [send(piece, xor(4 * m)) for m, piece in zip(range(1, 4), pieces)], pieces


def stack_kernel(keep, came, *outs):
    for m, out in enumerate(outs, 1):
        out[0] = keep[m]
        out[1] = came[m]


def stack_pieces(keep, came):
    return pl.pallas_call(
        stack_kernel,
        out_shape=[jax.ShapeDtypeStruct((2,) + keep.shape[1:], keep.dtype)] * 3,
        in_specs=[VMEM] * 2,
        out_specs=[VMEM] * 3,
        compiler_params=pltpu.CompilerParams(vmem_limit_bytes=8 * MIB),
        cost_estimate=pl.CostEstimate(flops=0, bytes_accessed=MIB, transcendentals=0),
        name="stack_cache",
    )(keep, came)


def pack_kernel(rank, keys, values, theirs, keep, give, sems):
    me = rank[0]
    copies = []
    for m in range(4):
        for j, out in enumerate((keep, give)):
            chip = (me ^ (4 * m + 2 * j)) // 2
            head = pl.ds(pl.multiple_of(chip * HD, HD), HD)
            for k, cache in enumerate((keys, values)):
                copies.append(
                    pltpu.make_async_copy(
                        cache.at[me % 2, :, head], out.at[m, 0, k], sems.at[m, j, k]
                    )
                )
                copies[-1].start()
            out[m, 1, 0] = theirs[0, :, head]
            out[m, 1, 1] = theirs[1, :, head]
    for copy in copies:
        copy.wait()


def pack(rank_id, key_cache, value_cache, theirs):
    return pl.pallas_call(
        pack_kernel,
        out_shape=[jax.ShapeDtypeStruct((4, 2, 2, CTX_DEV, HD), jnp.bfloat16)] * 2,
        in_specs=[SMEM] + [HBM] * 2 + [VMEM],
        out_specs=[VMEM] * 2,
        scratch_shapes=[pltpu.SemaphoreType.DMA((4, 2, 2))],
        compiler_params=pltpu.CompilerParams(vmem_limit_bytes=8 * MIB),
        cost_estimate=pl.CostEstimate(flops=0, bytes_accessed=MIB, transcendentals=0),
        name="pack_cache",
    )(rank_id, in_hbm(key_cache), in_hbm(value_cache), theirs)


def lanes(block, j):
    return block[:, 128 * j : 128 * j + 128].astype(jnp.float32)


def square_sums(blocks, total):
    for block in blocks:
        for j in range(block.shape[1] // 128):
            v = lanes(block, j)
            total = total + v * v
    return total


def row_factors(squares, features):
    mean = jnp.sum(squares, axis=1, keepdims=True) * (1.0 / features)
    return lax.rsqrt(mean + epsilon)


def normed_block(block, factors, gain_row):
    return jnp.concatenate(
        [
            (lanes(block, j) * factors * gain_row[:, 128 * j : 128 * j + 128]).astype(jnp.bfloat16)
            for j in range(block.shape[1] // 128)
        ],
        axis=1,
    )


def in_hbm(array):
    return pltpu.with_memory_space_constraint(array, pltpu.HBM)


def load_kernel(axis, blocks, first, second, out, sems):
    count, width = out.shape[0], out.shape[1 + axis]
    copies = []
    for i in range(count):
        block = pl.ds(pl.multiple_of(blocks[i] * width, width), width)
        for j, weight in enumerate((first, second)):
            half = pl.ds(j * HD, HD)
            copies.append(
                pltpu.make_async_copy(
                    weight.at[:, block] if axis else weight.at[block, :],
                    out.at[i, half, :] if axis else out.at[i, :, half],
                    sems.at[j, i],
                )
            )
            copies[-1].start()
    for copy in copies:
        copy.wait()


def load_weights(blocks, first, second, width, axis):
    count = blocks.shape[0]
    shape = (count, 2 * HD, width) if axis else (count, width, 2 * HD)
    return pl.pallas_call(
        functools.partial(load_kernel, axis),
        out_shape=jax.ShapeDtypeStruct(shape, jnp.bfloat16),
        in_specs=[SMEM] + [HBM] * 2,
        out_specs=VMEM,
        scratch_shapes=[pltpu.SemaphoreType.DMA((2, count))],
        compiler_params=pltpu.CompilerParams(vmem_limit_bytes=16 * MIB),
        cost_estimate=pl.CostEstimate(
            flops=0, bytes_accessed=8 * count * HD * width, transcendentals=0
        ),
        name="load_weights_%d" % axis,
    )(blocks, first, second)


def all_factors(blocks):
    total = square_sums(blocks, jnp.zeros((TOKENS, 128), jnp.float32))
    return row_factors(total, 16 * blocks[0].shape[1])


def project_kernel(ids, *refs):
    blocks, refs = refs[:16], refs[16:]
    gain, weights, cosine, sine, kv_cos, kv_sin = refs[:6]
    q_keep, q_send, fresh = refs[6:]
    factors = all_factors(blocks)
    total = jnp.zeros((TOKENS, 2 * HD), jnp.float32)
    for i in range(16):
        normed = normed_block(blocks[i], factors, gain[ids[i]])
        total = total + jnp.dot(normed, weights[i], preferred_element_type=jnp.float32)
    q, kv = total[:, :HD], total[:, HD:]
    q = (q * cosine[...] + pltpu.roll(q, HD // 2, 1) * sine[...]).astype(jnp.bfloat16)
    kv = (kv * kv_cos[...] + pltpu.roll(kv, HD // 2, 1) * kv_sin[...]).astype(jnp.bfloat16)
    core_one = ids[0] % 2 == 1
    q_keep[...] = jnp.where(core_one, q[SPAN:], q[:SPAN])
    q_send[...] = jnp.where(core_one, q[:SPAN], q[SPAN:])
    fresh[...] = kv


def project(ids, arrays, gain, weights, tables):
    return pl.pallas_call(
        project_kernel,
        out_shape=[jax.ShapeDtypeStruct((SPAN, HD), jnp.bfloat16)] * 2
        + [jax.ShapeDtypeStruct((TOKENS, HD), jnp.bfloat16)],
        in_specs=[SMEM] + [VMEM] * (len(arrays) + 6),
        out_specs=[VMEM] * 3,
        compiler_params=pltpu.CompilerParams(vmem_limit_bytes=24 * MIB),
        cost_estimate=pl.CostEstimate(
            flops=2 * TOKENS * weights.size, bytes_accessed=12 * MIB, transcendentals=0
        ),
        name="norm_project",
    )(ids, *arrays, gain, weights, *tables)


def cache_rows(cache, which):
    keep, came, rest = cache[0], cache[1], cache[2:]
    groups = [part[0, c, which] for part in (keep, came) for c in range(2)]
    groups += [part[x, c, which] for part in rest for x in range(2) for c in range(2)]
    return jnp.concatenate(groups, axis=0)


CONTRACT = (((1,), (1,)), ((), ()))


def scores_kernel(info, q, q_other, *refs):
    cache, scores = refs[:5], refs[5]
    core, rank = info[SEQS], info[SEQS + 1]
    queries = jnp.concatenate([q[...], q_other[...]], axis=0)
    old = lax.dot_general(
        queries, cache_rows(cache, 0), CONTRACT, preferred_element_type=jnp.float32
    )
    lane = lax.broadcasted_iota(jnp.int32, old.shape, 1)
    position = (rank ^ (lane // CTX_DEV)) * CTX_DEV + lane % CTX_DEV
    scores[...] = jnp.where(position < info[core], old * HD ** (-0.5), -1e30)


def cache_scores(info, q, q_other, cache):
    return pl.pallas_call(
        scores_kernel,
        out_shape=jax.ShapeDtypeStruct((TOKENS, 16 * CTX_DEV), jnp.float32),
        in_specs=[SMEM] + [VMEM] * 7,
        out_specs=VMEM,
        compiler_params=pltpu.CompilerParams(vmem_limit_bytes=16 * MIB),
        cost_estimate=pl.CostEstimate(flops=32 * MIB, bytes_accessed=MIB, transcendentals=0),
        name="cache_scores",
    )(info, q, q_other, *cache)


def attend_kernel(info, q, q_other, fresh_own, fresh_other, scores, *refs):
    cache, out = refs[:5], refs[5]
    core = info[SEQS]
    came = fresh_other[...]
    fresh_keys = jnp.where(core == 0, fresh_own[:SPAN, :], came)
    fresh_values = jnp.where(core == 0, came, fresh_own[SPAN:, :])
    queries = jnp.concatenate([q[...], q_other[...]], axis=0)
    old = scores[...]
    valid = old > -1e29
    fresh = lax.dot_general(
        queries, fresh_keys, CONTRACT, preferred_element_type=jnp.float32
    ) * HD ** (-0.5)
    place = lax.broadcasted_iota(jnp.int32, fresh.shape, 0) % SPAN
    causal = place >= lax.broadcasted_iota(jnp.int32, fresh.shape, 1)
    fresh = jnp.where(causal, fresh, -1e30)
    most = jnp.maximum(jnp.max(old, axis=1, keepdims=True), jnp.max(fresh, axis=1, keepdims=True))
    old_weights = jnp.where(valid, jnp.exp(old - most), 0.0)
    fresh_weights = jnp.where(causal, jnp.exp(fresh - most), 0.0)
    totals = jnp.sum(old_weights, axis=1, keepdims=True) + jnp.sum(
        fresh_weights, axis=1, keepdims=True
    )
    summed = jnp.dot(
        old_weights.astype(jnp.bfloat16), cache_rows(cache, 1), preferred_element_type=jnp.float32
    ) + jnp.dot(
        fresh_weights.astype(jnp.bfloat16), fresh_values, preferred_element_type=jnp.float32
    )
    attn = (summed / totals).astype(jnp.bfloat16)
    out[:, :HD] = attn[:SPAN]
    out[:, HD:] = attn[SPAN:]


def attend(info, q, q_other, fresh_own, fresh_other, scores, cache):
    return pl.pallas_call(
        attend_kernel,
        out_shape=jax.ShapeDtypeStruct((SPAN, 2 * HD), jnp.bfloat16),
        in_specs=[SMEM] + [VMEM] * 10,
        out_specs=VMEM,
        compiler_params=pltpu.CompilerParams(vmem_limit_bytes=16 * MIB),
        cost_estimate=pl.CostEstimate(
            flops=48 * MIB, bytes_accessed=2 * MIB, transcendentals=TOKENS * 1088
        ),
        name="attend",
    )(info, q, q_other, fresh_own, fresh_other, scores, *cache)


def both_heads(core, attn, attn_other):
    mine = attn[...]
    theirs = jnp.concatenate([attn_other[:, HD:], attn_other[:, :HD]], axis=1)
    core_one = core[0] == 1
    return jnp.concatenate(
        [jnp.where(core_one, theirs, mine), jnp.where(core_one, mine, theirs)], axis=0
    )


def share_shapes(shares, width, dtype):
    half, whole = [((SPAN, width), dtype)] * 2, [((TOKENS, width), dtype)]
    return [jax.ShapeDtypeStruct(*s) for _, other in shares for s in (whole if other else half)]


def share_lists(shares, arrays):
    arrays = list(arrays)
    return {key: [arrays.pop(0) for _ in range(2 - key[1])] for key in shares}


def write_share(value, outs):
    rows = TOKENS // len(outs)
    for i, out in enumerate(outs):
        out[...] = value[i * rows : (i + 1) * rows].astype(out.dtype)


def shares_kernel(first, last, core, attn, attn_other, weights, *outs):
    rows = both_heads(core, attn, attn_other)
    for i, refs in enumerate(share_lists(SHARES[first:last], outs).values()):
        write_share(jnp.dot(rows, weights[first + i], preferred_element_type=jnp.float32), refs)


def shares_of(core, attn, attn_other, weights, first, last, dtype=jnp.float32):
    width = weights.shape[2]
    out_shape = share_shapes(SHARES[first:last], width, dtype)
    arrays = pl.pallas_call(
        functools.partial(shares_kernel, first, last),
        out_shape=out_shape,
        in_specs=[SMEM] + [VMEM] * 3,
        out_specs=[VMEM] * len(out_shape),
        compiler_params=pltpu.CompilerParams(vmem_limit_bytes=16 * MIB),
        cost_estimate=pl.CostEstimate(
            flops=4 * TOKENS * HD * width * (last - first),
            bytes_accessed=(last - first) * MIB,
            transcendentals=0,
        ),
        name="shares_%d" % first,
    )(core, attn, attn_other, weights)
    return share_lists(SHARES[first:last], arrays)


def final_kernel(ids, *refs):
    blocks, refs = refs[:16], refs[16:]
    gain, out, staged, sems = refs
    width = staged.shape[2]
    factors = all_factors(blocks)
    copies = []
    for i in range(16):
        staged[i] = normed_block(blocks[i], factors, gain[ids[i]])
        copy = pltpu.make_async_copy(
            staged.at[i],
            out.at[:, pl.ds(pl.multiple_of(ids[i] * width, width), width)],
            sems.at[i],
        )
        copy.start()
        copies.append(copy)
    for copy in copies:
        copy.wait()


def final_norm(ids, arrays, gain):
    width = arrays[0].shape[1]
    return pl.pallas_call(
        final_kernel,
        out_shape=jax.ShapeDtypeStruct((TOKENS, 16 * width), jnp.bfloat16),
        in_specs=[SMEM] + [VMEM] * (len(arrays) + 1),
        out_specs=HBM,
        scratch_shapes=[
            pltpu.VMEM((16, TOKENS, width), jnp.bfloat16),
            pltpu.SemaphoreType.DMA((16,)),
        ],
        compiler_params=pltpu.CompilerParams(vmem_limit_bytes=24 * MIB),
        cost_estimate=pl.CostEstimate(
            flops=16 * MIB, bytes_accessed=12 * MIB, transcendentals=0
        ),
        name="final_norm",
    )(ids, *arrays, gain)


def per_device_ring(
    residual, attn_gain, ffn_gain, q_weight, kv_weight, o_weight, key_cache, value_cache, prefix
):
    rank = lax.axis_index("tp")
    core = rank % 2
    width = residual.shape[1]
    ids = gathered_ids(rank)
    to = share_ids(rank)
    core_id, rank_id = core[None].astype(jnp.int32), rank[None].astype(jnp.int32)
    info = jnp.concatenate([prefix, core_id, rank_id])

    weight_other = send(o_weight, SWAP)
    parts = split_cache(key_cache, value_cache, rank, rank_id)
    cache, pieces = move_cache(parts)
    mine, theirs = ring_gather(residual, weight_other, direct=True)
    weights = load_weights(ids, in_hbm(q_weight), in_hbm(kv_weight), width, 0)

    positions = (prefix[:, None] + jnp.arange(SPAN, dtype=jnp.int32)[None, :]).reshape(-1)
    cosine, sine = rope_tables(positions)
    cosine = jnp.concatenate([cosine, cosine], axis=1)
    sine = jnp.concatenate([-sine, sine], axis=1)
    holds_keys = rank < KVH
    tables = (cosine, sine, jnp.where(holds_keys, cosine, 1.0), jnp.where(holds_keys, sine, 0.0))

    gain = attn_gain.reshape(16, 1, width).astype(jnp.float32)
    mine[0] = after(mine[0], pieces)
    q_keep, q_send, fresh = project(ids, mine + theirs, gain, weights, tables)
    o_weights = load_weights(after(to, fresh), in_hbm(o_weight), weight_other, width, 1)
    q_other = send(q_send, SWAP)
    fresh_own = send(fresh, FRESH)
    fresh_other = send(jnp.where(core == 0, fresh_own[SPAN:], fresh_own[:SPAN]), SWAP)
    scores = cache_scores(info, after(q_keep, o_weights), q_other, cache)
    attn = attend(info, q_keep, q_other, fresh_own, fresh_other, scores, cache)
    attn_other = send(attn, SWAP)

    inputs = (core_id, attn, attn_other, o_weights)
    shares = shares_of(*inputs, 0, 2, jnp.bfloat16)
    shares.update(shares_of(*inputs, 2, len(SHARES)))
    one_way, other_way = ring_sum(shares)
    hidden = []
    for h, rows in enumerate((slice(0, SPAN), slice(SPAN, TOKENS))):
        projected = shares[0, 0][h] + one_way[h].astype(jnp.float32)
        projected = projected + other_way[rows].astype(jnp.float32)
        hidden.append((residual[rows].astype(jnp.float32) + projected).astype(jnp.bfloat16))

    hidden = jnp.concatenate(hidden, axis=0)
    mine, theirs = ring_gather(hidden)
    gain = ffn_gain.reshape(16, 1, width).astype(jnp.float32)
    return final_norm(ids, mine + theirs, gain)


def per_device(
    residual, attn_gain, ffn_gain, q_weight, kv_weight, o_weight, key_cache, value_cache, prefix
):
    tp_count = lax.axis_size("tp")
    tp_rank = lax.axis_index("tp")
    heads_all = HQ_DEV * tp_count
    group_size = heads_all // KVH
    token_count = SEQS * SPAN
    score_scale = HD ** (-0.5)
    whole_rows = lax.all_gather(residual, "tp", axis=1, tiled=True)
    normed = rms_rows(whole_rows, attn_gain).astype(jnp.bfloat16)
    positions = (prefix[:, None] + jnp.arange(SPAN, dtype=jnp.int32)[None, :]).reshape(-1)
    queries = jnp.dot(normed, q_weight, preferred_element_type=jnp.float32).reshape(
        token_count, HQ_DEV, HD
    )
    queries = rotate(queries, positions).astype(jnp.bfloat16)
    kv_part = jnp.dot(normed, kv_weight, preferred_element_type=jnp.float32)
    kv_whole = lax.all_gather(kv_part, "tp", axis=1, tiled=True)
    new_keys = rotate(kv_whole[:, : KVH * HD].reshape(token_count, KVH, HD), positions).astype(
        jnp.bfloat16
    )
    new_values = kv_whole[:, KVH * HD :].reshape(token_count, KVH, HD).astype(jnp.bfloat16)
    head_ids = tp_rank * HQ_DEV + jnp.arange(HQ_DEV, dtype=jnp.int32)
    own_kv = head_ids // group_size
    own_keys = jnp.take(new_keys, own_kv, axis=1).reshape(SEQS, SPAN, HQ_DEV, HD)
    own_values = jnp.take(new_values, own_kv, axis=1).reshape(SEQS, SPAN, HQ_DEV, HD)
    own_queries = queries.reshape(SEQS, SPAN, HQ_DEV, HD)
    causal = (jnp.arange(SPAN)[:, None] >= jnp.arange(SPAN)[None, :])[None, None]
    fresh_scores = (
        jnp.einsum("schd,skhd->shck", own_queries, own_keys, preferred_element_type=jnp.float32)
        * score_scale
    )
    fresh_scores = jnp.where(causal, fresh_scores, -1e30)
    fresh_max = fresh_scores.max(-1)
    gathered = lax.all_gather(queries.reshape(token_count, HQ_DEV * HD), "tp", axis=1, tiled=True)
    queries_all = gathered.reshape(SEQS, SPAN, KVH, group_size, HD)
    keys_local = key_cache.reshape(SEQS, CTX_DEV, KVH, HD)
    values_local = value_cache.reshape(SEQS, CTX_DEV, KVH, HD)
    local_scores = (
        jnp.einsum("sckgd,sjkd->skgcj", queries_all, keys_local, preferred_element_type=jnp.float32)
        * score_scale
    )
    first_slot = tp_rank * CTX_DEV
    is_valid = ((first_slot + jnp.arange(CTX_DEV, dtype=jnp.int32))[None, :] < prefix[:, None])[
        :, None, None, None, :
    ]
    local_scores = jnp.where(is_valid, local_scores, -1e30)
    local_max = local_scores.max(-1)
    local_weights = jnp.where(is_valid, jnp.exp(local_scores - local_max[..., None]), 0.0)
    local_total = local_weights.sum(-1)
    local_sum = jnp.einsum(
        "skgcj,sjkd->skgcd",
        local_weights.astype(jnp.bfloat16),
        values_local,
        preferred_element_type=jnp.float32,
    )
    sums_in, maxes_in, totals_in = (
        lax.all_to_all(
            local_sum.reshape(1, SEQS, heads_all, SPAN, HD),
            "tp",
            split_axis=2,
            concat_axis=0,
            tiled=True,
        ),
        lax.all_to_all(
            local_max.reshape(1, SEQS, heads_all, SPAN),
            "tp",
            split_axis=2,
            concat_axis=0,
            tiled=True,
        ),
        lax.all_to_all(
            local_total.reshape(1, SEQS, heads_all, SPAN),
            "tp",
            split_axis=2,
            concat_axis=0,
            tiled=True,
        ),
    )
    running_max = jnp.maximum(maxes_in.max(0), fresh_max)
    factors = jnp.exp(maxes_in - running_max[None])
    fresh_weights = jnp.where(causal, jnp.exp(fresh_scores - running_max[..., None]), 0.0)
    totals = (factors * totals_in).sum(0) + fresh_weights.sum(-1)
    summed = (factors[..., None] * sums_in).sum(0)
    summed = summed + jnp.einsum(
        "shck,skhd->shcd",
        fresh_weights.astype(jnp.bfloat16),
        own_values,
        preferred_element_type=jnp.float32,
    )
    attn = (summed / totals[..., None]).astype(jnp.bfloat16)
    attn = jnp.transpose(attn, (0, 2, 1, 3)).reshape(token_count, HQ_DEV * HD)
    share_part = lax.psum_scatter(
        lax.dot_general(
            o_weight, attn, (((0,), (1,)), ((), ())), preferred_element_type=jnp.float32
        ),
        "tp",
        scatter_dimension=0,
        tiled=True,
    )
    hidden = (residual.astype(jnp.float32) + share_part.T).astype(jnp.bfloat16)
    stream = lax.all_gather(hidden, "tp", axis=1, tiled=True)
    return rms_rows(stream, ffn_gain).astype(jnp.bfloat16)


def solution(mesh):
    return jax.shard_map(
        per_device_ring if mesh.shape["tp"] == 2 * CHIPS else per_device,
        mesh=mesh,
        in_specs=(
            P("replica", "tp"),
            P(),
            P(),
            P(None, "tp"),
            P(None, "tp"),
            P("tp", None),
            P("replica", "tp", None),
            P("replica", "tp", None),
            P("replica"),
        ),
        out_specs=P("replica", None),
        check_vma=False,
    )
```

```python
import functools

import jax
import jax.numpy as jnp
from jax import lax
from jax.experimental import pallas as pl
from jax.experimental.pallas import tpu as pltpu
from jax.sharding import PartitionSpec as P

HD = 128
KVH = 8
HQ_DEV = 1
SPAN = 64
SEQS = 2
CTX_DEV = 64
TOKENS = SEQS * SPAN
MIB = 1024 * 1024

epsilon = 1e-05


def rms_rows(rows, gain):
    values_f = rows.astype(jnp.float32)
    factor = lax.rsqrt(jnp.mean(values_f * values_f, axis=-1, keepdims=True) + epsilon)
    return values_f * factor * gain.astype(jnp.float32)


def rope_tables(positions):
    half_width = HD // 2
    frequency = 500000.0 ** (-jnp.arange(half_width, dtype=jnp.float32) / half_width)
    angles = positions.astype(jnp.float32)[:, None] * frequency[None, :]
    return jnp.cos(angles), jnp.sin(angles)


def rotate(vectors, positions):
    half_width = vectors.shape[-1] // 2
    cosine, sine = rope_tables(positions)
    cosine, sine = cosine[:, None, :], sine[:, None, :]
    first_half = vectors[..., :half_width]
    second_half = vectors[..., half_width:]
    return jnp.concatenate(
        [first_half * cosine - second_half * sine, second_half * cosine + first_half * sine],
        axis=-1,
    )


CHIPS = 8
RING = (0, 2, 4, 6, 7, 5, 3, 1)
ONWARD = [(2 * RING[i], 2 * RING[(i + 1) % CHIPS]) for i in range(CHIPS)] + [
    (2 * RING[i] + 1, 2 * RING[i - 1] + 1) for i in range(CHIPS)
]
ENTER = [(2 * RING[i], 2 * RING[i - 1] + 1) for i in range(CHIPS)] + [
    (2 * RING[i] + 1, 2 * RING[(i + 1) % CHIPS]) for i in range(CHIPS)
]
LEAVE = [(2 * RING[i], 2 * RING[(i + 1) % CHIPS] + 1) for i in range(CHIPS)] + [
    (2 * RING[i] + 1, 2 * RING[i - 1]) for i in range(CHIPS)
]
SWAP = [(t, t ^ 1) for t in range(2 * CHIPS)]
FRESH = [(k, 2 * k) for k in range(KVH)] + [(KVH + k, 2 * k + 1) for k in range(KVH)]
VMEM = pl.BlockSpec(memory_space=pltpu.VMEM)
SMEM = pl.BlockSpec(memory_space=pltpu.SMEM)
HBM = pl.BlockSpec(memory_space=pltpu.HBM)


def ring_place(rank):
    chip = rank // 2
    return jnp.where(chip % 2 == 0, chip // 2, CHIPS - 1 - chip // 2)


def chip_at(place):
    place = place % CHIPS
    return jnp.where(place < CHIPS // 2, 2 * place, 2 * CHIPS - 1 - 2 * place)


def send(array, pairs):
    return lax.ppermute(array, "tp", pairs)


def xor(bits):
    return [(t, t ^ bits) for t in range(2 * CHIPS)]


def after(array, *others):
    return lax.optimization_barrier((array, others))[0]


def ring_gather(own, ready=None, direct=False):
    straight, swapped = own, send(own, SWAP)
    crossed = own if direct else swapped
    mine, theirs = [own], [swapped]
    for step in range(1, 5):
        if step == 4 and ready is not None:
            straight = after(straight, ready)
        straight = send(straight, ONWARD)
        mine.append(straight)
        theirs.append(send(straight, SWAP))
        if step < 4:
            crossed = send(crossed, ENTER if direct and step == 1 else ONWARD)
            mine.append(crossed)
            theirs.append(send(crossed, SWAP))
    return mine, theirs


def gathered_ids(rank):
    place = ring_place(rank)
    ids = []
    for side in range(2):
        device = rank ^ side
        core = device % 2
        ids.append(device)
        for step in range(1, 5):
            chip = 2 * chip_at(place + (2 * core - 1) * step)
            ids += [chip + core, chip + 1 - core] if step < 4 else [chip + core]
    return jnp.stack(ids).astype(jnp.int32)


SHARES = ((4, 0), (3, 1), (3, 0), (2, 1), (2, 0), (1, 1), (1, 0), (0, 0))


def share_ids(rank):
    place, core = ring_place(rank), rank % 2
    return jnp.stack(
        [2 * chip_at(place + (1 - 2 * core) * d) + (core + other) % 2 for d, other in SHARES]
    ).astype(jnp.int32)


def ring_sum(shares):
    straight, crossed = shares[4, 0], shares[3, 1]
    for step in range(1, 5):
        straight = send(straight, ONWARD)
        if step < 4:
            crossed = send(crossed, LEAVE if step == 3 else ONWARD)
            straight = add_share(straight, shares[4 - step, 0])
        if step < 3:
            crossed = add_share(crossed, shares[3 - step, 1])
    return straight, crossed


def add_share(part, share):
    return (part.astype(jnp.float32) + share).astype(jnp.bfloat16)


def split_cache(key_cache, value_cache, rank, rank_id):
    core = rank % 2
    give = jnp.stack(
        [lax.dynamic_index_in_dim(c, 1 - core, 0, keepdims=False) for c in (key_cache, value_cache)]
    )
    theirs = send(give, SWAP)
    return pack(rank_id, key_cache, value_cache, theirs)


def move_cache(parts):
    keep, give = parts
    came = send(give, xor(2))
    pieces = stack_pieces(keep, came)
    return [keep, came] + [send(piece, xor(4 * m)) for m, piece in zip(range(1, 4), pieces)], pieces


def stack_kernel(keep, came, *outs):
    for m, out in enumerate(outs, 1):
        out[0] = keep[m]
        out[1] = came[m]


def stack_pieces(keep, came):
    return pl.pallas_call(
        stack_kernel,
        out_shape=[jax.ShapeDtypeStruct((2,) + keep.shape[1:], keep.dtype)] * 3,
        in_specs=[VMEM] * 2,
        out_specs=[VMEM] * 3,
        compiler_params=pltpu.CompilerParams(vmem_limit_bytes=8 * MIB),
        cost_estimate=pl.CostEstimate(flops=0, bytes_accessed=MIB, transcendentals=0),
        name="stack_cache",
    )(keep, came)


def pack_kernel(rank, keys, values, theirs, keep, give, sems):
    me = rank[0]
    copies = []
    for m in range(4):
        for j, out in enumerate((keep, give)):
            chip = (me ^ (4 * m + 2 * j)) // 2
            head = pl.ds(pl.multiple_of(chip * HD, HD), HD)
            for k, cache in enumerate((keys, values)):
                copies.append(
                    pltpu.make_async_copy(
                        cache.at[me % 2, :, head], out.at[m, 0, k], sems.at[m, j, k]
                    )
                )
                copies[-1].start()
            out[m, 1, 0] = theirs[0, :, head]
            out[m, 1, 1] = theirs[1, :, head]
    for copy in copies:
        copy.wait()


def pack(rank_id, key_cache, value_cache, theirs):
    return pl.pallas_call(
        pack_kernel,
        out_shape=[jax.ShapeDtypeStruct((4, 2, 2, CTX_DEV, HD), jnp.bfloat16)] * 2,
        in_specs=[SMEM] + [HBM] * 2 + [VMEM],
        out_specs=[VMEM] * 2,
        scratch_shapes=[pltpu.SemaphoreType.DMA((4, 2, 2))],
        compiler_params=pltpu.CompilerParams(vmem_limit_bytes=8 * MIB),
        cost_estimate=pl.CostEstimate(flops=0, bytes_accessed=MIB, transcendentals=0),
        name="pack_cache",
    )(rank_id, in_hbm(key_cache), in_hbm(value_cache), theirs)


def lanes(block, j):
    return block[:, 128 * j : 128 * j + 128].astype(jnp.float32)


def square_sums(blocks, total):
    for block in blocks:
        for j in range(block.shape[1] // 128):
            v = lanes(block, j)
            total = total + v * v
    return total


def row_factors(squares, features):
    mean = jnp.sum(squares, axis=1, keepdims=True) * (1.0 / features)
    return lax.rsqrt(mean + epsilon)


def normed_block(block, factors, gain_row):
    return jnp.concatenate(
        [
            (lanes(block, j) * factors * gain_row[:, 128 * j : 128 * j + 128]).astype(jnp.bfloat16)
            for j in range(block.shape[1] // 128)
        ],
        axis=1,
    )


def in_hbm(array):
    return pltpu.with_memory_space_constraint(array, pltpu.HBM)


def load_kernel(axis, blocks, first, second, out, sems):
    count, width = out.shape[0], out.shape[1 + axis]
    copies = []
    for i in range(count):
        block = pl.ds(pl.multiple_of(blocks[i] * width, width), width)
        for j, weight in enumerate((first, second)):
            half = pl.ds(j * HD, HD)
            copies.append(
                pltpu.make_async_copy(
                    weight.at[:, block] if axis else weight.at[block, :],
                    out.at[i, half, :] if axis else out.at[i, :, half],
                    sems.at[j, i],
                )
            )
            copies[-1].start()
    for copy in copies:
        copy.wait()


def load_weights(blocks, first, second, width, axis):
    count = blocks.shape[0]
    shape = (count, 2 * HD, width) if axis else (count, width, 2 * HD)
    return pl.pallas_call(
        functools.partial(load_kernel, axis),
        out_shape=jax.ShapeDtypeStruct(shape, jnp.bfloat16),
        in_specs=[SMEM] + [HBM] * 2,
        out_specs=VMEM,
        scratch_shapes=[pltpu.SemaphoreType.DMA((2, count))],
        compiler_params=pltpu.CompilerParams(vmem_limit_bytes=16 * MIB),
        cost_estimate=pl.CostEstimate(
            flops=0, bytes_accessed=8 * count * HD * width, transcendentals=0
        ),
        name="load_weights_%d" % axis,
    )(blocks, first, second)


def all_factors(blocks):
    total = square_sums(blocks, jnp.zeros((TOKENS, 128), jnp.float32))
    return row_factors(total, 16 * blocks[0].shape[1])


def project_kernel(ids, *refs):
    blocks, refs = refs[:16], refs[16:]
    gain, weights, cosine, sine, kv_cos, kv_sin = refs[:6]
    q_keep, q_send, fresh = refs[6:]
    factors = all_factors(blocks)
    total = jnp.zeros((TOKENS, 2 * HD), jnp.float32)
    for i in range(16):
        normed = normed_block(blocks[i], factors, gain[ids[i]])
        total = total + jnp.dot(normed, weights[i], preferred_element_type=jnp.float32)
    q, kv = total[:, :HD], total[:, HD:]
    q = (q * cosine[...] + pltpu.roll(q, HD // 2, 1) * sine[...]).astype(jnp.bfloat16)
    kv = (kv * kv_cos[...] + pltpu.roll(kv, HD // 2, 1) * kv_sin[...]).astype(jnp.bfloat16)
    core_one = ids[0] % 2 == 1
    q_keep[...] = jnp.where(core_one, q[SPAN:], q[:SPAN])
    q_send[...] = jnp.where(core_one, q[:SPAN], q[SPAN:])
    fresh[...] = kv


def project(ids, arrays, gain, weights, tables):
    return pl.pallas_call(
        project_kernel,
        out_shape=[jax.ShapeDtypeStruct((SPAN, HD), jnp.bfloat16)] * 2
        + [jax.ShapeDtypeStruct((TOKENS, HD), jnp.bfloat16)],
        in_specs=[SMEM] + [VMEM] * (len(arrays) + 6),
        out_specs=[VMEM] * 3,
        compiler_params=pltpu.CompilerParams(vmem_limit_bytes=24 * MIB),
        cost_estimate=pl.CostEstimate(
            flops=2 * TOKENS * weights.size, bytes_accessed=12 * MIB, transcendentals=0
        ),
        name="norm_project",
    )(ids, *arrays, gain, weights, *tables)


def cache_rows(cache, which):
    keep, came, rest = cache[0], cache[1], cache[2:]
    groups = [part[0, c, which] for part in (keep, came) for c in range(2)]
    groups += [part[x, c, which] for part in rest for x in range(2) for c in range(2)]
    return jnp.concatenate(groups, axis=0)


CONTRACT = (((1,), (1,)), ((), ()))


def scores_kernel(info, q, q_other, *refs):
    cache, scores = refs[:5], refs[5]
    core, rank = info[SEQS], info[SEQS + 1]
    queries = jnp.concatenate([q[...], q_other[...]], axis=0)
    old = lax.dot_general(
        queries, cache_rows(cache, 0), CONTRACT, preferred_element_type=jnp.float32
    )
    lane = lax.broadcasted_iota(jnp.int32, old.shape, 1)
    position = (rank ^ (lane // CTX_DEV)) * CTX_DEV + lane % CTX_DEV
    scores[...] = jnp.where(position < info[core], old * HD ** (-0.5), -1e30)


def cache_scores(info, q, q_other, cache):
    return pl.pallas_call(
        scores_kernel,
        out_shape=jax.ShapeDtypeStruct((TOKENS, 16 * CTX_DEV), jnp.float32),
        in_specs=[SMEM] + [VMEM] * 7,
        out_specs=VMEM,
        compiler_params=pltpu.CompilerParams(vmem_limit_bytes=16 * MIB),
        cost_estimate=pl.CostEstimate(flops=32 * MIB, bytes_accessed=MIB, transcendentals=0),
        name="cache_scores",
    )(info, q, q_other, *cache)


def attend_kernel(info, q, q_other, fresh_own, fresh_other, scores, *refs):
    cache, out = refs[:5], refs[5]
    core = info[SEQS]
    came = fresh_other[...]
    fresh_keys = jnp.where(core == 0, fresh_own[:SPAN, :], came)
    fresh_values = jnp.where(core == 0, came, fresh_own[SPAN:, :])
    queries = jnp.concatenate([q[...], q_other[...]], axis=0)
    old = scores[...]
    valid = old > -1e29
    fresh = lax.dot_general(
        queries, fresh_keys, CONTRACT, preferred_element_type=jnp.float32
    ) * HD ** (-0.5)
    place = lax.broadcasted_iota(jnp.int32, fresh.shape, 0) % SPAN
    causal = place >= lax.broadcasted_iota(jnp.int32, fresh.shape, 1)
    fresh = jnp.where(causal, fresh, -1e30)
    most = jnp.maximum(jnp.max(old, axis=1, keepdims=True), jnp.max(fresh, axis=1, keepdims=True))
    old_weights = jnp.where(valid, jnp.exp(old - most), 0.0)
    fresh_weights = jnp.where(causal, jnp.exp(fresh - most), 0.0)
    totals = jnp.sum(old_weights, axis=1, keepdims=True) + jnp.sum(
        fresh_weights, axis=1, keepdims=True
    )
    summed = jnp.dot(
        old_weights.astype(jnp.bfloat16), cache_rows(cache, 1), preferred_element_type=jnp.float32
    ) + jnp.dot(
        fresh_weights.astype(jnp.bfloat16), fresh_values, preferred_element_type=jnp.float32
    )
    attn = (summed / totals).astype(jnp.bfloat16)
    out[:, :HD] = attn[:SPAN]
    out[:, HD:] = attn[SPAN:]


def attend(info, q, q_other, fresh_own, fresh_other, scores, cache):
    return pl.pallas_call(
        attend_kernel,
        out_shape=jax.ShapeDtypeStruct((SPAN, 2 * HD), jnp.bfloat16),
        in_specs=[SMEM] + [VMEM] * 10,
        out_specs=VMEM,
        compiler_params=pltpu.CompilerParams(vmem_limit_bytes=16 * MIB),
        cost_estimate=pl.CostEstimate(
            flops=48 * MIB, bytes_accessed=2 * MIB, transcendentals=TOKENS * 1088
        ),
        name="attend",
    )(info, q, q_other, fresh_own, fresh_other, scores, *cache)


def both_heads(core, attn, attn_other):
    mine = attn[...]
    theirs = jnp.concatenate([attn_other[:, HD:], attn_other[:, :HD]], axis=1)
    core_one = core[0] == 1
    return jnp.concatenate(
        [jnp.where(core_one, theirs, mine), jnp.where(core_one, mine, theirs)], axis=0
    )


def shares_kernel(first, core, attn, attn_other, weights, *outs):
    rows = both_heads(core, attn, attn_other)
    for i, out in enumerate(outs):
        out[...] = jnp.dot(
            rows, weights[first + i], preferred_element_type=jnp.float32
        ).astype(out.dtype)


def shares_of(core, attn, attn_other, weights, first, last, dtype=jnp.float32):
    count, width = last - first, weights.shape[2]
    arrays = pl.pallas_call(
        functools.partial(shares_kernel, first),
        out_shape=[jax.ShapeDtypeStruct((TOKENS, width), dtype)] * count,
        in_specs=[SMEM] + [VMEM] * 3,
        out_specs=[VMEM] * count,
        compiler_params=pltpu.CompilerParams(vmem_limit_bytes=16 * MIB),
        cost_estimate=pl.CostEstimate(
            flops=4 * TOKENS * HD * width * count,
            bytes_accessed=count * MIB,
            transcendentals=0,
        ),
        name="shares_%d" % first,
    )(core, attn, attn_other, weights)
    return dict(zip(SHARES[first:last], arrays))


def final_kernel(ids, *refs):
    blocks, refs = refs[:16], refs[16:]
    gain, out, staged, sems = refs
    width = staged.shape[2]
    factors = all_factors(blocks)
    copies = []
    for i in range(16):
        staged[i] = normed_block(blocks[i], factors, gain[ids[i]])
        copy = pltpu.make_async_copy(
            staged.at[i],
            out.at[:, pl.ds(pl.multiple_of(ids[i] * width, width), width)],
            sems.at[i],
        )
        copy.start()
        copies.append(copy)
    for copy in copies:
        copy.wait()


def final_norm(ids, arrays, gain):
    width = arrays[0].shape[1]
    return pl.pallas_call(
        final_kernel,
        out_shape=jax.ShapeDtypeStruct((TOKENS, 16 * width), jnp.bfloat16),
        in_specs=[SMEM] + [VMEM] * (len(arrays) + 1),
        out_specs=HBM,
        scratch_shapes=[
            pltpu.VMEM((16, TOKENS, width), jnp.bfloat16),
            pltpu.SemaphoreType.DMA((16,)),
        ],
        compiler_params=pltpu.CompilerParams(vmem_limit_bytes=24 * MIB),
        cost_estimate=pl.CostEstimate(
            flops=16 * MIB, bytes_accessed=12 * MIB, transcendentals=0
        ),
        name="final_norm",
    )(ids, *arrays, gain)


def per_device_ring(
    residual, attn_gain, ffn_gain, q_weight, kv_weight, o_weight, key_cache, value_cache, prefix
):
    rank = lax.axis_index("tp")
    core = rank % 2
    width = residual.shape[1]
    ids = gathered_ids(rank)
    to = share_ids(rank)
    core_id, rank_id = core[None].astype(jnp.int32), rank[None].astype(jnp.int32)
    info = jnp.concatenate([prefix, core_id, rank_id])

    weight_other = send(o_weight, SWAP)
    parts = split_cache(key_cache, value_cache, rank, rank_id)
    cache, pieces = move_cache(parts)
    mine, theirs = ring_gather(residual, weight_other, direct=True)
    weights = load_weights(ids, in_hbm(q_weight), in_hbm(kv_weight), width, 0)

    positions = (prefix[:, None] + jnp.arange(SPAN, dtype=jnp.int32)[None, :]).reshape(-1)
    cosine, sine = rope_tables(positions)
    cosine = jnp.concatenate([cosine, cosine], axis=1)
    sine = jnp.concatenate([-sine, sine], axis=1)
    holds_keys = rank < KVH
    tables = (cosine, sine, jnp.where(holds_keys, cosine, 1.0), jnp.where(holds_keys, sine, 0.0))

    gain = attn_gain.reshape(16, 1, width).astype(jnp.float32)
    mine[0] = after(mine[0], pieces)
    q_keep, q_send, fresh = project(ids, mine + theirs, gain, weights, tables)
    o_weights = load_weights(after(to, fresh), in_hbm(o_weight), weight_other, width, 1)
    q_other = send(q_send, SWAP)
    fresh_own = send(after(fresh, cache[3:]), FRESH)
    fresh_other = send(jnp.where(core == 0, fresh_own[SPAN:], fresh_own[:SPAN]), SWAP)
    scores = cache_scores(info, after(q_keep, o_weights), q_other, cache)
    attn = attend(info, q_keep, q_other, fresh_own, fresh_other, scores, cache)
    attn_other = send(attn, SWAP)

    inputs = (core_id, attn, attn_other, o_weights)
    shares = shares_of(*inputs, 0, 2, jnp.bfloat16)
    shares.update(shares_of(*inputs, 2, len(SHARES)))
    one_way, other_way = ring_sum(shares)
    projected = shares[0, 0] + one_way.astype(jnp.float32) + other_way.astype(jnp.float32)
    hidden = (residual.astype(jnp.float32) + projected).astype(jnp.bfloat16)

    mine, theirs = ring_gather(hidden)
    gain = ffn_gain.reshape(16, 1, width).astype(jnp.float32)
    return final_norm(ids, mine + theirs, gain)


def per_device(
    residual, attn_gain, ffn_gain, q_weight, kv_weight, o_weight, key_cache, value_cache, prefix
):
    tp_count = lax.axis_size("tp")
    tp_rank = lax.axis_index("tp")
    heads_all = HQ_DEV * tp_count
    group_size = heads_all // KVH
    token_count = SEQS * SPAN
    score_scale = HD ** (-0.5)
    whole_rows = lax.all_gather(residual, "tp", axis=1, tiled=True)
    normed = rms_rows(whole_rows, attn_gain).astype(jnp.bfloat16)
    positions = (prefix[:, None] + jnp.arange(SPAN, dtype=jnp.int32)[None, :]).reshape(-1)
    queries = jnp.dot(normed, q_weight, preferred_element_type=jnp.float32).reshape(
        token_count, HQ_DEV, HD
    )
    queries = rotate(queries, positions).astype(jnp.bfloat16)
    kv_part = jnp.dot(normed, kv_weight, preferred_element_type=jnp.float32)
    kv_whole = lax.all_gather(kv_part, "tp", axis=1, tiled=True)
    new_keys = rotate(kv_whole[:, : KVH * HD].reshape(token_count, KVH, HD), positions).astype(
        jnp.bfloat16
    )
    new_values = kv_whole[:, KVH * HD :].reshape(token_count, KVH, HD).astype(jnp.bfloat16)
    head_ids = tp_rank * HQ_DEV + jnp.arange(HQ_DEV, dtype=jnp.int32)
    own_kv = head_ids // group_size
    own_keys = jnp.take(new_keys, own_kv, axis=1).reshape(SEQS, SPAN, HQ_DEV, HD)
    own_values = jnp.take(new_values, own_kv, axis=1).reshape(SEQS, SPAN, HQ_DEV, HD)
    own_queries = queries.reshape(SEQS, SPAN, HQ_DEV, HD)
    causal = (jnp.arange(SPAN)[:, None] >= jnp.arange(SPAN)[None, :])[None, None]
    fresh_scores = (
        jnp.einsum("schd,skhd->shck", own_queries, own_keys, preferred_element_type=jnp.float32)
        * score_scale
    )
    fresh_scores = jnp.where(causal, fresh_scores, -1e30)
    fresh_max = fresh_scores.max(-1)
    gathered = lax.all_gather(queries.reshape(token_count, HQ_DEV * HD), "tp", axis=1, tiled=True)
    queries_all = gathered.reshape(SEQS, SPAN, KVH, group_size, HD)
    keys_local = key_cache.reshape(SEQS, CTX_DEV, KVH, HD)
    values_local = value_cache.reshape(SEQS, CTX_DEV, KVH, HD)
    local_scores = (
        jnp.einsum("sckgd,sjkd->skgcj", queries_all, keys_local, preferred_element_type=jnp.float32)
        * score_scale
    )
    first_slot = tp_rank * CTX_DEV
    is_valid = ((first_slot + jnp.arange(CTX_DEV, dtype=jnp.int32))[None, :] < prefix[:, None])[
        :, None, None, None, :
    ]
    local_scores = jnp.where(is_valid, local_scores, -1e30)
    local_max = local_scores.max(-1)
    local_weights = jnp.where(is_valid, jnp.exp(local_scores - local_max[..., None]), 0.0)
    local_total = local_weights.sum(-1)
    local_sum = jnp.einsum(
        "skgcj,sjkd->skgcd",
        local_weights.astype(jnp.bfloat16),
        values_local,
        preferred_element_type=jnp.float32,
    )
    sums_in, maxes_in, totals_in = (
        lax.all_to_all(
            local_sum.reshape(1, SEQS, heads_all, SPAN, HD),
            "tp",
            split_axis=2,
            concat_axis=0,
            tiled=True,
        ),
        lax.all_to_all(
            local_max.reshape(1, SEQS, heads_all, SPAN),
            "tp",
            split_axis=2,
            concat_axis=0,
            tiled=True,
        ),
        lax.all_to_all(
            local_total.reshape(1, SEQS, heads_all, SPAN),
            "tp",
            split_axis=2,
            concat_axis=0,
            tiled=True,
        ),
    )
    running_max = jnp.maximum(maxes_in.max(0), fresh_max)
    factors = jnp.exp(maxes_in - running_max[None])
    fresh_weights = jnp.where(causal, jnp.exp(fresh_scores - running_max[..., None]), 0.0)
    totals = (factors * totals_in).sum(0) + fresh_weights.sum(-1)
    summed = (factors[..., None] * sums_in).sum(0)
    summed = summed + jnp.einsum(
        "shck,skhd->shcd",
        fresh_weights.astype(jnp.bfloat16),
        own_values,
        preferred_element_type=jnp.float32,
    )
    attn = (summed / totals[..., None]).astype(jnp.bfloat16)
    attn = jnp.transpose(attn, (0, 2, 1, 3)).reshape(token_count, HQ_DEV * HD)
    share_part = lax.psum_scatter(
        lax.dot_general(
            o_weight, attn, (((0,), (1,)), ((), ())), preferred_element_type=jnp.float32
        ),
        "tp",
        scatter_dimension=0,
        tiled=True,
    )
    hidden = (residual.astype(jnp.float32) + share_part.T).astype(jnp.bfloat16)
    stream = lax.all_gather(hidden, "tp", axis=1, tiled=True)
    return rms_rows(stream, ffn_gain).astype(jnp.bfloat16)


def solution(mesh):
    return jax.shard_map(
        per_device_ring if mesh.shape["tp"] == 2 * CHIPS else per_device,
        mesh=mesh,
        in_specs=(
            P("replica", "tp"),
            P(),
            P(),
            P(None, "tp"),
            P(None, "tp"),
            P("tp", None),
            P("replica", "tp", None),
            P("replica", "tp", None),
            P("replica"),
        ),
        out_specs=P("replica", None),
        check_vma=False,
    )
```

```python
import functools

import jax
import jax.numpy as jnp
from jax import lax
from jax.experimental import pallas as pl
from jax.experimental.pallas import tpu as pltpu
from jax.sharding import PartitionSpec as P

HD = 128
KVH = 8
HQ_DEV = 1
SPAN = 64
SEQS = 2
CTX_DEV = 64
TOKENS = SEQS * SPAN
MIB = 1024 * 1024

epsilon = 1e-05


def rms_rows(rows, gain):
    values_f = rows.astype(jnp.float32)
    factor = lax.rsqrt(jnp.mean(values_f * values_f, axis=-1, keepdims=True) + epsilon)
    return values_f * factor * gain.astype(jnp.float32)


def rope_tables(positions):
    half_width = HD // 2
    frequency = 500000.0 ** (-jnp.arange(half_width, dtype=jnp.float32) / half_width)
    angles = positions.astype(jnp.float32)[:, None] * frequency[None, :]
    return jnp.cos(angles), jnp.sin(angles)


def rotate(vectors, positions):
    half_width = vectors.shape[-1] // 2
    cosine, sine = rope_tables(positions)
    cosine, sine = cosine[:, None, :], sine[:, None, :]
    first_half = vectors[..., :half_width]
    second_half = vectors[..., half_width:]
    return jnp.concatenate(
        [first_half * cosine - second_half * sine, second_half * cosine + first_half * sine],
        axis=-1,
    )


CHIPS = 8
RING = (0, 2, 4, 6, 7, 5, 3, 1)
ONWARD = [(2 * RING[i], 2 * RING[(i + 1) % CHIPS]) for i in range(CHIPS)] + [
    (2 * RING[i] + 1, 2 * RING[i - 1] + 1) for i in range(CHIPS)
]
ENTER = [(2 * RING[i], 2 * RING[i - 1] + 1) for i in range(CHIPS)] + [
    (2 * RING[i] + 1, 2 * RING[(i + 1) % CHIPS]) for i in range(CHIPS)
]
LEAVE = [(2 * RING[i], 2 * RING[(i + 1) % CHIPS] + 1) for i in range(CHIPS)] + [
    (2 * RING[i] + 1, 2 * RING[i - 1]) for i in range(CHIPS)
]
SWAP = [(t, t ^ 1) for t in range(2 * CHIPS)]
FRESH = [(k, 2 * k) for k in range(KVH)] + [(KVH + k, 2 * k + 1) for k in range(KVH)]
VMEM = pl.BlockSpec(memory_space=pltpu.VMEM)
SMEM = pl.BlockSpec(memory_space=pltpu.SMEM)
HBM = pl.BlockSpec(memory_space=pltpu.HBM)


def ring_place(rank):
    chip = rank // 2
    return jnp.where(chip % 2 == 0, chip // 2, CHIPS - 1 - chip // 2)


def chip_at(place):
    place = place % CHIPS
    return jnp.where(place < CHIPS // 2, 2 * place, 2 * CHIPS - 1 - 2 * place)


def send(array, pairs):
    return lax.ppermute(array, "tp", pairs)


def xor(bits):
    return [(t, t ^ bits) for t in range(2 * CHIPS)]


def after(array, *others):
    return lax.optimization_barrier((array, others))[0]


def ring_gather(own, ready=None, direct=False):
    straight, swapped = own, None if direct else send(own, SWAP)
    crossed = own if direct else swapped
    mine = [own]
    for step in range(1, 5):
        if step == 4 and ready is not None:
            straight = after(straight, ready)
        straight = send(straight, ONWARD)
        mine.append(straight)
        if step < 4:
            crossed = send(crossed, ENTER if direct and step == 1 else ONWARD)
            mine.append(crossed)
    theirs = [send(own, SWAP) if direct else swapped]
    return mine, theirs + [send(block, SWAP) for block in mine[1:]]


def gathered_ids(rank):
    place = ring_place(rank)
    ids = []
    for side in range(2):
        device = rank ^ side
        core = device % 2
        ids.append(device)
        for step in range(1, 5):
            chip = 2 * chip_at(place + (2 * core - 1) * step)
            ids += [chip + core, chip + 1 - core] if step < 4 else [chip + core]
    return jnp.stack(ids).astype(jnp.int32)


SHARES = ((4, 0), (3, 1), (3, 0), (2, 1), (2, 0), (1, 1), (1, 0), (0, 0))


def share_ids(rank):
    place, core = ring_place(rank), rank % 2
    return jnp.stack(
        [2 * chip_at(place + (1 - 2 * core) * d) + (core + other) % 2 for d, other in SHARES]
    ).astype(jnp.int32)


def ring_sum(shares):
    straight, crossed = shares[4, 0], shares[3, 1]
    for step in range(1, 5):
        straight = send(straight, ONWARD)
        if step < 4:
            crossed = send(crossed, LEAVE if step == 3 else ONWARD)
            straight = add_share(straight, shares[4 - step, 0])
        if step < 3:
            crossed = add_share(crossed, shares[3 - step, 1])
    return straight, crossed


def add_share(part, share):
    return (part.astype(jnp.float32) + share).astype(jnp.bfloat16)


def split_cache(key_cache, value_cache, rank, rank_id):
    core = rank % 2
    give = jnp.stack(
        [lax.dynamic_index_in_dim(c, 1 - core, 0, keepdims=False) for c in (key_cache, value_cache)]
    )
    return pack(rank_id, key_cache, value_cache, send(give, SWAP))


def move_cache(parts, *when):
    keep, give = parts
    came = send(give, xor(2))
    pieces = [jnp.stack([keep[m], came[m]]) for m in range(1, 4)]
    return [keep, came] + [send(piece, xor(4 * m)) for m, piece in zip(range(1, 4), pieces)]


def pack_kernel(rank, keys, values, theirs, keep, give, sems):
    me = rank[0]
    copies = []
    for m in range(4):
        for j, out in enumerate((keep, give)):
            chip = (me ^ (4 * m + 2 * j)) // 2
            head = pl.ds(pl.multiple_of(chip * HD, HD), HD)
            for k, cache in enumerate((keys, values)):
                copies.append(
                    pltpu.make_async_copy(
                        cache.at[me % 2, :, head], out.at[m, 0, k], sems.at[m, j, k]
                    )
                )
                copies[-1].start()
            out[m, 1, 0] = theirs[0, :, head]
            out[m, 1, 1] = theirs[1, :, head]
    for copy in copies:
        copy.wait()


def pack(rank_id, key_cache, value_cache, theirs):
    return pl.pallas_call(
        pack_kernel,
        out_shape=[jax.ShapeDtypeStruct((4, 2, 2, CTX_DEV, HD), jnp.bfloat16)] * 2,
        in_specs=[SMEM] + [HBM] * 2 + [VMEM],
        out_specs=[VMEM] * 2,
        scratch_shapes=[pltpu.SemaphoreType.DMA((4, 2, 2))],
        compiler_params=pltpu.CompilerParams(vmem_limit_bytes=8 * MIB),
        cost_estimate=pl.CostEstimate(flops=0, bytes_accessed=MIB, transcendentals=0),
        name="pack_cache",
    )(rank_id, in_hbm(key_cache), in_hbm(value_cache), theirs)


def lanes(block, j):
    return block[:, 128 * j : 128 * j + 128].astype(jnp.float32)


def square_sums(blocks, total):
    for block in blocks:
        for j in range(block.shape[1] // 128):
            v = lanes(block, j)
            total = total + v * v
    return total


def row_factors(squares, features):
    mean = jnp.sum(squares, axis=1, keepdims=True) * (1.0 / features)
    return lax.rsqrt(mean + epsilon)


def normed_block(block, factors, gain_row):
    return jnp.concatenate(
        [
            (lanes(block, j) * factors * gain_row[:, 128 * j : 128 * j + 128]).astype(jnp.bfloat16)
            for j in range(block.shape[1] // 128)
        ],
        axis=1,
    )


def in_hbm(array):
    return pltpu.with_memory_space_constraint(array, pltpu.HBM)


def load_kernel(ids, wq, wkv, out, sems):
    count, width, _ = out.shape
    copies = []
    for i in range(count):
        rows = pl.ds(pl.multiple_of(ids[i] * width, width), width)
        for j, weight in enumerate((wq, wkv)):
            copies.append(
                pltpu.make_async_copy(
                    weight.at[rows, :], out.at[i, :, pl.ds(j * HD, HD)], sems.at[j, i]
                )
            )
            copies[-1].start()
    for copy in copies:
        copy.wait()


def load_weights(ids, wq, wkv, width):
    return pl.pallas_call(
        load_kernel,
        out_shape=jax.ShapeDtypeStruct((16, width, 2 * HD), jnp.bfloat16),
        in_specs=[SMEM] + [HBM] * 2,
        out_specs=VMEM,
        scratch_shapes=[pltpu.SemaphoreType.DMA((2, 16))],
        compiler_params=pltpu.CompilerParams(vmem_limit_bytes=16 * MIB),
        cost_estimate=pl.CostEstimate(flops=0, bytes_accessed=16 * MIB, transcendentals=0),
        name="load_weights",
    )(ids, in_hbm(wq), in_hbm(wkv))


def all_factors(blocks):
    total = square_sums(blocks, jnp.zeros((TOKENS, 128), jnp.float32))
    return row_factors(total, 16 * blocks[0].shape[1])


def project_kernel(ids, *refs):
    blocks, refs = refs[:16], refs[16:]
    gain, weights, cosine, sine, kv_cos, kv_sin = refs[:6]
    q_keep, q_send, fresh = refs[6:]
    factors = all_factors(blocks)
    total = jnp.zeros((TOKENS, 2 * HD), jnp.float32)
    for i in range(16):
        normed = normed_block(blocks[i], factors, gain[ids[i]])
        total = total + jnp.dot(normed, weights[i], preferred_element_type=jnp.float32)
    q, kv = total[:, :HD], total[:, HD:]
    q = (q * cosine[...] + pltpu.roll(q, HD // 2, 1) * sine[...]).astype(jnp.bfloat16)
    kv = (kv * kv_cos[...] + pltpu.roll(kv, HD // 2, 1) * kv_sin[...]).astype(jnp.bfloat16)
    core_one = ids[0] % 2 == 1
    q_keep[...] = jnp.where(core_one, q[SPAN:], q[:SPAN])
    q_send[...] = jnp.where(core_one, q[:SPAN], q[SPAN:])
    fresh[...] = kv


def project(ids, arrays, gain, weights, tables):
    return pl.pallas_call(
        project_kernel,
        out_shape=[jax.ShapeDtypeStruct((SPAN, HD), jnp.bfloat16)] * 2
        + [jax.ShapeDtypeStruct((TOKENS, HD), jnp.bfloat16)],
        in_specs=[SMEM] + [VMEM] * (len(arrays) + 6),
        out_specs=[VMEM] * 3,
        compiler_params=pltpu.CompilerParams(vmem_limit_bytes=24 * MIB),
        cost_estimate=pl.CostEstimate(
            flops=2 * TOKENS * weights.size, bytes_accessed=12 * MIB, transcendentals=0
        ),
        name="norm_project",
    )(ids, *arrays, gain, weights, *tables)


def share_copies(to, first, weight, weight_other, out, sems):
    count, _, width = out.shape
    copies = []
    for i in range(count):
        columns = pl.ds(pl.multiple_of(to[first + i] * width, width), width)
        pair = [
            pltpu.make_async_copy(part.at[:, columns], out.at[i, pl.ds(j * HD, HD), :], sems.at[j, i])
            for j, part in enumerate((weight, weight_other))
        ]
        for copy in pair:
            copy.start()
        copies.append(pair)
    return copies


def cache_rows(cache, which):
    keep, came, rest = cache[0], cache[1], cache[2:]
    groups = [part[0, c, which] for part in (keep, came) for c in range(2)]
    groups += [part[x, c, which] for part in rest for x in range(2) for c in range(2)]
    return jnp.concatenate(groups, axis=0)


CONTRACT = (((1,), (1,)), ((), ()))


def scores_kernel(info, to, q, q_other, *refs):
    cache, weight, weight_other, scores, weights, sems = refs[:5], *refs[5:]
    copies = share_copies(to, 0, weight, weight_other, weights, sems)
    core, rank = info[SEQS], info[SEQS + 1]
    queries = jnp.concatenate([q[...], q_other[...]], axis=0)
    old = lax.dot_general(
        queries, cache_rows(cache, 0), CONTRACT, preferred_element_type=jnp.float32
    )
    lane = lax.broadcasted_iota(jnp.int32, old.shape, 1)
    position = (rank ^ (lane // CTX_DEV)) * CTX_DEV + lane % CTX_DEV
    scores[...] = jnp.where(position < info[core], old * HD ** (-0.5), -1e30)
    for pair in copies:
        for copy in pair:
            copy.wait()


def cache_scores(info, to, q, q_other, cache, weight, weight_other, ahead):
    width = weight.shape[1] // 16
    return pl.pallas_call(
        scores_kernel,
        out_shape=[
            jax.ShapeDtypeStruct((TOKENS, 16 * CTX_DEV), jnp.float32),
            jax.ShapeDtypeStruct((ahead, 2 * HD, width), jnp.bfloat16),
        ],
        in_specs=[SMEM] * 2 + [VMEM] * 7 + [HBM] * 2,
        out_specs=[VMEM] * 2,
        scratch_shapes=[pltpu.SemaphoreType.DMA((2, ahead))],
        compiler_params=pltpu.CompilerParams(vmem_limit_bytes=16 * MIB),
        cost_estimate=pl.CostEstimate(
            flops=32 * MIB, bytes_accessed=3 * MIB, transcendentals=0
        ),
        name="cache_scores",
    )(info, to, q, q_other, *cache, in_hbm(weight), weight_other)


def attend_kernel(info, q, q_other, fresh_own, fresh_other, scores, *refs):
    cache, out = refs[:5], refs[5]
    core = info[SEQS]
    came = fresh_other[...]
    fresh_keys = jnp.where(core == 0, fresh_own[:SPAN, :], came)
    fresh_values = jnp.where(core == 0, came, fresh_own[SPAN:, :])
    queries = jnp.concatenate([q[...], q_other[...]], axis=0)
    old = scores[...]
    valid = old > -1e29
    fresh = lax.dot_general(
        queries, fresh_keys, CONTRACT, preferred_element_type=jnp.float32
    ) * HD ** (-0.5)
    place = lax.broadcasted_iota(jnp.int32, fresh.shape, 0) % SPAN
    causal = place >= lax.broadcasted_iota(jnp.int32, fresh.shape, 1)
    fresh = jnp.where(causal, fresh, -1e30)
    most = jnp.maximum(jnp.max(old, axis=1, keepdims=True), jnp.max(fresh, axis=1, keepdims=True))
    old_weights = jnp.where(valid, jnp.exp(old - most), 0.0)
    fresh_weights = jnp.where(causal, jnp.exp(fresh - most), 0.0)
    totals = jnp.sum(old_weights, axis=1, keepdims=True) + jnp.sum(
        fresh_weights, axis=1, keepdims=True
    )
    summed = jnp.dot(
        old_weights.astype(jnp.bfloat16), cache_rows(cache, 1), preferred_element_type=jnp.float32
    ) + jnp.dot(
        fresh_weights.astype(jnp.bfloat16), fresh_values, preferred_element_type=jnp.float32
    )
    attn = (summed / totals).astype(jnp.bfloat16)
    out[:, :HD] = attn[:SPAN]
    out[:, HD:] = attn[SPAN:]


def attend(info, q, q_other, fresh_own, fresh_other, scores, cache):
    return pl.pallas_call(
        attend_kernel,
        out_shape=jax.ShapeDtypeStruct((SPAN, 2 * HD), jnp.bfloat16),
        in_specs=[SMEM] + [VMEM] * 10,
        out_specs=VMEM,
        compiler_params=pltpu.CompilerParams(vmem_limit_bytes=16 * MIB),
        cost_estimate=pl.CostEstimate(
            flops=48 * MIB, bytes_accessed=2 * MIB, transcendentals=TOKENS * 1088
        ),
        name="attend",
    )(info, q, q_other, fresh_own, fresh_other, scores, *cache)


def both_heads(core, attn, attn_other):
    mine = attn[...]
    theirs = jnp.concatenate([attn_other[:, HD:], attn_other[:, :HD]], axis=1)
    core_one = core[0] == 1
    return jnp.concatenate(
        [jnp.where(core_one, theirs, mine), jnp.where(core_one, mine, theirs)], axis=0
    )


def first_shares_kernel(core, attn, attn_other, weights, *outs):
    rows = both_heads(core, attn, attn_other)
    for i, out in enumerate(outs):
        out[...] = jnp.dot(rows, weights[i], preferred_element_type=jnp.float32).astype(out.dtype)


def first_shares(shares, core, attn, attn_other, weights):
    count, _, width = weights.shape
    out_shape = [jax.ShapeDtypeStruct((TOKENS, width), jnp.bfloat16)] * count
    arrays = pl.pallas_call(
        first_shares_kernel,
        out_shape=out_shape,
        in_specs=[SMEM] + [VMEM] * 3,
        out_specs=[VMEM] * len(out_shape),
        compiler_params=pltpu.CompilerParams(vmem_limit_bytes=16 * MIB),
        cost_estimate=pl.CostEstimate(
            flops=2 * TOKENS * weights.size, bytes_accessed=count * MIB, transcendentals=0
        ),
        name="first_shares",
    )(core, attn, attn_other, weights)
    return dict(zip(shares, arrays))


def more_shares_kernel(first, core, to, attn, attn_other, weight, weight_other, *refs):
    outs, (weights, sems) = refs[:-2], refs[-2:]
    copies = share_copies(to, first, weight, weight_other, weights, sems)
    rows = both_heads(core, attn, attn_other)
    for i, out in enumerate(outs):
        for copy in copies[i]:
            copy.wait()
        out[...] = jnp.dot(rows, weights[i], preferred_element_type=jnp.float32)


def more_shares(core, to, attn, attn_other, weight, weight_other, first, last):
    count, width = last - first, weight.shape[1] // 16
    out_shape = [jax.ShapeDtypeStruct((TOKENS, width), jnp.float32)] * count
    arrays = pl.pallas_call(
        functools.partial(more_shares_kernel, first),
        out_shape=out_shape,
        in_specs=[SMEM] * 2 + [VMEM] * 2 + [HBM] * 2,
        out_specs=[VMEM] * len(out_shape),
        scratch_shapes=[
            pltpu.VMEM((count, 2 * HD, width), jnp.bfloat16),
            pltpu.SemaphoreType.DMA((2, count)),
        ],
        compiler_params=pltpu.CompilerParams(vmem_limit_bytes=16 * MIB),
        cost_estimate=pl.CostEstimate(
            flops=4 * TOKENS * HD * width * count,
            bytes_accessed=count * MIB,
            transcendentals=0,
        ),
        name="shares_%d" % first,
    )(core, to, attn, attn_other, in_hbm(weight), weight_other)
    return dict(zip(SHARES[first:last], arrays))


def final_kernel(ids, *refs):
    blocks, refs = refs[:16], refs[16:]
    gain, out, staged, sems = refs
    width = staged.shape[2]
    factors = all_factors(blocks)
    copies = []
    for i in range(16):
        staged[i] = normed_block(blocks[i], factors, gain[ids[i]])
        copy = pltpu.make_async_copy(
            staged.at[i],
            out.at[:, pl.ds(pl.multiple_of(ids[i] * width, width), width)],
            sems.at[i],
        )
        copy.start()
        copies.append(copy)
    for copy in copies:
        copy.wait()


def final_norm(ids, arrays, gain):
    width = arrays[0].shape[1]
    return pl.pallas_call(
        final_kernel,
        out_shape=jax.ShapeDtypeStruct((TOKENS, 16 * width), jnp.bfloat16),
        in_specs=[SMEM] + [VMEM] * (len(arrays) + 1),
        out_specs=HBM,
        scratch_shapes=[
            pltpu.VMEM((16, TOKENS, width), jnp.bfloat16),
            pltpu.SemaphoreType.DMA((16,)),
        ],
        compiler_params=pltpu.CompilerParams(vmem_limit_bytes=24 * MIB),
        cost_estimate=pl.CostEstimate(
            flops=16 * MIB, bytes_accessed=12 * MIB, transcendentals=0
        ),
        name="final_norm",
    )(ids, *arrays, gain)


def per_device_ring(
    residual, attn_gain, ffn_gain, q_weight, kv_weight, o_weight, key_cache, value_cache, prefix
):
    rank = lax.axis_index("tp")
    core = rank % 2
    width = residual.shape[1]
    ids = gathered_ids(rank)
    to = share_ids(rank)
    core_id, rank_id = core[None].astype(jnp.int32), rank[None].astype(jnp.int32)
    info = jnp.concatenate([prefix, core_id, rank_id])

    weight_other = send(o_weight, SWAP)
    parts = split_cache(key_cache, value_cache, rank, rank_id)
    mine, theirs = ring_gather(residual, weight_other, direct=True)
    weights = load_weights(ids, q_weight, kv_weight, width)
    cache = move_cache(parts)

    positions = (prefix[:, None] + jnp.arange(SPAN, dtype=jnp.int32)[None, :]).reshape(-1)
    cosine, sine = rope_tables(positions)
    cosine = jnp.concatenate([cosine, cosine], axis=1)
    sine = jnp.concatenate([-sine, sine], axis=1)
    holds_keys = rank < KVH
    tables = (cosine, sine, jnp.where(holds_keys, cosine, 1.0), jnp.where(holds_keys, sine, 0.0))

    gain = attn_gain.reshape(16, 1, width).astype(jnp.float32)
    mine[0] = after(mine[0], cache[1])
    q_keep, q_send, fresh = project(ids, mine + theirs, gain, weights, tables)
    q_other = send(q_send, SWAP)
    fresh_own = send(fresh, FRESH)
    fresh_other = send(jnp.where(core == 0, fresh_own[SPAN:], fresh_own[:SPAN]), SWAP)
    scores, first_weights = cache_scores(
        info, to, q_keep, q_other, cache, o_weight, weight_other, 2
    )
    attn = attend(info, q_keep, q_other, fresh_own, fresh_other, scores, cache)
    attn_other = send(attn, SWAP)

    shares = first_shares(SHARES[:2], core_id, attn, attn_other, first_weights)
    inputs = (attn, attn_other, o_weight, weight_other)
    for first, last in ((2, 4), (4, len(SHARES))):
        shares.update(more_shares(core_id, to, *inputs, first, last))
    one_way, other_way = ring_sum(shares)
    projected = shares[0, 0] + one_way.astype(jnp.float32) + other_way.astype(jnp.float32)
    hidden = (residual.astype(jnp.float32) + projected).astype(jnp.bfloat16)

    mine, theirs = ring_gather(hidden)
    gain = ffn_gain.reshape(16, 1, width).astype(jnp.float32)
    return final_norm(ids, mine + theirs, gain)


def per_device(
    residual, attn_gain, ffn_gain, q_weight, kv_weight, o_weight, key_cache, value_cache, prefix
):
    tp_count = lax.axis_size("tp")
    tp_rank = lax.axis_index("tp")
    heads_all = HQ_DEV * tp_count
    group_size = heads_all // KVH
    token_count = SEQS * SPAN
    score_scale = HD ** (-0.5)
    whole_rows = lax.all_gather(residual, "tp", axis=1, tiled=True)
    normed = rms_rows(whole_rows, attn_gain).astype(jnp.bfloat16)
    positions = (prefix[:, None] + jnp.arange(SPAN, dtype=jnp.int32)[None, :]).reshape(-1)
    queries = jnp.dot(normed, q_weight, preferred_element_type=jnp.float32).reshape(
        token_count, HQ_DEV, HD
    )
    queries = rotate(queries, positions).astype(jnp.bfloat16)
    kv_part = jnp.dot(normed, kv_weight, preferred_element_type=jnp.float32)
    kv_whole = lax.all_gather(kv_part, "tp", axis=1, tiled=True)
    new_keys = rotate(kv_whole[:, : KVH * HD].reshape(token_count, KVH, HD), positions).astype(
        jnp.bfloat16
    )
    new_values = kv_whole[:, KVH * HD :].reshape(token_count, KVH, HD).astype(jnp.bfloat16)
    head_ids = tp_rank * HQ_DEV + jnp.arange(HQ_DEV, dtype=jnp.int32)
    own_kv = head_ids // group_size
    own_keys = jnp.take(new_keys, own_kv, axis=1).reshape(SEQS, SPAN, HQ_DEV, HD)
    own_values = jnp.take(new_values, own_kv, axis=1).reshape(SEQS, SPAN, HQ_DEV, HD)
    own_queries = queries.reshape(SEQS, SPAN, HQ_DEV, HD)
    causal = (jnp.arange(SPAN)[:, None] >= jnp.arange(SPAN)[None, :])[None, None]
    fresh_scores = (
        jnp.einsum("schd,skhd->shck", own_queries, own_keys, preferred_element_type=jnp.float32)
        * score_scale
    )
    fresh_scores = jnp.where(causal, fresh_scores, -1e30)
    fresh_max = fresh_scores.max(-1)
    gathered = lax.all_gather(queries.reshape(token_count, HQ_DEV * HD), "tp", axis=1, tiled=True)
    queries_all = gathered.reshape(SEQS, SPAN, KVH, group_size, HD)
    keys_local = key_cache.reshape(SEQS, CTX_DEV, KVH, HD)
    values_local = value_cache.reshape(SEQS, CTX_DEV, KVH, HD)
    local_scores = (
        jnp.einsum("sckgd,sjkd->skgcj", queries_all, keys_local, preferred_element_type=jnp.float32)
        * score_scale
    )
    first_slot = tp_rank * CTX_DEV
    is_valid = ((first_slot + jnp.arange(CTX_DEV, dtype=jnp.int32))[None, :] < prefix[:, None])[
        :, None, None, None, :
    ]
    local_scores = jnp.where(is_valid, local_scores, -1e30)
    local_max = local_scores.max(-1)
    local_weights = jnp.where(is_valid, jnp.exp(local_scores - local_max[..., None]), 0.0)
    local_total = local_weights.sum(-1)
    local_sum = jnp.einsum(
        "skgcj,sjkd->skgcd",
        local_weights.astype(jnp.bfloat16),
        values_local,
        preferred_element_type=jnp.float32,
    )
    sums_in, maxes_in, totals_in = (
        lax.all_to_all(
            local_sum.reshape(1, SEQS, heads_all, SPAN, HD),
            "tp",
            split_axis=2,
            concat_axis=0,
            tiled=True,
        ),
        lax.all_to_all(
            local_max.reshape(1, SEQS, heads_all, SPAN),
            "tp",
            split_axis=2,
            concat_axis=0,
            tiled=True,
        ),
        lax.all_to_all(
            local_total.reshape(1, SEQS, heads_all, SPAN),
            "tp",
            split_axis=2,
            concat_axis=0,
            tiled=True,
        ),
    )
    running_max = jnp.maximum(maxes_in.max(0), fresh_max)
    factors = jnp.exp(maxes_in - running_max[None])
    fresh_weights = jnp.where(causal, jnp.exp(fresh_scores - running_max[..., None]), 0.0)
    totals = (factors * totals_in).sum(0) + fresh_weights.sum(-1)
    summed = (factors[..., None] * sums_in).sum(0)
    summed = summed + jnp.einsum(
        "shck,skhd->shcd",
        fresh_weights.astype(jnp.bfloat16),
        own_values,
        preferred_element_type=jnp.float32,
    )
    attn = (summed / totals[..., None]).astype(jnp.bfloat16)
    attn = jnp.transpose(attn, (0, 2, 1, 3)).reshape(token_count, HQ_DEV * HD)
    share_part = lax.psum_scatter(
        lax.dot_general(
            o_weight, attn, (((0,), (1,)), ((), ())), preferred_element_type=jnp.float32
        ),
        "tp",
        scatter_dimension=0,
        tiled=True,
    )
    hidden = (residual.astype(jnp.float32) + share_part.T).astype(jnp.bfloat16)
    stream = lax.all_gather(hidden, "tp", axis=1, tiled=True)
    return rms_rows(stream, ffn_gain).astype(jnp.bfloat16)


def solution(mesh):
    return jax.shard_map(
        per_device_ring if mesh.shape["tp"] == 2 * CHIPS else per_device,
        mesh=mesh,
        in_specs=(
            P("replica", "tp"),
            P(),
            P(),
            P(None, "tp"),
            P(None, "tp"),
            P("tp", None),
            P("replica", "tp", None),
            P("replica", "tp", None),
            P("replica"),
        ),
        out_specs=P("replica", None),
        check_vma=False,
    )
```

```python
import functools

import jax
import jax.numpy as jnp
from jax import lax
from jax.experimental import pallas as pl
from jax.experimental.pallas import tpu as pltpu
from jax.sharding import PartitionSpec as P

HD = 128
KVH = 8
HQ_DEV = 1
SPAN = 64
SEQS = 2
CTX_DEV = 64
TOKENS = SEQS * SPAN
MIB = 1024 * 1024

epsilon = 1e-05


def rms_rows(rows, gain):
    values_f = rows.astype(jnp.float32)
    factor = lax.rsqrt(jnp.mean(values_f * values_f, axis=-1, keepdims=True) + epsilon)
    return values_f * factor * gain.astype(jnp.float32)


def rope_tables(positions):
    half_width = HD // 2
    frequency = 500000.0 ** (-jnp.arange(half_width, dtype=jnp.float32) / half_width)
    angles = positions.astype(jnp.float32)[:, None] * frequency[None, :]
    return jnp.cos(angles), jnp.sin(angles)


def rotate(vectors, positions):
    half_width = vectors.shape[-1] // 2
    cosine, sine = rope_tables(positions)
    cosine, sine = cosine[:, None, :], sine[:, None, :]
    first_half = vectors[..., :half_width]
    second_half = vectors[..., half_width:]
    return jnp.concatenate(
        [first_half * cosine - second_half * sine, second_half * cosine + first_half * sine],
        axis=-1,
    )


CHIPS = 8
RING = (0, 2, 4, 6, 7, 5, 3, 1)
ONWARD = [(2 * RING[i], 2 * RING[(i + 1) % CHIPS]) for i in range(CHIPS)] + [
    (2 * RING[i] + 1, 2 * RING[i - 1] + 1) for i in range(CHIPS)
]
ENTER = [(2 * RING[i], 2 * RING[i - 1] + 1) for i in range(CHIPS)] + [
    (2 * RING[i] + 1, 2 * RING[(i + 1) % CHIPS]) for i in range(CHIPS)
]
LEAVE = [(2 * RING[i], 2 * RING[(i + 1) % CHIPS] + 1) for i in range(CHIPS)] + [
    (2 * RING[i] + 1, 2 * RING[i - 1]) for i in range(CHIPS)
]
SWAP = [(t, t ^ 1) for t in range(2 * CHIPS)]
FRESH = [(k, 2 * k) for k in range(KVH)] + [(KVH + k, 2 * k + 1) for k in range(KVH)]
VMEM = pl.BlockSpec(memory_space=pltpu.VMEM)
SMEM = pl.BlockSpec(memory_space=pltpu.SMEM)
HBM = pl.BlockSpec(memory_space=pltpu.HBM)


def ring_place(rank):
    chip = rank // 2
    return jnp.where(chip % 2 == 0, chip // 2, CHIPS - 1 - chip // 2)


def chip_at(place):
    place = place % CHIPS
    return jnp.where(place < CHIPS // 2, 2 * place, 2 * CHIPS - 1 - 2 * place)


def send(array, pairs):
    return lax.ppermute(array, "tp", pairs)


def xor(bits):
    return [(t, t ^ bits) for t in range(2 * CHIPS)]


def after(array, *others):
    return lax.optimization_barrier((array, others))[0]


def ring_gather(own, ready=None, direct=False, early=None):
    straight, swapped = own, None if direct else send(own, SWAP)
    crossed = own if direct else swapped
    mine = [own]
    for step in range(1, 5):
        if step == 2 and early is not None:
            straight = after(straight, early)
        if step == 4 and ready is not None:
            straight = after(straight, ready)
        straight = send(straight, ONWARD)
        mine.append(straight)
        if step < 4:
            crossed = send(crossed, ENTER if direct and step == 1 else ONWARD)
            mine.append(crossed)
    theirs = [send(own, SWAP) if direct else swapped]
    return mine, theirs + [send(block, SWAP) for block in mine[1:]]


def gathered_ids(rank):
    place = ring_place(rank)
    ids = []
    for side in range(2):
        device = rank ^ side
        core = device % 2
        ids.append(device)
        for step in range(1, 5):
            chip = 2 * chip_at(place + (2 * core - 1) * step)
            ids += [chip + core, chip + 1 - core] if step < 4 else [chip + core]
    return jnp.stack(ids).astype(jnp.int32)


SHARES = ((4, 0), (3, 1), (3, 0), (2, 1), (2, 0), (1, 1), (1, 0), (0, 0))


def share_ids(rank):
    place, core = ring_place(rank), rank % 2
    return jnp.stack(
        [2 * chip_at(place + (1 - 2 * core) * d) + (core + other) % 2 for d, other in SHARES]
    ).astype(jnp.int32)


def ring_sum(shares):
    straight, crossed = shares[4, 0], shares[3, 1]
    for step in range(1, 5):
        straight = send(straight, ONWARD)
        if step < 4:
            crossed = send(crossed, LEAVE if step == 3 else ONWARD)
            straight = add_share(straight, shares[4 - step, 0])
        if step < 3:
            crossed = add_share(crossed, shares[3 - step, 1])
    return straight, crossed


def add_share(part, share):
    return (part.astype(jnp.float32) + share).astype(jnp.bfloat16)


def split_cache(key_cache, value_cache, rank, rank_id):
    core = rank % 2
    give = jnp.stack(
        [lax.dynamic_index_in_dim(c, 1 - core, 0, keepdims=False) for c in (key_cache, value_cache)]
    )
    return pack(rank_id, key_cache, value_cache, send(give, SWAP))


def move_cache(parts, *when):
    keep, give = parts
    came = send(give, xor(2))
    pieces = [jnp.stack([keep[m], came[m]]) for m in range(1, 4)]
    return [keep, came] + [send(piece, xor(4 * m)) for m, piece in zip(range(1, 4), pieces)]


def pack_kernel(rank, keys, values, theirs, keep, give, sems):
    me = rank[0]
    copies = []
    for m in range(4):
        for j, out in enumerate((keep, give)):
            chip = (me ^ (4 * m + 2 * j)) // 2
            head = pl.ds(pl.multiple_of(chip * HD, HD), HD)
            for k, cache in enumerate((keys, values)):
                copies.append(
                    pltpu.make_async_copy(
                        cache.at[me % 2, :, head], out.at[m, 0, k], sems.at[m, j, k]
                    )
                )
                copies[-1].start()
            out[m, 1, 0] = theirs[0, :, head]
            out[m, 1, 1] = theirs[1, :, head]
    for copy in copies:
        copy.wait()


def pack(rank_id, key_cache, value_cache, theirs):
    return pl.pallas_call(
        pack_kernel,
        out_shape=[jax.ShapeDtypeStruct((4, 2, 2, CTX_DEV, HD), jnp.bfloat16)] * 2,
        in_specs=[SMEM] + [HBM] * 2 + [VMEM],
        out_specs=[VMEM] * 2,
        scratch_shapes=[pltpu.SemaphoreType.DMA((4, 2, 2))],
        compiler_params=pltpu.CompilerParams(vmem_limit_bytes=8 * MIB),
        cost_estimate=pl.CostEstimate(flops=0, bytes_accessed=MIB, transcendentals=0),
        name="pack_cache",
    )(rank_id, in_hbm(key_cache), in_hbm(value_cache), theirs)


def lanes(block, j):
    return block[:, 128 * j : 128 * j + 128].astype(jnp.float32)


def square_sums(blocks, total):
    for block in blocks:
        for j in range(block.shape[1] // 128):
            v = lanes(block, j)
            total = total + v * v
    return total


def row_factors(squares, features):
    mean = jnp.sum(squares, axis=1, keepdims=True) * (1.0 / features)
    return lax.rsqrt(mean + epsilon)


def normed_block(block, factors, gain_row):
    return jnp.concatenate(
        [
            (lanes(block, j) * factors * gain_row[:, 128 * j : 128 * j + 128]).astype(jnp.bfloat16)
            for j in range(block.shape[1] // 128)
        ],
        axis=1,
    )


def in_hbm(array):
    return pltpu.with_memory_space_constraint(array, pltpu.HBM)


def load_kernel(ids, wq, wkv, out, sems):
    count, width, _ = out.shape
    copies = []
    for i in range(count):
        rows = pl.ds(pl.multiple_of(ids[i] * width, width), width)
        for j, weight in enumerate((wq, wkv)):
            copies.append(
                pltpu.make_async_copy(
                    weight.at[rows, :], out.at[i, :, pl.ds(j * HD, HD)], sems.at[j, i]
                )
            )
            copies[-1].start()
    for copy in copies:
        copy.wait()


def load_weights(ids, wq, wkv, width):
    return pl.pallas_call(
        load_kernel,
        out_shape=jax.ShapeDtypeStruct((16, width, 2 * HD), jnp.bfloat16),
        in_specs=[SMEM] + [HBM] * 2,
        out_specs=VMEM,
        scratch_shapes=[pltpu.SemaphoreType.DMA((2, 16))],
        compiler_params=pltpu.CompilerParams(vmem_limit_bytes=16 * MIB),
        cost_estimate=pl.CostEstimate(flops=0, bytes_accessed=16 * MIB, transcendentals=0),
        name="load_weights",
    )(ids, in_hbm(wq), in_hbm(wkv))


def all_factors(blocks):
    total = square_sums(blocks, jnp.zeros((TOKENS, 128), jnp.float32))
    return row_factors(total, 16 * blocks[0].shape[1])


def project_kernel(ids, *refs):
    blocks, refs = refs[:16], refs[16:]
    gain, weights, cosine, sine, kv_cos, kv_sin = refs[:6]
    q_keep, q_send, fresh = refs[6:]
    factors = all_factors(blocks)
    total = jnp.zeros((TOKENS, 2 * HD), jnp.float32)
    for i in range(16):
        normed = normed_block(blocks[i], factors, gain[ids[i]])
        total = total + jnp.dot(normed, weights[i], preferred_element_type=jnp.float32)
    q, kv = total[:, :HD], total[:, HD:]
    q = (q * cosine[...] + pltpu.roll(q, HD // 2, 1) * sine[...]).astype(jnp.bfloat16)
    kv = (kv * kv_cos[...] + pltpu.roll(kv, HD // 2, 1) * kv_sin[...]).astype(jnp.bfloat16)
    core_one = ids[0] % 2 == 1
    q_keep[...] = jnp.where(core_one, q[SPAN:], q[:SPAN])
    q_send[...] = jnp.where(core_one, q[:SPAN], q[SPAN:])
    fresh[...] = kv


def project(ids, arrays, gain, weights, tables):
    return pl.pallas_call(
        project_kernel,
        out_shape=[jax.ShapeDtypeStruct((SPAN, HD), jnp.bfloat16)] * 2
        + [jax.ShapeDtypeStruct((TOKENS, HD), jnp.bfloat16)],
        in_specs=[SMEM] + [VMEM] * (len(arrays) + 6),
        out_specs=[VMEM] * 3,
        compiler_params=pltpu.CompilerParams(vmem_limit_bytes=24 * MIB),
        cost_estimate=pl.CostEstimate(
            flops=2 * TOKENS * weights.size, bytes_accessed=12 * MIB, transcendentals=0
        ),
        name="norm_project",
    )(ids, *arrays, gain, weights, *tables)


def share_copies(to, first, weight, weight_other, out, sems):
    count, _, width = out.shape
    copies = []
    for i in range(count):
        columns = pl.ds(pl.multiple_of(to[first + i] * width, width), width)
        pair = [
            pltpu.make_async_copy(part.at[:, columns], out.at[i, pl.ds(j * HD, HD), :], sems.at[j, i])
            for j, part in enumerate((weight, weight_other))
        ]
        for copy in pair:
            copy.start()
        copies.append(pair)
    return copies


def cache_rows(cache, which):
    keep, came, rest = cache[0], cache[1], cache[2:]
    groups = [part[0, c, which] for part in (keep, came) for c in range(2)]
    groups += [part[x, c, which] for part in rest for x in range(2) for c in range(2)]
    return jnp.concatenate(groups, axis=0)


CONTRACT = (((1,), (1,)), ((), ()))


def scores_kernel(info, to, q, q_other, *refs):
    cache, weight, weight_other, scores, weights, sems = refs[:5], *refs[5:]
    copies = share_copies(to, 0, weight, weight_other, weights, sems)
    core, rank = info[SEQS], info[SEQS + 1]
    queries = jnp.concatenate([q[...], q_other[...]], axis=0)
    old = lax.dot_general(
        queries, cache_rows(cache, 0), CONTRACT, preferred_element_type=jnp.float32
    )
    lane = lax.broadcasted_iota(jnp.int32, old.shape, 1)
    position = (rank ^ (lane // CTX_DEV)) * CTX_DEV + lane % CTX_DEV
    scores[...] = jnp.where(position < info[core], old * HD ** (-0.5), -1e30)
    for pair in copies:
        for copy in pair:
            copy.wait()


def cache_scores(info, to, q, q_other, cache, weight, weight_other, ahead):
    width = weight.shape[1] // 16
    return pl.pallas_call(
        scores_kernel,
        out_shape=[
            jax.ShapeDtypeStruct((TOKENS, 16 * CTX_DEV), jnp.float32),
            jax.ShapeDtypeStruct((ahead, 2 * HD, width), jnp.bfloat16),
        ],
        in_specs=[SMEM] * 2 + [VMEM] * 7 + [HBM] * 2,
        out_specs=[VMEM] * 2,
        scratch_shapes=[pltpu.SemaphoreType.DMA((2, ahead))],
        compiler_params=pltpu.CompilerParams(vmem_limit_bytes=16 * MIB),
        cost_estimate=pl.CostEstimate(
            flops=32 * MIB, bytes_accessed=3 * MIB, transcendentals=0
        ),
        name="cache_scores",
    )(info, to, q, q_other, *cache, in_hbm(weight), weight_other)


def attend_kernel(info, q, q_other, fresh_own, fresh_other, scores, *refs):
    cache, out = refs[:5], refs[5]
    core = info[SEQS]
    came = fresh_other[...]
    fresh_keys = jnp.where(core == 0, fresh_own[:SPAN, :], came)
    fresh_values = jnp.where(core == 0, came, fresh_own[SPAN:, :])
    queries = jnp.concatenate([q[...], q_other[...]], axis=0)
    old = scores[...]
    valid = old > -1e29
    fresh = lax.dot_general(
        queries, fresh_keys, CONTRACT, preferred_element_type=jnp.float32
    ) * HD ** (-0.5)
    place = lax.broadcasted_iota(jnp.int32, fresh.shape, 0) % SPAN
    causal = place >= lax.broadcasted_iota(jnp.int32, fresh.shape, 1)
    fresh = jnp.where(causal, fresh, -1e30)
    most = jnp.maximum(jnp.max(old, axis=1, keepdims=True), jnp.max(fresh, axis=1, keepdims=True))
    old_weights = jnp.where(valid, jnp.exp(old - most), 0.0)
    fresh_weights = jnp.where(causal, jnp.exp(fresh - most), 0.0)
    totals = jnp.sum(old_weights, axis=1, keepdims=True) + jnp.sum(
        fresh_weights, axis=1, keepdims=True
    )
    summed = jnp.dot(
        old_weights.astype(jnp.bfloat16), cache_rows(cache, 1), preferred_element_type=jnp.float32
    ) + jnp.dot(
        fresh_weights.astype(jnp.bfloat16), fresh_values, preferred_element_type=jnp.float32
    )
    attn = (summed / totals).astype(jnp.bfloat16)
    out[:, :HD] = attn[:SPAN]
    out[:, HD:] = attn[SPAN:]


def attend(info, q, q_other, fresh_own, fresh_other, scores, cache):
    return pl.pallas_call(
        attend_kernel,
        out_shape=jax.ShapeDtypeStruct((SPAN, 2 * HD), jnp.bfloat16),
        in_specs=[SMEM] + [VMEM] * 10,
        out_specs=VMEM,
        compiler_params=pltpu.CompilerParams(vmem_limit_bytes=16 * MIB),
        cost_estimate=pl.CostEstimate(
            flops=48 * MIB, bytes_accessed=2 * MIB, transcendentals=TOKENS * 1088
        ),
        name="attend",
    )(info, q, q_other, fresh_own, fresh_other, scores, *cache)


def both_heads(core, attn, attn_other):
    mine = attn[...]
    theirs = jnp.concatenate([attn_other[:, HD:], attn_other[:, :HD]], axis=1)
    core_one = core[0] == 1
    return jnp.concatenate(
        [jnp.where(core_one, theirs, mine), jnp.where(core_one, mine, theirs)], axis=0
    )


def first_shares_kernel(core, attn, attn_other, weights, *outs):
    rows = both_heads(core, attn, attn_other)
    for i, out in enumerate(outs):
        out[...] = jnp.dot(rows, weights[i], preferred_element_type=jnp.float32).astype(out.dtype)


def first_shares(shares, core, attn, attn_other, weights):
    count, _, width = weights.shape
    out_shape = [jax.ShapeDtypeStruct((TOKENS, width), jnp.bfloat16)] * count
    arrays = pl.pallas_call(
        first_shares_kernel,
        out_shape=out_shape,
        in_specs=[SMEM] + [VMEM] * 3,
        out_specs=[VMEM] * len(out_shape),
        compiler_params=pltpu.CompilerParams(vmem_limit_bytes=16 * MIB),
        cost_estimate=pl.CostEstimate(
            flops=2 * TOKENS * weights.size, bytes_accessed=count * MIB, transcendentals=0
        ),
        name="first_shares",
    )(core, attn, attn_other, weights)
    return dict(zip(shares, arrays))


def more_shares_kernel(first, core, to, attn, attn_other, weight, weight_other, *refs):
    outs, (weights, sems) = refs[:-2], refs[-2:]
    copies = share_copies(to, first, weight, weight_other, weights, sems)
    rows = both_heads(core, attn, attn_other)
    for i, out in enumerate(outs):
        for copy in copies[i]:
            copy.wait()
        out[...] = jnp.dot(rows, weights[i], preferred_element_type=jnp.float32)


def more_shares(core, to, attn, attn_other, weight, weight_other, first, last):
    count, width = last - first, weight.shape[1] // 16
    out_shape = [jax.ShapeDtypeStruct((TOKENS, width), jnp.float32)] * count
    arrays = pl.pallas_call(
        functools.partial(more_shares_kernel, first),
        out_shape=out_shape,
        in_specs=[SMEM] * 2 + [VMEM] * 2 + [HBM] * 2,
        out_specs=[VMEM] * len(out_shape),
        scratch_shapes=[
            pltpu.VMEM((count, 2 * HD, width), jnp.bfloat16),
            pltpu.SemaphoreType.DMA((2, count)),
        ],
        compiler_params=pltpu.CompilerParams(vmem_limit_bytes=16 * MIB),
        cost_estimate=pl.CostEstimate(
            flops=4 * TOKENS * HD * width * count,
            bytes_accessed=count * MIB,
            transcendentals=0,
        ),
        name="shares_%d" % first,
    )(core, to, attn, attn_other, in_hbm(weight), weight_other)
    return dict(zip(SHARES[first:last], arrays))


def final_kernel(ids, *refs):
    blocks, refs = refs[:16], refs[16:]
    gain, out, staged, sems = refs
    width = staged.shape[2]
    factors = all_factors(blocks)
    copies = []
    for i in range(16):
        staged[i] = normed_block(blocks[i], factors, gain[ids[i]])
        copy = pltpu.make_async_copy(
            staged.at[i],
            out.at[:, pl.ds(pl.multiple_of(ids[i] * width, width), width)],
            sems.at[i],
        )
        copy.start()
        copies.append(copy)
    for copy in copies:
        copy.wait()


def final_norm(ids, arrays, gain):
    width = arrays[0].shape[1]
    return pl.pallas_call(
        final_kernel,
        out_shape=jax.ShapeDtypeStruct((TOKENS, 16 * width), jnp.bfloat16),
        in_specs=[SMEM] + [VMEM] * (len(arrays) + 1),
        out_specs=HBM,
        scratch_shapes=[
            pltpu.VMEM((16, TOKENS, width), jnp.bfloat16),
            pltpu.SemaphoreType.DMA((16,)),
        ],
        compiler_params=pltpu.CompilerParams(vmem_limit_bytes=24 * MIB),
        cost_estimate=pl.CostEstimate(
            flops=16 * MIB, bytes_accessed=12 * MIB, transcendentals=0
        ),
        name="final_norm",
    )(ids, *arrays, gain)


def per_device_ring(
    residual, attn_gain, ffn_gain, q_weight, kv_weight, o_weight, key_cache, value_cache, prefix
):
    rank = lax.axis_index("tp")
    core = rank % 2
    width = residual.shape[1]
    ids = gathered_ids(rank)
    to = share_ids(rank)
    core_id, rank_id = core[None].astype(jnp.int32), rank[None].astype(jnp.int32)
    info = jnp.concatenate([prefix, core_id, rank_id])

    weight_other = send(o_weight, SWAP)
    parts = split_cache(key_cache, value_cache, rank, rank_id)
    weights = load_weights(ids, q_weight, kv_weight, width)
    mine, theirs = ring_gather(residual, weight_other, direct=True, early=weights)
    cache = move_cache(parts)

    positions = (prefix[:, None] + jnp.arange(SPAN, dtype=jnp.int32)[None, :]).reshape(-1)
    cosine, sine = rope_tables(positions)
    cosine = jnp.concatenate([cosine, cosine], axis=1)
    sine = jnp.concatenate([-sine, sine], axis=1)
    holds_keys = rank < KVH
    tables = (cosine, sine, jnp.where(holds_keys, cosine, 1.0), jnp.where(holds_keys, sine, 0.0))

    gain = attn_gain.reshape(16, 1, width).astype(jnp.float32)
    mine[0] = after(mine[0], cache[1])
    q_keep, q_send, fresh = project(ids, mine + theirs, gain, weights, tables)
    q_other = send(q_send, SWAP)
    fresh_own = send(fresh, FRESH)
    fresh_other = send(jnp.where(core == 0, fresh_own[SPAN:], fresh_own[:SPAN]), SWAP)
    scores, first_weights = cache_scores(
        info, to, q_keep, q_other, cache, o_weight, weight_other, 2
    )
    attn = attend(info, q_keep, q_other, fresh_own, fresh_other, scores, cache)
    attn_other = send(attn, SWAP)

    shares = first_shares(SHARES[:2], core_id, attn, attn_other, first_weights)
    inputs = (attn, attn_other, o_weight, weight_other)
    for first, last in ((2, 4), (4, len(SHARES))):
        shares.update(more_shares(core_id, to, *inputs, first, last))
    one_way, other_way = ring_sum(shares)
    projected = shares[0, 0] + one_way.astype(jnp.float32) + other_way.astype(jnp.float32)
    hidden = (residual.astype(jnp.float32) + projected).astype(jnp.bfloat16)

    mine, theirs = ring_gather(hidden)
    gain = ffn_gain.reshape(16, 1, width).astype(jnp.float32)
    return final_norm(ids, mine + theirs, gain)


def per_device(
    residual, attn_gain, ffn_gain, q_weight, kv_weight, o_weight, key_cache, value_cache, prefix
):
    tp_count = lax.axis_size("tp")
    tp_rank = lax.axis_index("tp")
    heads_all = HQ_DEV * tp_count
    group_size = heads_all // KVH
    token_count = SEQS * SPAN
    score_scale = HD ** (-0.5)
    whole_rows = lax.all_gather(residual, "tp", axis=1, tiled=True)
    normed = rms_rows(whole_rows, attn_gain).astype(jnp.bfloat16)
    positions = (prefix[:, None] + jnp.arange(SPAN, dtype=jnp.int32)[None, :]).reshape(-1)
    queries = jnp.dot(normed, q_weight, preferred_element_type=jnp.float32).reshape(
        token_count, HQ_DEV, HD
    )
    queries = rotate(queries, positions).astype(jnp.bfloat16)
    kv_part = jnp.dot(normed, kv_weight, preferred_element_type=jnp.float32)
    kv_whole = lax.all_gather(kv_part, "tp", axis=1, tiled=True)
    new_keys = rotate(kv_whole[:, : KVH * HD].reshape(token_count, KVH, HD), positions).astype(
        jnp.bfloat16
    )
    new_values = kv_whole[:, KVH * HD :].reshape(token_count, KVH, HD).astype(jnp.bfloat16)
    head_ids = tp_rank * HQ_DEV + jnp.arange(HQ_DEV, dtype=jnp.int32)
    own_kv = head_ids // group_size
    own_keys = jnp.take(new_keys, own_kv, axis=1).reshape(SEQS, SPAN, HQ_DEV, HD)
    own_values = jnp.take(new_values, own_kv, axis=1).reshape(SEQS, SPAN, HQ_DEV, HD)
    own_queries = queries.reshape(SEQS, SPAN, HQ_DEV, HD)
    causal = (jnp.arange(SPAN)[:, None] >= jnp.arange(SPAN)[None, :])[None, None]
    fresh_scores = (
        jnp.einsum("schd,skhd->shck", own_queries, own_keys, preferred_element_type=jnp.float32)
        * score_scale
    )
    fresh_scores = jnp.where(causal, fresh_scores, -1e30)
    fresh_max = fresh_scores.max(-1)
    gathered = lax.all_gather(queries.reshape(token_count, HQ_DEV * HD), "tp", axis=1, tiled=True)
    queries_all = gathered.reshape(SEQS, SPAN, KVH, group_size, HD)
    keys_local = key_cache.reshape(SEQS, CTX_DEV, KVH, HD)
    values_local = value_cache.reshape(SEQS, CTX_DEV, KVH, HD)
    local_scores = (
        jnp.einsum("sckgd,sjkd->skgcj", queries_all, keys_local, preferred_element_type=jnp.float32)
        * score_scale
    )
    first_slot = tp_rank * CTX_DEV
    is_valid = ((first_slot + jnp.arange(CTX_DEV, dtype=jnp.int32))[None, :] < prefix[:, None])[
        :, None, None, None, :
    ]
    local_scores = jnp.where(is_valid, local_scores, -1e30)
    local_max = local_scores.max(-1)
    local_weights = jnp.where(is_valid, jnp.exp(local_scores - local_max[..., None]), 0.0)
    local_total = local_weights.sum(-1)
    local_sum = jnp.einsum(
        "skgcj,sjkd->skgcd",
        local_weights.astype(jnp.bfloat16),
        values_local,
        preferred_element_type=jnp.float32,
    )
    sums_in, maxes_in, totals_in = (
        lax.all_to_all(
            local_sum.reshape(1, SEQS, heads_all, SPAN, HD),
            "tp",
            split_axis=2,
            concat_axis=0,
            tiled=True,
        ),
        lax.all_to_all(
            local_max.reshape(1, SEQS, heads_all, SPAN),
            "tp",
            split_axis=2,
            concat_axis=0,
            tiled=True,
        ),
        lax.all_to_all(
            local_total.reshape(1, SEQS, heads_all, SPAN),
            "tp",
            split_axis=2,
            concat_axis=0,
            tiled=True,
        ),
    )
    running_max = jnp.maximum(maxes_in.max(0), fresh_max)
    factors = jnp.exp(maxes_in - running_max[None])
    fresh_weights = jnp.where(causal, jnp.exp(fresh_scores - running_max[..., None]), 0.0)
    totals = (factors * totals_in).sum(0) + fresh_weights.sum(-1)
    summed = (factors[..., None] * sums_in).sum(0)
    summed = summed + jnp.einsum(
        "shck,skhd->shcd",
        fresh_weights.astype(jnp.bfloat16),
        own_values,
        preferred_element_type=jnp.float32,
    )
    attn = (summed / totals[..., None]).astype(jnp.bfloat16)
    attn = jnp.transpose(attn, (0, 2, 1, 3)).reshape(token_count, HQ_DEV * HD)
    share_part = lax.psum_scatter(
        lax.dot_general(
            o_weight, attn, (((0,), (1,)), ((), ())), preferred_element_type=jnp.float32
        ),
        "tp",
        scatter_dimension=0,
        tiled=True,
    )
    hidden = (residual.astype(jnp.float32) + share_part.T).astype(jnp.bfloat16)
    stream = lax.all_gather(hidden, "tp", axis=1, tiled=True)
    return rms_rows(stream, ffn_gain).astype(jnp.bfloat16)


def solution(mesh):
    return jax.shard_map(
        per_device_ring if mesh.shape["tp"] == 2 * CHIPS else per_device,
        mesh=mesh,
        in_specs=(
            P("replica", "tp"),
            P(),
            P(),
            P(None, "tp"),
            P(None, "tp"),
            P("tp", None),
            P("replica", "tp", None),
            P("replica", "tp", None),
            P("replica"),
        ),
        out_specs=P("replica", None),
        check_vma=False,
    )
```

```python
import functools

import jax
import jax.numpy as jnp
from jax import lax
from jax.experimental import pallas as pl
from jax.experimental.pallas import tpu as pltpu
from jax.sharding import PartitionSpec as P

HD = 128
KVH = 8
HQ_DEV = 1
SPAN = 64
SEQS = 2
CTX_DEV = 64
TOKENS = SEQS * SPAN
MIB = 1024 * 1024

epsilon = 1e-05


def rms_rows(rows, gain):
    values_f = rows.astype(jnp.float32)
    factor = lax.rsqrt(jnp.mean(values_f * values_f, axis=-1, keepdims=True) + epsilon)
    return values_f * factor * gain.astype(jnp.float32)


def rope_tables(positions):
    half_width = HD // 2
    frequency = 500000.0 ** (-jnp.arange(half_width, dtype=jnp.float32) / half_width)
    angles = positions.astype(jnp.float32)[:, None] * frequency[None, :]
    return jnp.cos(angles), jnp.sin(angles)


def rotate(vectors, positions):
    half_width = vectors.shape[-1] // 2
    cosine, sine = rope_tables(positions)
    cosine, sine = cosine[:, None, :], sine[:, None, :]
    first_half = vectors[..., :half_width]
    second_half = vectors[..., half_width:]
    return jnp.concatenate(
        [first_half * cosine - second_half * sine, second_half * cosine + first_half * sine],
        axis=-1,
    )


CHIPS = 8
RING = (0, 2, 4, 6, 7, 5, 3, 1)
ONWARD = [(2 * RING[i], 2 * RING[(i + 1) % CHIPS]) for i in range(CHIPS)] + [
    (2 * RING[i] + 1, 2 * RING[i - 1] + 1) for i in range(CHIPS)
]
ENTER = [(2 * RING[i], 2 * RING[i - 1] + 1) for i in range(CHIPS)] + [
    (2 * RING[i] + 1, 2 * RING[(i + 1) % CHIPS]) for i in range(CHIPS)
]
LEAVE = [(2 * RING[i], 2 * RING[(i + 1) % CHIPS] + 1) for i in range(CHIPS)] + [
    (2 * RING[i] + 1, 2 * RING[i - 1]) for i in range(CHIPS)
]
SWAP = [(t, t ^ 1) for t in range(2 * CHIPS)]
FRESH = [(k, 2 * k) for k in range(KVH)] + [(KVH + k, 2 * k + 1) for k in range(KVH)]
VMEM = pl.BlockSpec(memory_space=pltpu.VMEM)
SMEM = pl.BlockSpec(memory_space=pltpu.SMEM)
HBM = pl.BlockSpec(memory_space=pltpu.HBM)


def ring_place(rank):
    chip = rank // 2
    return jnp.where(chip % 2 == 0, chip // 2, CHIPS - 1 - chip // 2)


def chip_at(place):
    place = place % CHIPS
    return jnp.where(place < CHIPS // 2, 2 * place, 2 * CHIPS - 1 - 2 * place)


def send(array, pairs):
    return lax.ppermute(array, "tp", pairs)


def xor(bits):
    return [(t, t ^ bits) for t in range(2 * CHIPS)]


def after(array, *others):
    return lax.optimization_barrier((array, others))[0]


def ring_gather(own, ready=None, direct=False, early=None):
    straight, swapped = own, None if direct else send(own, SWAP)
    crossed = own if direct else swapped
    mine = [own]
    for step in range(1, 5):
        if step == 2 and early is not None:
            straight = after(straight, early)
        if step == 4 and ready is not None:
            straight = after(straight, ready)
        straight = send(straight, ONWARD)
        mine.append(straight)
        if step < 4:
            crossed = send(crossed, ENTER if direct and step == 1 else ONWARD)
            mine.append(crossed)
    theirs = [send(own, SWAP) if direct else swapped]
    return mine, theirs + [send(block, SWAP) for block in mine[1:]]


def gathered_ids(rank):
    place = ring_place(rank)
    ids = []
    for side in range(2):
        device = rank ^ side
        core = device % 2
        ids.append(device)
        for step in range(1, 5):
            chip = 2 * chip_at(place + (2 * core - 1) * step)
            ids += [chip + core, chip + 1 - core] if step < 4 else [chip + core]
    return jnp.stack(ids).astype(jnp.int32)


SHARES = ((4, 0), (3, 1), (3, 0), (2, 1), (2, 0), (1, 1), (1, 0), (0, 0))


def share_ids(rank):
    place, core = ring_place(rank), rank % 2
    return jnp.stack(
        [2 * chip_at(place + (1 - 2 * core) * d) + (core + other) % 2 for d, other in SHARES]
    ).astype(jnp.int32)


def ring_sum(shares):
    straight, crossed = shares[4, 0], shares[3, 1]
    for step in range(1, 5):
        straight = send(straight, ONWARD)
        if step < 4:
            crossed = send(crossed, LEAVE if step == 3 else ONWARD)
            straight = add_share(straight, shares[4 - step, 0])
        if step < 3:
            crossed = add_share(crossed, shares[3 - step, 1])
    return straight, crossed


def add_share(part, share):
    return (part.astype(jnp.float32) + share).astype(jnp.bfloat16)


def split_cache(key_cache, value_cache, rank, rank_id):
    core = rank % 2
    give = jnp.stack(
        [lax.dynamic_index_in_dim(c, 1 - core, 0, keepdims=False) for c in (key_cache, value_cache)]
    )
    return pack(rank_id, key_cache, value_cache, send(give, SWAP))


def move_cache(parts, *when):
    keep, give = parts
    came = send(give, xor(2))
    pieces = [jnp.stack([keep[m], came[m]]) for m in range(1, 4)]
    return [keep, came] + [send(piece, xor(4 * m)) for m, piece in zip(range(1, 4), pieces)]


def pack_kernel(rank, keys, values, theirs, keep, give, sems):
    me = rank[0]
    copies = []
    for m in range(4):
        for j, out in enumerate((keep, give)):
            chip = (me ^ (4 * m + 2 * j)) // 2
            head = pl.ds(pl.multiple_of(chip * HD, HD), HD)
            for k, cache in enumerate((keys, values)):
                copies.append(
                    pltpu.make_async_copy(
                        cache.at[me % 2, :, head], out.at[m, 0, k], sems.at[m, j, k]
                    )
                )
                copies[-1].start()
            out[m, 1, 0] = theirs[0, :, head]
            out[m, 1, 1] = theirs[1, :, head]
    for copy in copies:
        copy.wait()


def pack(rank_id, key_cache, value_cache, theirs):
    return pl.pallas_call(
        pack_kernel,
        out_shape=[jax.ShapeDtypeStruct((4, 2, 2, CTX_DEV, HD), jnp.bfloat16)] * 2,
        in_specs=[SMEM] + [HBM] * 2 + [VMEM],
        out_specs=[VMEM] * 2,
        scratch_shapes=[pltpu.SemaphoreType.DMA((4, 2, 2))],
        compiler_params=pltpu.CompilerParams(vmem_limit_bytes=8 * MIB),
        cost_estimate=pl.CostEstimate(flops=0, bytes_accessed=MIB, transcendentals=0),
        name="pack_cache",
    )(rank_id, in_hbm(key_cache), in_hbm(value_cache), theirs)


def lanes(block, j):
    return block[:, 128 * j : 128 * j + 128].astype(jnp.float32)


def square_sums(blocks, total):
    for block in blocks:
        for j in range(block.shape[1] // 128):
            v = lanes(block, j)
            total = total + v * v
    return total


def row_factors(squares, features):
    mean = jnp.sum(squares, axis=1, keepdims=True) * (1.0 / features)
    return lax.rsqrt(mean + epsilon)


def normed_block(block, factors, gain_row):
    return jnp.concatenate(
        [
            (lanes(block, j) * factors * gain_row[:, 128 * j : 128 * j + 128]).astype(jnp.bfloat16)
            for j in range(block.shape[1] // 128)
        ],
        axis=1,
    )


def in_hbm(array):
    return pltpu.with_memory_space_constraint(array, pltpu.HBM)


def load_kernel(ids, wq, wkv, out, sems):
    count, width, _ = out.shape
    copies = []
    for i in range(count):
        rows = pl.ds(pl.multiple_of(ids[i] * width, width), width)
        for j, weight in enumerate((wq, wkv)):
            copies.append(
                pltpu.make_async_copy(
                    weight.at[rows, :], out.at[i, :, pl.ds(j * HD, HD)], sems.at[j, i]
                )
            )
            copies[-1].start()
    for copy in copies:
        copy.wait()


def load_weights(ids, wq, wkv, width):
    return pl.pallas_call(
        load_kernel,
        out_shape=pltpu.VMEM((16, width, 2 * HD), jnp.bfloat16),
        in_specs=[SMEM] + [HBM] * 2,
        out_specs=VMEM,
        scratch_shapes=[pltpu.SemaphoreType.DMA((2, 16))],
        compiler_params=pltpu.CompilerParams(vmem_limit_bytes=16 * MIB),
        cost_estimate=pl.CostEstimate(flops=0, bytes_accessed=16 * MIB, transcendentals=0),
        name="load_weights",
    )(ids, in_hbm(wq), in_hbm(wkv))


def all_factors(blocks):
    total = square_sums(blocks, jnp.zeros((TOKENS, 128), jnp.float32))
    return row_factors(total, 16 * blocks[0].shape[1])


def project_kernel(ids, *refs):
    blocks, refs = refs[:16], refs[16:]
    gain, weights, cosine, sine, kv_cos, kv_sin = refs[:6]
    q_keep, q_send, fresh = refs[6:]
    factors = all_factors(blocks)
    total = jnp.zeros((TOKENS, 2 * HD), jnp.float32)
    for i in range(16):
        normed = normed_block(blocks[i], factors, gain[ids[i]])
        total = total + jnp.dot(normed, weights[i], preferred_element_type=jnp.float32)
    q, kv = total[:, :HD], total[:, HD:]
    q = (q * cosine[...] + pltpu.roll(q, HD // 2, 1) * sine[...]).astype(jnp.bfloat16)
    kv = (kv * kv_cos[...] + pltpu.roll(kv, HD // 2, 1) * kv_sin[...]).astype(jnp.bfloat16)
    core_one = ids[0] % 2 == 1
    q_keep[...] = jnp.where(core_one, q[SPAN:], q[:SPAN])
    q_send[...] = jnp.where(core_one, q[:SPAN], q[SPAN:])
    fresh[...] = kv


def project(ids, arrays, gain, weights, tables):
    return pl.pallas_call(
        project_kernel,
        out_shape=[jax.ShapeDtypeStruct((SPAN, HD), jnp.bfloat16)] * 2
        + [jax.ShapeDtypeStruct((TOKENS, HD), jnp.bfloat16)],
        in_specs=[SMEM] + [VMEM] * (len(arrays) + 6),
        out_specs=[VMEM] * 3,
        compiler_params=pltpu.CompilerParams(vmem_limit_bytes=24 * MIB),
        cost_estimate=pl.CostEstimate(
            flops=2 * TOKENS * weights.size, bytes_accessed=12 * MIB, transcendentals=0
        ),
        name="norm_project",
    )(ids, *arrays, gain, pltpu.with_memory_space_constraint(weights, pltpu.VMEM), *tables)


def share_copies(to, first, weight, weight_other, out, sems):
    count, _, width = out.shape
    copies = []
    for i in range(count):
        columns = pl.ds(pl.multiple_of(to[first + i] * width, width), width)
        pair = [
            pltpu.make_async_copy(part.at[:, columns], out.at[i, pl.ds(j * HD, HD), :], sems.at[j, i])
            for j, part in enumerate((weight, weight_other))
        ]
        for copy in pair:
            copy.start()
        copies.append(pair)
    return copies


def cache_rows(cache, which):
    keep, came, rest = cache[0], cache[1], cache[2:]
    groups = [part[0, c, which] for part in (keep, came) for c in range(2)]
    groups += [part[x, c, which] for part in rest for x in range(2) for c in range(2)]
    return jnp.concatenate(groups, axis=0)


CONTRACT = (((1,), (1,)), ((), ()))


def scores_kernel(info, to, q, q_other, *refs):
    cache, weight, weight_other, scores, weights, sems = refs[:5], *refs[5:]
    copies = share_copies(to, 0, weight, weight_other, weights, sems)
    core, rank = info[SEQS], info[SEQS + 1]
    queries = jnp.concatenate([q[...], q_other[...]], axis=0)
    old = lax.dot_general(
        queries, cache_rows(cache, 0), CONTRACT, preferred_element_type=jnp.float32
    )
    lane = lax.broadcasted_iota(jnp.int32, old.shape, 1)
    position = (rank ^ (lane // CTX_DEV)) * CTX_DEV + lane % CTX_DEV
    scores[...] = jnp.where(position < info[core], old * HD ** (-0.5), -1e30)
    for pair in copies:
        for copy in pair:
            copy.wait()


def cache_scores(info, to, q, q_other, cache, weight, weight_other, ahead):
    width = weight.shape[1] // 16
    return pl.pallas_call(
        scores_kernel,
        out_shape=[
            jax.ShapeDtypeStruct((TOKENS, 16 * CTX_DEV), jnp.float32),
            jax.ShapeDtypeStruct((ahead, 2 * HD, width), jnp.bfloat16),
        ],
        in_specs=[SMEM] * 2 + [VMEM] * 7 + [HBM] * 2,
        out_specs=[VMEM] * 2,
        scratch_shapes=[pltpu.SemaphoreType.DMA((2, ahead))],
        compiler_params=pltpu.CompilerParams(vmem_limit_bytes=16 * MIB),
        cost_estimate=pl.CostEstimate(
            flops=32 * MIB, bytes_accessed=3 * MIB, transcendentals=0
        ),
        name="cache_scores",
    )(info, to, q, q_other, *cache, in_hbm(weight), weight_other)


def attend_kernel(info, q, q_other, fresh_own, fresh_other, scores, *refs):
    cache, out = refs[:5], refs[5]
    core = info[SEQS]
    came = fresh_other[...]
    fresh_keys = jnp.where(core == 0, fresh_own[:SPAN, :], came)
    fresh_values = jnp.where(core == 0, came, fresh_own[SPAN:, :])
    queries = jnp.concatenate([q[...], q_other[...]], axis=0)
    old = scores[...]
    valid = old > -1e29
    fresh = lax.dot_general(
        queries, fresh_keys, CONTRACT, preferred_element_type=jnp.float32
    ) * HD ** (-0.5)
    place = lax.broadcasted_iota(jnp.int32, fresh.shape, 0) % SPAN
    causal = place >= lax.broadcasted_iota(jnp.int32, fresh.shape, 1)
    fresh = jnp.where(causal, fresh, -1e30)
    most = jnp.maximum(jnp.max(old, axis=1, keepdims=True), jnp.max(fresh, axis=1, keepdims=True))
    old_weights = jnp.where(valid, jnp.exp(old - most), 0.0)
    fresh_weights = jnp.where(causal, jnp.exp(fresh - most), 0.0)
    totals = jnp.sum(old_weights, axis=1, keepdims=True) + jnp.sum(
        fresh_weights, axis=1, keepdims=True
    )
    summed = jnp.dot(
        old_weights.astype(jnp.bfloat16), cache_rows(cache, 1), preferred_element_type=jnp.float32
    ) + jnp.dot(
        fresh_weights.astype(jnp.bfloat16), fresh_values, preferred_element_type=jnp.float32
    )
    attn = (summed / totals).astype(jnp.bfloat16)
    out[:, :HD] = attn[:SPAN]
    out[:, HD:] = attn[SPAN:]


def attend(info, q, q_other, fresh_own, fresh_other, scores, cache):
    return pl.pallas_call(
        attend_kernel,
        out_shape=jax.ShapeDtypeStruct((SPAN, 2 * HD), jnp.bfloat16),
        in_specs=[SMEM] + [VMEM] * 10,
        out_specs=VMEM,
        compiler_params=pltpu.CompilerParams(vmem_limit_bytes=16 * MIB),
        cost_estimate=pl.CostEstimate(
            flops=48 * MIB, bytes_accessed=2 * MIB, transcendentals=TOKENS * 1088
        ),
        name="attend",
    )(info, q, q_other, fresh_own, fresh_other, scores, *cache)


def both_heads(core, attn, attn_other):
    mine = attn[...]
    theirs = jnp.concatenate([attn_other[:, HD:], attn_other[:, :HD]], axis=1)
    core_one = core[0] == 1
    return jnp.concatenate(
        [jnp.where(core_one, theirs, mine), jnp.where(core_one, mine, theirs)], axis=0
    )


def first_shares_kernel(core, attn, attn_other, weights, *outs):
    rows = both_heads(core, attn, attn_other)
    for i, out in enumerate(outs):
        out[...] = jnp.dot(rows, weights[i], preferred_element_type=jnp.float32).astype(out.dtype)


def first_shares(shares, core, attn, attn_other, weights):
    count, _, width = weights.shape
    out_shape = [jax.ShapeDtypeStruct((TOKENS, width), jnp.bfloat16)] * count
    arrays = pl.pallas_call(
        first_shares_kernel,
        out_shape=out_shape,
        in_specs=[SMEM] + [VMEM] * 3,
        out_specs=[VMEM] * len(out_shape),
        compiler_params=pltpu.CompilerParams(vmem_limit_bytes=16 * MIB),
        cost_estimate=pl.CostEstimate(
            flops=2 * TOKENS * weights.size, bytes_accessed=count * MIB, transcendentals=0
        ),
        name="first_shares",
    )(core, attn, attn_other, weights)
    return dict(zip(shares, arrays))


def more_shares_kernel(first, core, to, attn, attn_other, weight, weight_other, *refs):
    outs, (weights, sems) = refs[:-2], refs[-2:]
    copies = share_copies(to, first, weight, weight_other, weights, sems)
    rows = both_heads(core, attn, attn_other)
    for i, out in enumerate(outs):
        for copy in copies[i]:
            copy.wait()
        out[...] = jnp.dot(rows, weights[i], preferred_element_type=jnp.float32)


def more_shares(core, to, attn, attn_other, weight, weight_other, first, last):
    count, width = last - first, weight.shape[1] // 16
    out_shape = [jax.ShapeDtypeStruct((TOKENS, width), jnp.float32)] * count
    arrays = pl.pallas_call(
        functools.partial(more_shares_kernel, first),
        out_shape=out_shape,
        in_specs=[SMEM] * 2 + [VMEM] * 2 + [HBM] * 2,
        out_specs=[VMEM] * len(out_shape),
        scratch_shapes=[
            pltpu.VMEM((count, 2 * HD, width), jnp.bfloat16),
            pltpu.SemaphoreType.DMA((2, count)),
        ],
        compiler_params=pltpu.CompilerParams(vmem_limit_bytes=16 * MIB),
        cost_estimate=pl.CostEstimate(
            flops=4 * TOKENS * HD * width * count,
            bytes_accessed=count * MIB,
            transcendentals=0,
        ),
        name="shares_%d" % first,
    )(core, to, attn, attn_other, in_hbm(weight), weight_other)
    return dict(zip(SHARES[first:last], arrays))


def final_kernel(ids, *refs):
    blocks, refs = refs[:16], refs[16:]
    gain, out, staged, sems = refs
    width = staged.shape[2]
    factors = all_factors(blocks)
    copies = []
    for i in range(16):
        staged[i] = normed_block(blocks[i], factors, gain[ids[i]])
        copy = pltpu.make_async_copy(
            staged.at[i],
            out.at[:, pl.ds(pl.multiple_of(ids[i] * width, width), width)],
            sems.at[i],
        )
        copy.start()
        copies.append(copy)
    for copy in copies:
        copy.wait()


def final_norm(ids, arrays, gain):
    width = arrays[0].shape[1]
    return pl.pallas_call(
        final_kernel,
        out_shape=jax.ShapeDtypeStruct((TOKENS, 16 * width), jnp.bfloat16),
        in_specs=[SMEM] + [VMEM] * (len(arrays) + 1),
        out_specs=HBM,
        scratch_shapes=[
            pltpu.VMEM((16, TOKENS, width), jnp.bfloat16),
            pltpu.SemaphoreType.DMA((16,)),
        ],
        compiler_params=pltpu.CompilerParams(vmem_limit_bytes=24 * MIB),
        cost_estimate=pl.CostEstimate(
            flops=16 * MIB, bytes_accessed=12 * MIB, transcendentals=0
        ),
        name="final_norm",
    )(ids, *arrays, gain)


def per_device_ring(
    residual, attn_gain, ffn_gain, q_weight, kv_weight, o_weight, key_cache, value_cache, prefix
):
    rank = lax.axis_index("tp")
    core = rank % 2
    width = residual.shape[1]
    ids = gathered_ids(rank)
    to = share_ids(rank)
    core_id, rank_id = core[None].astype(jnp.int32), rank[None].astype(jnp.int32)
    info = jnp.concatenate([prefix, core_id, rank_id])

    weight_other = send(o_weight, SWAP)
    parts = split_cache(key_cache, value_cache, rank, rank_id)
    weights = load_weights(ids, q_weight, kv_weight, width)
    mine, theirs = ring_gather(residual, weight_other, direct=True, early=weights)
    cache = move_cache(parts)

    positions = (prefix[:, None] + jnp.arange(SPAN, dtype=jnp.int32)[None, :]).reshape(-1)
    cosine, sine = rope_tables(positions)
    cosine = jnp.concatenate([cosine, cosine], axis=1)
    sine = jnp.concatenate([-sine, sine], axis=1)
    holds_keys = rank < KVH
    tables = (cosine, sine, jnp.where(holds_keys, cosine, 1.0), jnp.where(holds_keys, sine, 0.0))

    gain = attn_gain.reshape(16, 1, width).astype(jnp.float32)
    mine[0] = after(mine[0], cache[1])
    q_keep, q_send, fresh = project(ids, mine + theirs, gain, weights, tables)
    q_other = send(q_send, SWAP)
    fresh_own = send(fresh, FRESH)
    fresh_other = send(jnp.where(core == 0, fresh_own[SPAN:], fresh_own[:SPAN]), SWAP)
    scores, first_weights = cache_scores(
        info, to, q_keep, q_other, cache, o_weight, weight_other, 2
    )
    attn = attend(info, q_keep, q_other, fresh_own, fresh_other, scores, cache)
    attn_other = send(attn, SWAP)

    shares = first_shares(SHARES[:2], core_id, attn, attn_other, first_weights)
    inputs = (attn, attn_other, o_weight, weight_other)
    for first, last in ((2, 4), (4, len(SHARES))):
        shares.update(more_shares(core_id, to, *inputs, first, last))
    one_way, other_way = ring_sum(shares)
    projected = shares[0, 0] + one_way.astype(jnp.float32) + other_way.astype(jnp.float32)
    hidden = (residual.astype(jnp.float32) + projected).astype(jnp.bfloat16)

    mine, theirs = ring_gather(hidden)
    gain = ffn_gain.reshape(16, 1, width).astype(jnp.float32)
    return final_norm(ids, mine + theirs, gain)


def per_device(
    residual, attn_gain, ffn_gain, q_weight, kv_weight, o_weight, key_cache, value_cache, prefix
):
    tp_count = lax.axis_size("tp")
    tp_rank = lax.axis_index("tp")
    heads_all = HQ_DEV * tp_count
    group_size = heads_all // KVH
    token_count = SEQS * SPAN
    score_scale = HD ** (-0.5)
    whole_rows = lax.all_gather(residual, "tp", axis=1, tiled=True)
    normed = rms_rows(whole_rows, attn_gain).astype(jnp.bfloat16)
    positions = (prefix[:, None] + jnp.arange(SPAN, dtype=jnp.int32)[None, :]).reshape(-1)
    queries = jnp.dot(normed, q_weight, preferred_element_type=jnp.float32).reshape(
        token_count, HQ_DEV, HD
    )
    queries = rotate(queries, positions).astype(jnp.bfloat16)
    kv_part = jnp.dot(normed, kv_weight, preferred_element_type=jnp.float32)
    kv_whole = lax.all_gather(kv_part, "tp", axis=1, tiled=True)
    new_keys = rotate(kv_whole[:, : KVH * HD].reshape(token_count, KVH, HD), positions).astype(
        jnp.bfloat16
    )
    new_values = kv_whole[:, KVH * HD :].reshape(token_count, KVH, HD).astype(jnp.bfloat16)
    head_ids = tp_rank * HQ_DEV + jnp.arange(HQ_DEV, dtype=jnp.int32)
    own_kv = head_ids // group_size
    own_keys = jnp.take(new_keys, own_kv, axis=1).reshape(SEQS, SPAN, HQ_DEV, HD)
    own_values = jnp.take(new_values, own_kv, axis=1).reshape(SEQS, SPAN, HQ_DEV, HD)
    own_queries = queries.reshape(SEQS, SPAN, HQ_DEV, HD)
    causal = (jnp.arange(SPAN)[:, None] >= jnp.arange(SPAN)[None, :])[None, None]
    fresh_scores = (
        jnp.einsum("schd,skhd->shck", own_queries, own_keys, preferred_element_type=jnp.float32)
        * score_scale
    )
    fresh_scores = jnp.where(causal, fresh_scores, -1e30)
    fresh_max = fresh_scores.max(-1)
    gathered = lax.all_gather(queries.reshape(token_count, HQ_DEV * HD), "tp", axis=1, tiled=True)
    queries_all = gathered.reshape(SEQS, SPAN, KVH, group_size, HD)
    keys_local = key_cache.reshape(SEQS, CTX_DEV, KVH, HD)
    values_local = value_cache.reshape(SEQS, CTX_DEV, KVH, HD)
    local_scores = (
        jnp.einsum("sckgd,sjkd->skgcj", queries_all, keys_local, preferred_element_type=jnp.float32)
        * score_scale
    )
    first_slot = tp_rank * CTX_DEV
    is_valid = ((first_slot + jnp.arange(CTX_DEV, dtype=jnp.int32))[None, :] < prefix[:, None])[
        :, None, None, None, :
    ]
    local_scores = jnp.where(is_valid, local_scores, -1e30)
    local_max = local_scores.max(-1)
    local_weights = jnp.where(is_valid, jnp.exp(local_scores - local_max[..., None]), 0.0)
    local_total = local_weights.sum(-1)
    local_sum = jnp.einsum(
        "skgcj,sjkd->skgcd",
        local_weights.astype(jnp.bfloat16),
        values_local,
        preferred_element_type=jnp.float32,
    )
    sums_in, maxes_in, totals_in = (
        lax.all_to_all(
            local_sum.reshape(1, SEQS, heads_all, SPAN, HD),
            "tp",
            split_axis=2,
            concat_axis=0,
            tiled=True,
        ),
        lax.all_to_all(
            local_max.reshape(1, SEQS, heads_all, SPAN),
            "tp",
            split_axis=2,
            concat_axis=0,
            tiled=True,
        ),
        lax.all_to_all(
            local_total.reshape(1, SEQS, heads_all, SPAN),
            "tp",
            split_axis=2,
            concat_axis=0,
            tiled=True,
        ),
    )
    running_max = jnp.maximum(maxes_in.max(0), fresh_max)
    factors = jnp.exp(maxes_in - running_max[None])
    fresh_weights = jnp.where(causal, jnp.exp(fresh_scores - running_max[..., None]), 0.0)
    totals = (factors * totals_in).sum(0) + fresh_weights.sum(-1)
    summed = (factors[..., None] * sums_in).sum(0)
    summed = summed + jnp.einsum(
        "shck,skhd->shcd",
        fresh_weights.astype(jnp.bfloat16),
        own_values,
        preferred_element_type=jnp.float32,
    )
    attn = (summed / totals[..., None]).astype(jnp.bfloat16)
    attn = jnp.transpose(attn, (0, 2, 1, 3)).reshape(token_count, HQ_DEV * HD)
    share_part = lax.psum_scatter(
        lax.dot_general(
            o_weight, attn, (((0,), (1,)), ((), ())), preferred_element_type=jnp.float32
        ),
        "tp",
        scatter_dimension=0,
        tiled=True,
    )
    hidden = (residual.astype(jnp.float32) + share_part.T).astype(jnp.bfloat16)
    stream = lax.all_gather(hidden, "tp", axis=1, tiled=True)
    return rms_rows(stream, ffn_gain).astype(jnp.bfloat16)


def solution(mesh):
    return jax.shard_map(
        per_device_ring if mesh.shape["tp"] == 2 * CHIPS else per_device,
        mesh=mesh,
        in_specs=(
            P("replica", "tp"),
            P(),
            P(),
            P(None, "tp"),
            P(None, "tp"),
            P("tp", None),
            P("replica", "tp", None),
            P("replica", "tp", None),
            P("replica"),
        ),
        out_specs=P("replica", None),
        check_vma=False,
    )
```

```python
import functools

import jax
import jax.numpy as jnp
from jax import lax
from jax.experimental import pallas as pl
from jax.experimental.pallas import tpu as pltpu
from jax.sharding import PartitionSpec as P

HD = 128
KVH = 8
HQ_DEV = 1
SPAN = 64
SEQS = 2
CTX_DEV = 64
TOKENS = SEQS * SPAN
MIB = 1024 * 1024

epsilon = 1e-05


def rms_rows(rows, gain):
    values_f = rows.astype(jnp.float32)
    factor = lax.rsqrt(jnp.mean(values_f * values_f, axis=-1, keepdims=True) + epsilon)
    return values_f * factor * gain.astype(jnp.float32)


def rope_tables(positions):
    half_width = HD // 2
    frequency = 500000.0 ** (-jnp.arange(half_width, dtype=jnp.float32) / half_width)
    angles = positions.astype(jnp.float32)[:, None] * frequency[None, :]
    return jnp.cos(angles), jnp.sin(angles)


def rotate(vectors, positions):
    half_width = vectors.shape[-1] // 2
    cosine, sine = rope_tables(positions)
    cosine, sine = cosine[:, None, :], sine[:, None, :]
    first_half = vectors[..., :half_width]
    second_half = vectors[..., half_width:]
    return jnp.concatenate(
        [first_half * cosine - second_half * sine, second_half * cosine + first_half * sine],
        axis=-1,
    )


CHIPS = 8
RING = (0, 2, 4, 6, 7, 5, 3, 1)
ONWARD = [(2 * RING[i], 2 * RING[(i + 1) % CHIPS]) for i in range(CHIPS)] + [
    (2 * RING[i] + 1, 2 * RING[i - 1] + 1) for i in range(CHIPS)
]
ENTER = [(2 * RING[i], 2 * RING[i - 1] + 1) for i in range(CHIPS)] + [
    (2 * RING[i] + 1, 2 * RING[(i + 1) % CHIPS]) for i in range(CHIPS)
]
LEAVE = [(2 * RING[i], 2 * RING[(i + 1) % CHIPS] + 1) for i in range(CHIPS)] + [
    (2 * RING[i] + 1, 2 * RING[i - 1]) for i in range(CHIPS)
]
SWAP = [(t, t ^ 1) for t in range(2 * CHIPS)]
FRESH = [(k, 2 * k) for k in range(KVH)] + [(KVH + k, 2 * k + 1) for k in range(KVH)]
VMEM = pl.BlockSpec(memory_space=pltpu.VMEM)
SMEM = pl.BlockSpec(memory_space=pltpu.SMEM)
HBM = pl.BlockSpec(memory_space=pltpu.HBM)


def ring_place(rank):
    chip = rank // 2
    return jnp.where(chip % 2 == 0, chip // 2, CHIPS - 1 - chip // 2)


def chip_at(place):
    place = place % CHIPS
    return jnp.where(place < CHIPS // 2, 2 * place, 2 * CHIPS - 1 - 2 * place)


def send(array, pairs):
    return lax.ppermute(array, "tp", pairs)


def xor(bits):
    return [(t, t ^ bits) for t in range(2 * CHIPS)]


def after(array, *others):
    return lax.optimization_barrier((array, others))[0]


def ring_gather(own, ready=None, direct=False):
    straight, swapped = own, None if direct else send(own, SWAP)
    crossed = own if direct else swapped
    mine = [own]
    for step in range(1, 5):
        if step == 4 and ready is not None:
            straight = after(straight, ready)
        straight = send(straight, ONWARD)
        mine.append(straight)
        if step < 4:
            crossed = send(crossed, ENTER if direct and step == 1 else ONWARD)
            mine.append(crossed)
    theirs = [send(own, SWAP) if direct else swapped]
    return mine, theirs + [send(block, SWAP) for block in mine[1:]]


def gathered_ids(rank):
    place = ring_place(rank)
    ids = []
    for side in range(2):
        device = rank ^ side
        core = device % 2
        ids.append(device)
        for step in range(1, 5):
            chip = 2 * chip_at(place + (2 * core - 1) * step)
            ids += [chip + core, chip + 1 - core] if step < 4 else [chip + core]
    return jnp.stack(ids).astype(jnp.int32)


SHARES = ((4, 0), (3, 1), (3, 0), (2, 1), (2, 0), (1, 1), (1, 0), (0, 0))


def share_ids(rank):
    place, core = ring_place(rank), rank % 2
    return jnp.stack(
        [2 * chip_at(place + (1 - 2 * core) * d) + (core + other) % 2 for d, other in SHARES]
    ).astype(jnp.int32)


def ring_sum(shares):
    straight, crossed = shares[4, 0], shares[3, 1]
    for step in range(1, 5):
        straight = send(straight, ONWARD)
        if step < 4:
            crossed = send(crossed, LEAVE if step == 3 else ONWARD)
            straight = add_share(straight, shares[4 - step, 0])
        if step < 3:
            crossed = add_share(crossed, shares[3 - step, 1])
    return straight, crossed


def add_share(part, share):
    return (part.astype(jnp.float32) + share).astype(jnp.bfloat16)


def split_cache(key_cache, value_cache, rank, rank_id):
    core = rank % 2
    give = jnp.stack(
        [lax.dynamic_index_in_dim(c, 1 - core, 0, keepdims=False) for c in (key_cache, value_cache)]
    )
    return pack(rank_id, key_cache, value_cache, send(give, SWAP))


def move_cache(parts, *when):
    keep, give = parts
    came = send(give, xor(2))
    pieces = [jnp.stack([keep[m], came[m]]) for m in range(1, 4)]
    return [keep, came] + [send(piece, xor(4 * m)) for m, piece in zip(range(1, 4), pieces)]


def pack_kernel(rank, keys, values, theirs, keep, give, sems):
    me = rank[0]
    copies = []
    for m in range(4):
        for j, out in enumerate((keep, give)):
            chip = (me ^ (4 * m + 2 * j)) // 2
            head = pl.ds(pl.multiple_of(chip * HD, HD), HD)
            for k, cache in enumerate((keys, values)):
                copies.append(
                    pltpu.make_async_copy(
                        cache.at[me % 2, :, head], out.at[m, 0, k], sems.at[m, j, k]
                    )
                )
                copies[-1].start()
            out[m, 1, 0] = theirs[0, :, head]
            out[m, 1, 1] = theirs[1, :, head]
    for copy in copies:
        copy.wait()


def pack(rank_id, key_cache, value_cache, theirs):
    return pl.pallas_call(
        pack_kernel,
        out_shape=[jax.ShapeDtypeStruct((4, 2, 2, CTX_DEV, HD), jnp.bfloat16)] * 2,
        in_specs=[SMEM] + [HBM] * 2 + [VMEM],
        out_specs=[VMEM] * 2,
        scratch_shapes=[pltpu.SemaphoreType.DMA((4, 2, 2))],
        compiler_params=pltpu.CompilerParams(vmem_limit_bytes=8 * MIB),
        cost_estimate=pl.CostEstimate(flops=0, bytes_accessed=MIB, transcendentals=0),
        name="pack_cache",
    )(rank_id, in_hbm(key_cache), in_hbm(value_cache), theirs)


def lanes(block, j):
    return block[:, 128 * j : 128 * j + 128].astype(jnp.float32)


def square_sums(blocks, total):
    for block in blocks:
        for j in range(block.shape[1] // 128):
            v = lanes(block, j)
            total = total + v * v
    return total


def row_factors(squares, features):
    mean = jnp.sum(squares, axis=1, keepdims=True) * (1.0 / features)
    return lax.rsqrt(mean + epsilon)


def normed_block(block, factors, gain_row):
    return jnp.concatenate(
        [
            (lanes(block, j) * factors * gain_row[:, 128 * j : 128 * j + 128]).astype(jnp.bfloat16)
            for j in range(block.shape[1] // 128)
        ],
        axis=1,
    )


def in_hbm(array):
    return pltpu.with_memory_space_constraint(array, pltpu.HBM)


def load_kernel(ids, wq, wkv, out, sems):
    count, width, _ = out.shape
    copies = []
    for i in range(count):
        rows = pl.ds(pl.multiple_of(ids[i] * width, width), width)
        for j, weight in enumerate((wq, wkv)):
            copies.append(
                pltpu.make_async_copy(
                    weight.at[rows, :], out.at[i, :, pl.ds(j * HD, HD)], sems.at[j, i]
                )
            )
            copies[-1].start()
    for copy in copies:
        copy.wait()


def load_weights(ids, wq, wkv, width):
    return pl.pallas_call(
        load_kernel,
        out_shape=jax.ShapeDtypeStruct((16, width, 2 * HD), jnp.bfloat16),
        in_specs=[SMEM] + [HBM] * 2,
        out_specs=VMEM,
        scratch_shapes=[pltpu.SemaphoreType.DMA((2, 16))],
        compiler_params=pltpu.CompilerParams(vmem_limit_bytes=16 * MIB),
        cost_estimate=pl.CostEstimate(flops=0, bytes_accessed=16 * MIB, transcendentals=0),
        name="load_weights",
    )(ids, in_hbm(wq), in_hbm(wkv))


def all_factors(blocks):
    total = square_sums(blocks, jnp.zeros((TOKENS, 128), jnp.float32))
    return row_factors(total, 16 * blocks[0].shape[1])


def project_kernel(ids, to, *refs):
    blocks, refs = refs[:16], refs[16:]
    gain, weights, cosine, sine, kv_cos, kv_sin, wo, wo_other = refs[:8]
    q_keep, q_send, fresh, first_weights, sems = refs[8:]
    copies = share_copies(to, 0, wo, wo_other, first_weights, sems)
    factors = all_factors(blocks)
    total = jnp.zeros((TOKENS, 2 * HD), jnp.float32)
    for i in range(16):
        normed = normed_block(blocks[i], factors, gain[ids[i]])
        total = total + jnp.dot(normed, weights[i], preferred_element_type=jnp.float32)
    q, kv = total[:, :HD], total[:, HD:]
    q = (q * cosine[...] + pltpu.roll(q, HD // 2, 1) * sine[...]).astype(jnp.bfloat16)
    kv = (kv * kv_cos[...] + pltpu.roll(kv, HD // 2, 1) * kv_sin[...]).astype(jnp.bfloat16)
    core_one = ids[0] % 2 == 1
    q_keep[...] = jnp.where(core_one, q[SPAN:], q[:SPAN])
    q_send[...] = jnp.where(core_one, q[:SPAN], q[SPAN:])
    fresh[...] = kv
    for pair in copies:
        for copy in pair:
            copy.wait()


def project(ids, to, arrays, gain, weights, tables, wo, wo_other, ahead):
    width = arrays[0].shape[1]
    return pl.pallas_call(
        project_kernel,
        out_shape=[jax.ShapeDtypeStruct((SPAN, HD), jnp.bfloat16)] * 2
        + [
            jax.ShapeDtypeStruct((TOKENS, HD), jnp.bfloat16),
            jax.ShapeDtypeStruct((ahead, 2 * HD, width), jnp.bfloat16),
        ],
        in_specs=[SMEM] * 2 + [VMEM] * (len(arrays) + 6) + [HBM] * 2,
        out_specs=[VMEM] * 4,
        scratch_shapes=[pltpu.SemaphoreType.DMA((2, ahead))],
        compiler_params=pltpu.CompilerParams(vmem_limit_bytes=24 * MIB),
        cost_estimate=pl.CostEstimate(
            flops=2 * TOKENS * weights.size, bytes_accessed=12 * MIB, transcendentals=0
        ),
        name="norm_project",
    )(ids, to, *arrays, gain, weights, *tables, in_hbm(wo), wo_other)


def share_copies(to, first, weight, weight_other, out, sems):
    count, _, width = out.shape
    copies = []
    for i in range(count):
        columns = pl.ds(pl.multiple_of(to[first + i] * width, width), width)
        pair = [
            pltpu.make_async_copy(part.at[:, columns], out.at[i, pl.ds(j * HD, HD), :], sems.at[j, i])
            for j, part in enumerate((weight, weight_other))
        ]
        for copy in pair:
            copy.start()
        copies.append(pair)
    return copies


def cache_rows(cache, which):
    keep, came, rest = cache[0], cache[1], cache[2:]
    groups = [part[0, c, which] for part in (keep, came) for c in range(2)]
    groups += [part[x, c, which] for part in rest for x in range(2) for c in range(2)]
    return jnp.concatenate(groups, axis=0)


CONTRACT = (((1,), (1,)), ((), ()))


def scores_kernel(info, q, q_other, *refs):
    cache, scores = refs[:5], refs[5]
    core, rank = info[SEQS], info[SEQS + 1]
    queries = jnp.concatenate([q[...], q_other[...]], axis=0)
    old = lax.dot_general(
        queries, cache_rows(cache, 0), CONTRACT, preferred_element_type=jnp.float32
    )
    lane = lax.broadcasted_iota(jnp.int32, old.shape, 1)
    position = (rank ^ (lane // CTX_DEV)) * CTX_DEV + lane % CTX_DEV
    scores[...] = jnp.where(position < info[core], old * HD ** (-0.5), -1e30)


def cache_scores(info, q, q_other, cache):
    return pl.pallas_call(
        scores_kernel,
        out_shape=jax.ShapeDtypeStruct((TOKENS, 16 * CTX_DEV), jnp.float32),
        in_specs=[SMEM] + [VMEM] * 7,
        out_specs=VMEM,
        compiler_params=pltpu.CompilerParams(vmem_limit_bytes=16 * MIB),
        cost_estimate=pl.CostEstimate(flops=32 * MIB, bytes_accessed=MIB, transcendentals=0),
        name="cache_scores",
    )(info, q, q_other, *cache)


def attend_kernel(info, q, q_other, fresh_own, fresh_other, scores, *refs):
    cache, out = refs[:5], refs[5]
    core = info[SEQS]
    came = fresh_other[...]
    fresh_keys = jnp.where(core == 0, fresh_own[:SPAN, :], came)
    fresh_values = jnp.where(core == 0, came, fresh_own[SPAN:, :])
    queries = jnp.concatenate([q[...], q_other[...]], axis=0)
    old = scores[...]
    valid = old > -1e29
    fresh = lax.dot_general(
        queries, fresh_keys, CONTRACT, preferred_element_type=jnp.float32
    ) * HD ** (-0.5)
    place = lax.broadcasted_iota(jnp.int32, fresh.shape, 0) % SPAN
    causal = place >= lax.broadcasted_iota(jnp.int32, fresh.shape, 1)
    fresh = jnp.where(causal, fresh, -1e30)
    most = jnp.maximum(jnp.max(old, axis=1, keepdims=True), jnp.max(fresh, axis=1, keepdims=True))
    old_weights = jnp.where(valid, jnp.exp(old - most), 0.0)
    fresh_weights = jnp.where(causal, jnp.exp(fresh - most), 0.0)
    totals = jnp.sum(old_weights, axis=1, keepdims=True) + jnp.sum(
        fresh_weights, axis=1, keepdims=True
    )
    summed = jnp.dot(
        old_weights.astype(jnp.bfloat16), cache_rows(cache, 1), preferred_element_type=jnp.float32
    ) + jnp.dot(
        fresh_weights.astype(jnp.bfloat16), fresh_values, preferred_element_type=jnp.float32
    )
    attn = (summed / totals).astype(jnp.bfloat16)
    out[:, :HD] = attn[:SPAN]
    out[:, HD:] = attn[SPAN:]


def attend(info, q, q_other, fresh_own, fresh_other, scores, cache):
    return pl.pallas_call(
        attend_kernel,
        out_shape=jax.ShapeDtypeStruct((SPAN, 2 * HD), jnp.bfloat16),
        in_specs=[SMEM] + [VMEM] * 10,
        out_specs=VMEM,
        compiler_params=pltpu.CompilerParams(vmem_limit_bytes=16 * MIB),
        cost_estimate=pl.CostEstimate(
            flops=48 * MIB, bytes_accessed=2 * MIB, transcendentals=TOKENS * 1088
        ),
        name="attend",
    )(info, q, q_other, fresh_own, fresh_other, scores, *cache)


def both_heads(core, attn, attn_other):
    mine = attn[...]
    theirs = jnp.concatenate([attn_other[:, HD:], attn_other[:, :HD]], axis=1)
    core_one = core[0] == 1
    return jnp.concatenate(
        [jnp.where(core_one, theirs, mine), jnp.where(core_one, mine, theirs)], axis=0
    )


def first_shares_kernel(core, attn, attn_other, weights, *outs):
    rows = both_heads(core, attn, attn_other)
    for i, out in enumerate(outs):
        out[...] = jnp.dot(rows, weights[i], preferred_element_type=jnp.float32).astype(out.dtype)


def first_shares(shares, core, attn, attn_other, weights):
    count, _, width = weights.shape
    out_shape = [jax.ShapeDtypeStruct((TOKENS, width), jnp.bfloat16)] * count
    arrays = pl.pallas_call(
        first_shares_kernel,
        out_shape=out_shape,
        in_specs=[SMEM] + [VMEM] * 3,
        out_specs=[VMEM] * len(out_shape),
        compiler_params=pltpu.CompilerParams(vmem_limit_bytes=16 * MIB),
        cost_estimate=pl.CostEstimate(
            flops=2 * TOKENS * weights.size, bytes_accessed=count * MIB, transcendentals=0
        ),
        name="first_shares",
    )(core, attn, attn_other, weights)
    return dict(zip(shares, arrays))


def more_shares_kernel(first, core, to, attn, attn_other, weight, weight_other, *refs):
    outs, (weights, sems) = refs[:-2], refs[-2:]
    copies = share_copies(to, first, weight, weight_other, weights, sems)
    rows = both_heads(core, attn, attn_other)
    for i, out in enumerate(outs):
        for copy in copies[i]:
            copy.wait()
        out[...] = jnp.dot(rows, weights[i], preferred_element_type=jnp.float32)


def more_shares(core, to, attn, attn_other, weight, weight_other, first, last):
    count, width = last - first, weight.shape[1] // 16
    out_shape = [jax.ShapeDtypeStruct((TOKENS, width), jnp.float32)] * count
    arrays = pl.pallas_call(
        functools.partial(more_shares_kernel, first),
        out_shape=out_shape,
        in_specs=[SMEM] * 2 + [VMEM] * 2 + [HBM] * 2,
        out_specs=[VMEM] * len(out_shape),
        scratch_shapes=[
            pltpu.VMEM((count, 2 * HD, width), jnp.bfloat16),
            pltpu.SemaphoreType.DMA((2, count)),
        ],
        compiler_params=pltpu.CompilerParams(vmem_limit_bytes=16 * MIB),
        cost_estimate=pl.CostEstimate(
            flops=4 * TOKENS * HD * width * count,
            bytes_accessed=count * MIB,
            transcendentals=0,
        ),
        name="shares_%d" % first,
    )(core, to, attn, attn_other, in_hbm(weight), weight_other)
    return dict(zip(SHARES[first:last], arrays))


def final_kernel(ids, *refs):
    blocks, refs = refs[:16], refs[16:]
    gain, out, staged, sems = refs
    width = staged.shape[2]
    factors = all_factors(blocks)
    copies = []
    for i in range(16):
        staged[i] = normed_block(blocks[i], factors, gain[ids[i]])
        copy = pltpu.make_async_copy(
            staged.at[i],
            out.at[:, pl.ds(pl.multiple_of(ids[i] * width, width), width)],
            sems.at[i],
        )
        copy.start()
        copies.append(copy)
    for copy in copies:
        copy.wait()


def final_norm(ids, arrays, gain):
    width = arrays[0].shape[1]
    return pl.pallas_call(
        final_kernel,
        out_shape=jax.ShapeDtypeStruct((TOKENS, 16 * width), jnp.bfloat16),
        in_specs=[SMEM] + [VMEM] * (len(arrays) + 1),
        out_specs=HBM,
        scratch_shapes=[
            pltpu.VMEM((16, TOKENS, width), jnp.bfloat16),
            pltpu.SemaphoreType.DMA((16,)),
        ],
        compiler_params=pltpu.CompilerParams(vmem_limit_bytes=24 * MIB),
        cost_estimate=pl.CostEstimate(
            flops=16 * MIB, bytes_accessed=12 * MIB, transcendentals=0
        ),
        name="final_norm",
    )(ids, *arrays, gain)


def per_device_ring(
    residual, attn_gain, ffn_gain, q_weight, kv_weight, o_weight, key_cache, value_cache, prefix
):
    rank = lax.axis_index("tp")
    core = rank % 2
    width = residual.shape[1]
    ids = gathered_ids(rank)
    to = share_ids(rank)
    core_id, rank_id = core[None].astype(jnp.int32), rank[None].astype(jnp.int32)
    info = jnp.concatenate([prefix, core_id, rank_id])

    weight_other = send(o_weight, SWAP)
    parts = split_cache(key_cache, value_cache, rank, rank_id)
    mine, theirs = ring_gather(residual, weight_other, direct=True)
    weights = load_weights(ids, q_weight, kv_weight, width)
    cache = move_cache(parts)

    positions = (prefix[:, None] + jnp.arange(SPAN, dtype=jnp.int32)[None, :]).reshape(-1)
    cosine, sine = rope_tables(positions)
    cosine = jnp.concatenate([cosine, cosine], axis=1)
    sine = jnp.concatenate([-sine, sine], axis=1)
    holds_keys = rank < KVH
    tables = (cosine, sine, jnp.where(holds_keys, cosine, 1.0), jnp.where(holds_keys, sine, 0.0))

    gain = attn_gain.reshape(16, 1, width).astype(jnp.float32)
    mine[0] = after(mine[0], cache[1])
    q_keep, q_send, fresh, first_weights = project(
        ids, to, mine + theirs, gain, weights, tables, o_weight, weight_other, 2
    )
    q_other = send(q_send, SWAP)
    fresh_own = send(fresh, FRESH)
    fresh_other = send(jnp.where(core == 0, fresh_own[SPAN:], fresh_own[:SPAN]), SWAP)
    scores = cache_scores(info, q_keep, q_other, cache)
    attn = attend(info, q_keep, q_other, fresh_own, fresh_other, scores, cache)
    attn_other = send(attn, SWAP)

    shares = first_shares(SHARES[:2], core_id, attn, attn_other, first_weights)
    shares.update(
        more_shares(core_id, to, attn, attn_other, o_weight, weight_other, 2, len(SHARES))
    )
    one_way, other_way = ring_sum(shares)
    projected = shares[0, 0] + one_way.astype(jnp.float32) + other_way.astype(jnp.float32)
    hidden = (residual.astype(jnp.float32) + projected).astype(jnp.bfloat16)

    mine, theirs = ring_gather(hidden)
    gain = ffn_gain.reshape(16, 1, width).astype(jnp.float32)
    return final_norm(ids, mine + theirs, gain)


def per_device(
    residual, attn_gain, ffn_gain, q_weight, kv_weight, o_weight, key_cache, value_cache, prefix
):
    tp_count = lax.axis_size("tp")
    tp_rank = lax.axis_index("tp")
    heads_all = HQ_DEV * tp_count
    group_size = heads_all // KVH
    token_count = SEQS * SPAN
    score_scale = HD ** (-0.5)
    whole_rows = lax.all_gather(residual, "tp", axis=1, tiled=True)
    normed = rms_rows(whole_rows, attn_gain).astype(jnp.bfloat16)
    positions = (prefix[:, None] + jnp.arange(SPAN, dtype=jnp.int32)[None, :]).reshape(-1)
    queries = jnp.dot(normed, q_weight, preferred_element_type=jnp.float32).reshape(
        token_count, HQ_DEV, HD
    )
    queries = rotate(queries, positions).astype(jnp.bfloat16)
    kv_part = jnp.dot(normed, kv_weight, preferred_element_type=jnp.float32)
    kv_whole = lax.all_gather(kv_part, "tp", axis=1, tiled=True)
    new_keys = rotate(kv_whole[:, : KVH * HD].reshape(token_count, KVH, HD), positions).astype(
        jnp.bfloat16
    )
    new_values = kv_whole[:, KVH * HD :].reshape(token_count, KVH, HD).astype(jnp.bfloat16)
    head_ids = tp_rank * HQ_DEV + jnp.arange(HQ_DEV, dtype=jnp.int32)
    own_kv = head_ids // group_size
    own_keys = jnp.take(new_keys, own_kv, axis=1).reshape(SEQS, SPAN, HQ_DEV, HD)
    own_values = jnp.take(new_values, own_kv, axis=1).reshape(SEQS, SPAN, HQ_DEV, HD)
    own_queries = queries.reshape(SEQS, SPAN, HQ_DEV, HD)
    causal = (jnp.arange(SPAN)[:, None] >= jnp.arange(SPAN)[None, :])[None, None]
    fresh_scores = (
        jnp.einsum("schd,skhd->shck", own_queries, own_keys, preferred_element_type=jnp.float32)
        * score_scale
    )
    fresh_scores = jnp.where(causal, fresh_scores, -1e30)
    fresh_max = fresh_scores.max(-1)
    gathered = lax.all_gather(queries.reshape(token_count, HQ_DEV * HD), "tp", axis=1, tiled=True)
    queries_all = gathered.reshape(SEQS, SPAN, KVH, group_size, HD)
    keys_local = key_cache.reshape(SEQS, CTX_DEV, KVH, HD)
    values_local = value_cache.reshape(SEQS, CTX_DEV, KVH, HD)
    local_scores = (
        jnp.einsum("sckgd,sjkd->skgcj", queries_all, keys_local, preferred_element_type=jnp.float32)
        * score_scale
    )
    first_slot = tp_rank * CTX_DEV
    is_valid = ((first_slot + jnp.arange(CTX_DEV, dtype=jnp.int32))[None, :] < prefix[:, None])[
        :, None, None, None, :
    ]
    local_scores = jnp.where(is_valid, local_scores, -1e30)
    local_max = local_scores.max(-1)
    local_weights = jnp.where(is_valid, jnp.exp(local_scores - local_max[..., None]), 0.0)
    local_total = local_weights.sum(-1)
    local_sum = jnp.einsum(
        "skgcj,sjkd->skgcd",
        local_weights.astype(jnp.bfloat16),
        values_local,
        preferred_element_type=jnp.float32,
    )
    sums_in, maxes_in, totals_in = (
        lax.all_to_all(
            local_sum.reshape(1, SEQS, heads_all, SPAN, HD),
            "tp",
            split_axis=2,
            concat_axis=0,
            tiled=True,
        ),
        lax.all_to_all(
            local_max.reshape(1, SEQS, heads_all, SPAN),
            "tp",
            split_axis=2,
            concat_axis=0,
            tiled=True,
        ),
        lax.all_to_all(
            local_total.reshape(1, SEQS, heads_all, SPAN),
            "tp",
            split_axis=2,
            concat_axis=0,
            tiled=True,
        ),
    )
    running_max = jnp.maximum(maxes_in.max(0), fresh_max)
    factors = jnp.exp(maxes_in - running_max[None])
    fresh_weights = jnp.where(causal, jnp.exp(fresh_scores - running_max[..., None]), 0.0)
    totals = (factors * totals_in).sum(0) + fresh_weights.sum(-1)
    summed = (factors[..., None] * sums_in).sum(0)
    summed = summed + jnp.einsum(
        "shck,skhd->shcd",
        fresh_weights.astype(jnp.bfloat16),
        own_values,
        preferred_element_type=jnp.float32,
    )
    attn = (summed / totals[..., None]).astype(jnp.bfloat16)
    attn = jnp.transpose(attn, (0, 2, 1, 3)).reshape(token_count, HQ_DEV * HD)
    share_part = lax.psum_scatter(
        lax.dot_general(
            o_weight, attn, (((0,), (1,)), ((), ())), preferred_element_type=jnp.float32
        ),
        "tp",
        scatter_dimension=0,
        tiled=True,
    )
    hidden = (residual.astype(jnp.float32) + share_part.T).astype(jnp.bfloat16)
    stream = lax.all_gather(hidden, "tp", axis=1, tiled=True)
    return rms_rows(stream, ffn_gain).astype(jnp.bfloat16)


def solution(mesh):
    return jax.shard_map(
        per_device_ring if mesh.shape["tp"] == 2 * CHIPS else per_device,
        mesh=mesh,
        in_specs=(
            P("replica", "tp"),
            P(),
            P(),
            P(None, "tp"),
            P(None, "tp"),
            P("tp", None),
            P("replica", "tp", None),
            P("replica", "tp", None),
            P("replica"),
        ),
        out_specs=P("replica", None),
        check_vma=False,
    )
```

```python
import functools

import jax
import jax.numpy as jnp
from jax import lax
from jax.experimental import pallas as pl
from jax.experimental.pallas import tpu as pltpu
from jax.sharding import PartitionSpec as P

HD = 128
KVH = 8
HQ_DEV = 1
SPAN = 64
SEQS = 2
CTX_DEV = 64
TOKENS = SEQS * SPAN
MIB = 1024 * 1024

epsilon = 1e-05


def rms_rows(rows, gain):
    values_f = rows.astype(jnp.float32)
    factor = lax.rsqrt(jnp.mean(values_f * values_f, axis=-1, keepdims=True) + epsilon)
    return values_f * factor * gain.astype(jnp.float32)


def rope_tables(positions):
    half_width = HD // 2
    frequency = 500000.0 ** (-jnp.arange(half_width, dtype=jnp.float32) / half_width)
    angles = positions.astype(jnp.float32)[:, None] * frequency[None, :]
    return jnp.cos(angles), jnp.sin(angles)


def rotate(vectors, positions):
    half_width = vectors.shape[-1] // 2
    cosine, sine = rope_tables(positions)
    cosine, sine = cosine[:, None, :], sine[:, None, :]
    first_half = vectors[..., :half_width]
    second_half = vectors[..., half_width:]
    return jnp.concatenate(
        [first_half * cosine - second_half * sine, second_half * cosine + first_half * sine],
        axis=-1,
    )


CHIPS = 8
RING = (0, 2, 4, 6, 7, 5, 3, 1)
ONWARD = [(2 * RING[i], 2 * RING[(i + 1) % CHIPS]) for i in range(CHIPS)] + [
    (2 * RING[i] + 1, 2 * RING[i - 1] + 1) for i in range(CHIPS)
]
ENTER = [(2 * RING[i], 2 * RING[i - 1] + 1) for i in range(CHIPS)] + [
    (2 * RING[i] + 1, 2 * RING[(i + 1) % CHIPS]) for i in range(CHIPS)
]
LEAVE = [(2 * RING[i], 2 * RING[(i + 1) % CHIPS] + 1) for i in range(CHIPS)] + [
    (2 * RING[i] + 1, 2 * RING[i - 1]) for i in range(CHIPS)
]
SWAP = [(t, t ^ 1) for t in range(2 * CHIPS)]
FRESH = [(k, 2 * k) for k in range(KVH)] + [(KVH + k, 2 * k + 1) for k in range(KVH)]
VMEM = pl.BlockSpec(memory_space=pltpu.VMEM)
SMEM = pl.BlockSpec(memory_space=pltpu.SMEM)
HBM = pl.BlockSpec(memory_space=pltpu.HBM)


def ring_place(rank):
    chip = rank // 2
    return jnp.where(chip % 2 == 0, chip // 2, CHIPS - 1 - chip // 2)


def chip_at(place):
    place = place % CHIPS
    return jnp.where(place < CHIPS // 2, 2 * place, 2 * CHIPS - 1 - 2 * place)


def send(array, pairs):
    return lax.ppermute(array, "tp", pairs)


def xor(bits):
    return [(t, t ^ bits) for t in range(2 * CHIPS)]


def after(array, *others):
    return lax.optimization_barrier((array, others))[0]


def ring_gather(own, ready=None, direct=False):
    straight, swapped = own, None if direct else send(own, SWAP)
    crossed = own if direct else swapped
    mine = [own]
    for step in range(1, 5):
        if step == 4 and ready is not None:
            straight = after(straight, ready)
        straight = send(straight, ONWARD)
        mine.append(straight)
        if step < 4:
            crossed = send(crossed, ENTER if direct and step == 1 else ONWARD)
            mine.append(crossed)
    theirs = [send(own, SWAP) if direct else swapped]
    return mine, theirs + [send(block, SWAP) for block in mine[1:]]


def gathered_ids(rank):
    place = ring_place(rank)
    ids = []
    for side in range(2):
        device = rank ^ side
        core = device % 2
        ids.append(device)
        for step in range(1, 5):
            chip = 2 * chip_at(place + (2 * core - 1) * step)
            ids += [chip + core, chip + 1 - core] if step < 4 else [chip + core]
    return jnp.stack(ids).astype(jnp.int32)


SHARES = ((4, 0), (3, 1), (3, 0), (2, 1), (2, 0), (1, 1), (1, 0), (0, 0))


def share_ids(rank):
    place, core = ring_place(rank), rank % 2
    return jnp.stack(
        [2 * chip_at(place + (1 - 2 * core) * d) + (core + other) % 2 for d, other in SHARES]
    ).astype(jnp.int32)


def ring_sum(shares):
    straight, crossed = shares[4, 0], shares[3, 1]
    for step in range(1, 5):
        straight = send(straight, ONWARD)
        if step < 4:
            crossed = send(crossed, LEAVE if step == 3 else ONWARD)
            straight = add_share(straight, shares[4 - step, 0])
        if step < 3:
            crossed = add_share(crossed, shares[3 - step, 1])
    return straight, crossed


def add_share(part, share):
    return (part.astype(jnp.float32) + share).astype(jnp.bfloat16)


def split_cache(key_cache, value_cache, rank, rank_id):
    core = rank % 2
    give = jnp.stack(
        [lax.dynamic_index_in_dim(c, 1 - core, 0, keepdims=False) for c in (key_cache, value_cache)]
    )
    return pack(rank_id, key_cache, value_cache, send(give, SWAP))


def move_cache(parts, *when):
    keep, give = parts
    came = send(give, xor(2))
    pieces = [jnp.stack([keep[m], came[m]]) for m in range(1, 4)]
    return [keep, came] + [send(piece, xor(4 * m)) for m, piece in zip(range(1, 4), pieces)]


def pack_kernel(rank, keys, values, theirs, keep, give, sems):
    me = rank[0]
    copies = []
    for m in range(4):
        for j, out in enumerate((keep, give)):
            chip = (me ^ (4 * m + 2 * j)) // 2
            head = pl.ds(pl.multiple_of(chip * HD, HD), HD)
            for k, cache in enumerate((keys, values)):
                copies.append(
                    pltpu.make_async_copy(
                        cache.at[me % 2, :, head], out.at[m, 0, k], sems.at[m, j, k]
                    )
                )
                copies[-1].start()
            out[m, 1, 0] = theirs[0, :, head]
            out[m, 1, 1] = theirs[1, :, head]
    for copy in copies:
        copy.wait()


def pack(rank_id, key_cache, value_cache, theirs):
    return pl.pallas_call(
        pack_kernel,
        out_shape=[jax.ShapeDtypeStruct((4, 2, 2, CTX_DEV, HD), jnp.bfloat16)] * 2,
        in_specs=[SMEM] + [HBM] * 2 + [VMEM],
        out_specs=[VMEM] * 2,
        scratch_shapes=[pltpu.SemaphoreType.DMA((4, 2, 2))],
        compiler_params=pltpu.CompilerParams(vmem_limit_bytes=8 * MIB),
        cost_estimate=pl.CostEstimate(flops=0, bytes_accessed=MIB, transcendentals=0),
        name="pack_cache",
    )(rank_id, in_hbm(key_cache), in_hbm(value_cache), theirs)


def lanes(block, j):
    return block[:, 128 * j : 128 * j + 128].astype(jnp.float32)


def square_sums(blocks, total):
    for block in blocks:
        for j in range(block.shape[1] // 128):
            v = lanes(block, j)
            total = total + v * v
    return total


def row_factors(squares, features):
    mean = jnp.sum(squares, axis=1, keepdims=True) * (1.0 / features)
    return lax.rsqrt(mean + epsilon)


def normed_block(block, factors, gain_row):
    return jnp.concatenate(
        [
            (lanes(block, j) * factors * gain_row[:, 128 * j : 128 * j + 128]).astype(jnp.bfloat16)
            for j in range(block.shape[1] // 128)
        ],
        axis=1,
    )


def in_hbm(array):
    return pltpu.with_memory_space_constraint(array, pltpu.HBM)


def load_kernel(ids, wq, wkv, out, sems):
    count, width, _ = out.shape
    copies = []
    for i in range(count):
        rows = pl.ds(pl.multiple_of(ids[i] * width, width), width)
        for j, weight in enumerate((wq, wkv)):
            copies.append(
                pltpu.make_async_copy(
                    weight.at[rows, :], out.at[i, :, pl.ds(j * HD, HD)], sems.at[j, i]
                )
            )
            copies[-1].start()
    for copy in copies:
        copy.wait()


def load_weights(ids, wq, wkv, width):
    return pl.pallas_call(
        load_kernel,
        out_shape=jax.ShapeDtypeStruct((16, width, 2 * HD), jnp.bfloat16),
        in_specs=[SMEM] + [HBM] * 2,
        out_specs=VMEM,
        scratch_shapes=[pltpu.SemaphoreType.DMA((2, 16))],
        compiler_params=pltpu.CompilerParams(vmem_limit_bytes=16 * MIB),
        cost_estimate=pl.CostEstimate(flops=0, bytes_accessed=16 * MIB, transcendentals=0),
        name="load_weights",
    )(ids, in_hbm(wq), in_hbm(wkv))


def all_factors(blocks):
    total = square_sums(blocks, jnp.zeros((TOKENS, 128), jnp.float32))
    return row_factors(total, 16 * blocks[0].shape[1])


def project_kernel(ids, to, *refs):
    blocks, refs = refs[:16], refs[16:]
    gain, weights, cosine, sine, kv_cos, kv_sin, wo, wo_other = refs[:8]
    q_keep, q_send, fresh, first_weights, sems = refs[8:]
    copies = share_copies(to, 0, wo, wo_other, first_weights, sems)
    factors = all_factors(blocks)
    total = jnp.zeros((TOKENS, 2 * HD), jnp.float32)
    for i in range(16):
        normed = normed_block(blocks[i], factors, gain[ids[i]])
        total = total + jnp.dot(normed, weights[i], preferred_element_type=jnp.float32)
    q, kv = total[:, :HD], total[:, HD:]
    q = (q * cosine[...] + pltpu.roll(q, HD // 2, 1) * sine[...]).astype(jnp.bfloat16)
    kv = (kv * kv_cos[...] + pltpu.roll(kv, HD // 2, 1) * kv_sin[...]).astype(jnp.bfloat16)
    core_one = ids[0] % 2 == 1
    q_keep[...] = jnp.where(core_one, q[SPAN:], q[:SPAN])
    q_send[...] = jnp.where(core_one, q[:SPAN], q[SPAN:])
    fresh[...] = kv
    for pair in copies:
        for copy in pair:
            copy.wait()


def project(ids, to, arrays, gain, weights, tables, wo, wo_other, ahead):
    width = arrays[0].shape[1]
    return pl.pallas_call(
        project_kernel,
        out_shape=[jax.ShapeDtypeStruct((SPAN, HD), jnp.bfloat16)] * 2
        + [
            jax.ShapeDtypeStruct((TOKENS, HD), jnp.bfloat16),
            jax.ShapeDtypeStruct((ahead, 2 * HD, width), jnp.bfloat16),
        ],
        in_specs=[SMEM] * 2 + [VMEM] * (len(arrays) + 6) + [HBM] * 2,
        out_specs=[VMEM] * 4,
        scratch_shapes=[pltpu.SemaphoreType.DMA((2, ahead))],
        compiler_params=pltpu.CompilerParams(vmem_limit_bytes=15 * MIB),
        cost_estimate=pl.CostEstimate(
            flops=2 * TOKENS * weights.size, bytes_accessed=12 * MIB, transcendentals=0
        ),
        name="norm_project",
    )(ids, to, *arrays, gain, weights, *tables, in_hbm(wo), wo_other)


def share_copies(to, first, weight, weight_other, out, sems):
    count, _, width = out.shape
    copies = []
    for i in range(count):
        columns = pl.ds(pl.multiple_of(to[first + i] * width, width), width)
        pair = [
            pltpu.make_async_copy(part.at[:, columns], out.at[i, pl.ds(j * HD, HD), :], sems.at[j, i])
            for j, part in enumerate((weight, weight_other))
        ]
        for copy in pair:
            copy.start()
        copies.append(pair)
    return copies


def cache_rows(cache, which):
    keep, came, rest = cache[0], cache[1], cache[2:]
    groups = [part[0, c, which] for part in (keep, came) for c in range(2)]
    groups += [part[x, c, which] for part in rest for x in range(2) for c in range(2)]
    return jnp.concatenate(groups, axis=0)


CONTRACT = (((1,), (1,)), ((), ()))


def scores_kernel(info, q, q_other, *refs):
    cache, scores = refs[:5], refs[5]
    core, rank = info[SEQS], info[SEQS + 1]
    queries = jnp.concatenate([q[...], q_other[...]], axis=0)
    old = lax.dot_general(
        queries, cache_rows(cache, 0), CONTRACT, preferred_element_type=jnp.float32
    )
    lane = lax.broadcasted_iota(jnp.int32, old.shape, 1)
    position = (rank ^ (lane // CTX_DEV)) * CTX_DEV + lane % CTX_DEV
    scores[...] = jnp.where(position < info[core], old * HD ** (-0.5), -1e30)


def cache_scores(info, q, q_other, cache):
    return pl.pallas_call(
        scores_kernel,
        out_shape=jax.ShapeDtypeStruct((TOKENS, 16 * CTX_DEV), jnp.float32),
        in_specs=[SMEM] + [VMEM] * 7,
        out_specs=VMEM,
        compiler_params=pltpu.CompilerParams(vmem_limit_bytes=16 * MIB),
        cost_estimate=pl.CostEstimate(flops=32 * MIB, bytes_accessed=MIB, transcendentals=0),
        name="cache_scores",
    )(info, q, q_other, *cache)


def attend_kernel(info, q, q_other, fresh_own, fresh_other, scores, *refs):
    cache, out = refs[:5], refs[5]
    core = info[SEQS]
    came = fresh_other[...]
    fresh_keys = jnp.where(core == 0, fresh_own[:SPAN, :], came)
    fresh_values = jnp.where(core == 0, came, fresh_own[SPAN:, :])
    queries = jnp.concatenate([q[...], q_other[...]], axis=0)
    old = scores[...]
    valid = old > -1e29
    fresh = lax.dot_general(
        queries, fresh_keys, CONTRACT, preferred_element_type=jnp.float32
    ) * HD ** (-0.5)
    place = lax.broadcasted_iota(jnp.int32, fresh.shape, 0) % SPAN
    causal = place >= lax.broadcasted_iota(jnp.int32, fresh.shape, 1)
    fresh = jnp.where(causal, fresh, -1e30)
    most = jnp.maximum(jnp.max(old, axis=1, keepdims=True), jnp.max(fresh, axis=1, keepdims=True))
    old_weights = jnp.where(valid, jnp.exp(old - most), 0.0)
    fresh_weights = jnp.where(causal, jnp.exp(fresh - most), 0.0)
    totals = jnp.sum(old_weights, axis=1, keepdims=True) + jnp.sum(
        fresh_weights, axis=1, keepdims=True
    )
    summed = jnp.dot(
        old_weights.astype(jnp.bfloat16), cache_rows(cache, 1), preferred_element_type=jnp.float32
    ) + jnp.dot(
        fresh_weights.astype(jnp.bfloat16), fresh_values, preferred_element_type=jnp.float32
    )
    attn = (summed / totals).astype(jnp.bfloat16)
    out[:, :HD] = attn[:SPAN]
    out[:, HD:] = attn[SPAN:]


def attend(info, q, q_other, fresh_own, fresh_other, scores, cache):
    return pl.pallas_call(
        attend_kernel,
        out_shape=jax.ShapeDtypeStruct((SPAN, 2 * HD), jnp.bfloat16),
        in_specs=[SMEM] + [VMEM] * 10,
        out_specs=VMEM,
        compiler_params=pltpu.CompilerParams(vmem_limit_bytes=16 * MIB),
        cost_estimate=pl.CostEstimate(
            flops=48 * MIB, bytes_accessed=2 * MIB, transcendentals=TOKENS * 1088
        ),
        name="attend",
    )(info, q, q_other, fresh_own, fresh_other, scores, *cache)


def both_heads(core, attn, attn_other):
    mine = attn[...]
    theirs = jnp.concatenate([attn_other[:, HD:], attn_other[:, :HD]], axis=1)
    core_one = core[0] == 1
    return jnp.concatenate(
        [jnp.where(core_one, theirs, mine), jnp.where(core_one, mine, theirs)], axis=0
    )


def first_shares_kernel(core, attn, attn_other, weights, *outs):
    rows = both_heads(core, attn, attn_other)
    for i, out in enumerate(outs):
        out[...] = jnp.dot(rows, weights[i], preferred_element_type=jnp.float32).astype(out.dtype)


def first_shares(shares, core, attn, attn_other, weights):
    count, _, width = weights.shape
    out_shape = [jax.ShapeDtypeStruct((TOKENS, width), jnp.bfloat16)] * count
    arrays = pl.pallas_call(
        first_shares_kernel,
        out_shape=out_shape,
        in_specs=[SMEM] + [VMEM] * 3,
        out_specs=[VMEM] * len(out_shape),
        compiler_params=pltpu.CompilerParams(vmem_limit_bytes=16 * MIB),
        cost_estimate=pl.CostEstimate(
            flops=2 * TOKENS * weights.size, bytes_accessed=count * MIB, transcendentals=0
        ),
        name="first_shares",
    )(core, attn, attn_other, weights)
    return dict(zip(shares, arrays))


def more_shares_kernel(first, core, to, attn, attn_other, weight, weight_other, *refs):
    outs, (weights, sems) = refs[:-2], refs[-2:]
    copies = share_copies(to, first, weight, weight_other, weights, sems)
    rows = both_heads(core, attn, attn_other)
    for i, out in enumerate(outs):
        for copy in copies[i]:
            copy.wait()
        out[...] = jnp.dot(rows, weights[i], preferred_element_type=jnp.float32)


def more_shares(core, to, attn, attn_other, weight, weight_other, first, last):
    count, width = last - first, weight.shape[1] // 16
    out_shape = [jax.ShapeDtypeStruct((TOKENS, width), jnp.float32)] * count
    arrays = pl.pallas_call(
        functools.partial(more_shares_kernel, first),
        out_shape=out_shape,
        in_specs=[SMEM] * 2 + [VMEM] * 2 + [HBM] * 2,
        out_specs=[VMEM] * len(out_shape),
        scratch_shapes=[
            pltpu.VMEM((count, 2 * HD, width), jnp.bfloat16),
            pltpu.SemaphoreType.DMA((2, count)),
        ],
        compiler_params=pltpu.CompilerParams(vmem_limit_bytes=16 * MIB),
        cost_estimate=pl.CostEstimate(
            flops=4 * TOKENS * HD * width * count,
            bytes_accessed=count * MIB,
            transcendentals=0,
        ),
        name="shares_%d" % first,
    )(core, to, attn, attn_other, in_hbm(weight), weight_other)
    return dict(zip(SHARES[first:last], arrays))


def final_kernel(ids, *refs):
    blocks, refs = refs[:16], refs[16:]
    gain, out, staged, sems = refs
    width = staged.shape[2]
    factors = all_factors(blocks)
    copies = []
    for i in range(16):
        staged[i] = normed_block(blocks[i], factors, gain[ids[i]])
        copy = pltpu.make_async_copy(
            staged.at[i],
            out.at[:, pl.ds(pl.multiple_of(ids[i] * width, width), width)],
            sems.at[i],
        )
        copy.start()
        copies.append(copy)
    for copy in copies:
        copy.wait()


def final_norm(ids, arrays, gain):
    width = arrays[0].shape[1]
    return pl.pallas_call(
        final_kernel,
        out_shape=jax.ShapeDtypeStruct((TOKENS, 16 * width), jnp.bfloat16),
        in_specs=[SMEM] + [VMEM] * (len(arrays) + 1),
        out_specs=HBM,
        scratch_shapes=[
            pltpu.VMEM((16, TOKENS, width), jnp.bfloat16),
            pltpu.SemaphoreType.DMA((16,)),
        ],
        compiler_params=pltpu.CompilerParams(vmem_limit_bytes=15 * MIB),
        cost_estimate=pl.CostEstimate(
            flops=16 * MIB, bytes_accessed=12 * MIB, transcendentals=0
        ),
        name="final_norm",
    )(ids, *arrays, gain)


def per_device_ring(
    residual, attn_gain, ffn_gain, q_weight, kv_weight, o_weight, key_cache, value_cache, prefix
):
    rank = lax.axis_index("tp")
    core = rank % 2
    width = residual.shape[1]
    ids = gathered_ids(rank)
    to = share_ids(rank)
    core_id, rank_id = core[None].astype(jnp.int32), rank[None].astype(jnp.int32)
    info = jnp.concatenate([prefix, core_id, rank_id])

    weight_other = send(o_weight, SWAP)
    parts = split_cache(key_cache, value_cache, rank, rank_id)
    mine, theirs = ring_gather(residual, weight_other, direct=True)
    weights = load_weights(ids, q_weight, kv_weight, width)
    cache = move_cache(parts)

    positions = (prefix[:, None] + jnp.arange(SPAN, dtype=jnp.int32)[None, :]).reshape(-1)
    cosine, sine = rope_tables(positions)
    cosine = jnp.concatenate([cosine, cosine], axis=1)
    sine = jnp.concatenate([-sine, sine], axis=1)
    holds_keys = rank < KVH
    tables = (cosine, sine, jnp.where(holds_keys, cosine, 1.0), jnp.where(holds_keys, sine, 0.0))

    gain = attn_gain.reshape(16, 1, width).astype(jnp.float32)
    mine[0] = after(mine[0], cache[1])
    q_keep, q_send, fresh, first_weights = project(
        ids, to, mine + theirs, gain, weights, tables, o_weight, weight_other, 2
    )
    q_other = send(q_send, SWAP)
    fresh_own = send(fresh, FRESH)
    fresh_other = send(jnp.where(core == 0, fresh_own[SPAN:], fresh_own[:SPAN]), SWAP)
    scores = cache_scores(info, q_keep, q_other, cache)
    attn = attend(info, q_keep, q_other, fresh_own, fresh_other, scores, cache)
    attn_other = send(attn, SWAP)

    shares = first_shares(SHARES[:2], core_id, attn, attn_other, first_weights)
    shares.update(
        more_shares(core_id, to, attn, attn_other, o_weight, weight_other, 2, len(SHARES))
    )
    one_way, other_way = ring_sum(shares)
    projected = shares[0, 0] + one_way.astype(jnp.float32) + other_way.astype(jnp.float32)
    hidden = (residual.astype(jnp.float32) + projected).astype(jnp.bfloat16)

    mine, theirs = ring_gather(hidden)
    gain = ffn_gain.reshape(16, 1, width).astype(jnp.float32)
    return final_norm(ids, mine + theirs, gain)


def per_device(
    residual, attn_gain, ffn_gain, q_weight, kv_weight, o_weight, key_cache, value_cache, prefix
):
    tp_count = lax.axis_size("tp")
    tp_rank = lax.axis_index("tp")
    heads_all = HQ_DEV * tp_count
    group_size = heads_all // KVH
    token_count = SEQS * SPAN
    score_scale = HD ** (-0.5)
    whole_rows = lax.all_gather(residual, "tp", axis=1, tiled=True)
    normed = rms_rows(whole_rows, attn_gain).astype(jnp.bfloat16)
    positions = (prefix[:, None] + jnp.arange(SPAN, dtype=jnp.int32)[None, :]).reshape(-1)
    queries = jnp.dot(normed, q_weight, preferred_element_type=jnp.float32).reshape(
        token_count, HQ_DEV, HD
    )
    queries = rotate(queries, positions).astype(jnp.bfloat16)
    kv_part = jnp.dot(normed, kv_weight, preferred_element_type=jnp.float32)
    kv_whole = lax.all_gather(kv_part, "tp", axis=1, tiled=True)
    new_keys = rotate(kv_whole[:, : KVH * HD].reshape(token_count, KVH, HD), positions).astype(
        jnp.bfloat16
    )
    new_values = kv_whole[:, KVH * HD :].reshape(token_count, KVH, HD).astype(jnp.bfloat16)
    head_ids = tp_rank * HQ_DEV + jnp.arange(HQ_DEV, dtype=jnp.int32)
    own_kv = head_ids // group_size
    own_keys = jnp.take(new_keys, own_kv, axis=1).reshape(SEQS, SPAN, HQ_DEV, HD)
    own_values = jnp.take(new_values, own_kv, axis=1).reshape(SEQS, SPAN, HQ_DEV, HD)
    own_queries = queries.reshape(SEQS, SPAN, HQ_DEV, HD)
    causal = (jnp.arange(SPAN)[:, None] >= jnp.arange(SPAN)[None, :])[None, None]
    fresh_scores = (
        jnp.einsum("schd,skhd->shck", own_queries, own_keys, preferred_element_type=jnp.float32)
        * score_scale
    )
    fresh_scores = jnp.where(causal, fresh_scores, -1e30)
    fresh_max = fresh_scores.max(-1)
    gathered = lax.all_gather(queries.reshape(token_count, HQ_DEV * HD), "tp", axis=1, tiled=True)
    queries_all = gathered.reshape(SEQS, SPAN, KVH, group_size, HD)
    keys_local = key_cache.reshape(SEQS, CTX_DEV, KVH, HD)
    values_local = value_cache.reshape(SEQS, CTX_DEV, KVH, HD)
    local_scores = (
        jnp.einsum("sckgd,sjkd->skgcj", queries_all, keys_local, preferred_element_type=jnp.float32)
        * score_scale
    )
    first_slot = tp_rank * CTX_DEV
    is_valid = ((first_slot + jnp.arange(CTX_DEV, dtype=jnp.int32))[None, :] < prefix[:, None])[
        :, None, None, None, :
    ]
    local_scores = jnp.where(is_valid, local_scores, -1e30)
    local_max = local_scores.max(-1)
    local_weights = jnp.where(is_valid, jnp.exp(local_scores - local_max[..., None]), 0.0)
    local_total = local_weights.sum(-1)
    local_sum = jnp.einsum(
        "skgcj,sjkd->skgcd",
        local_weights.astype(jnp.bfloat16),
        values_local,
        preferred_element_type=jnp.float32,
    )
    sums_in, maxes_in, totals_in = (
        lax.all_to_all(
            local_sum.reshape(1, SEQS, heads_all, SPAN, HD),
            "tp",
            split_axis=2,
            concat_axis=0,
            tiled=True,
        ),
        lax.all_to_all(
            local_max.reshape(1, SEQS, heads_all, SPAN),
            "tp",
            split_axis=2,
            concat_axis=0,
            tiled=True,
        ),
        lax.all_to_all(
            local_total.reshape(1, SEQS, heads_all, SPAN),
            "tp",
            split_axis=2,
            concat_axis=0,
            tiled=True,
        ),
    )
    running_max = jnp.maximum(maxes_in.max(0), fresh_max)
    factors = jnp.exp(maxes_in - running_max[None])
    fresh_weights = jnp.where(causal, jnp.exp(fresh_scores - running_max[..., None]), 0.0)
    totals = (factors * totals_in).sum(0) + fresh_weights.sum(-1)
    summed = (factors[..., None] * sums_in).sum(0)
    summed = summed + jnp.einsum(
        "shck,skhd->shcd",
        fresh_weights.astype(jnp.bfloat16),
        own_values,
        preferred_element_type=jnp.float32,
    )
    attn = (summed / totals[..., None]).astype(jnp.bfloat16)
    attn = jnp.transpose(attn, (0, 2, 1, 3)).reshape(token_count, HQ_DEV * HD)
    share_part = lax.psum_scatter(
        lax.dot_general(
            o_weight, attn, (((0,), (1,)), ((), ())), preferred_element_type=jnp.float32
        ),
        "tp",
        scatter_dimension=0,
        tiled=True,
    )
    hidden = (residual.astype(jnp.float32) + share_part.T).astype(jnp.bfloat16)
    stream = lax.all_gather(hidden, "tp", axis=1, tiled=True)
    return rms_rows(stream, ffn_gain).astype(jnp.bfloat16)


def solution(mesh):
    return jax.shard_map(
        per_device_ring if mesh.shape["tp"] == 2 * CHIPS else per_device,
        mesh=mesh,
        in_specs=(
            P("replica", "tp"),
            P(),
            P(),
            P(None, "tp"),
            P(None, "tp"),
            P("tp", None),
            P("replica", "tp", None),
            P("replica", "tp", None),
            P("replica"),
        ),
        out_specs=P("replica", None),
        check_vma=False,
    )
```

```python
import functools

import jax
import jax.numpy as jnp
from jax import lax
from jax.experimental import pallas as pl
from jax.experimental.pallas import tpu as pltpu
from jax.sharding import PartitionSpec as P

HD = 128
KVH = 8
HQ_DEV = 1
SPAN = 64
SEQS = 2
CTX_DEV = 64
TOKENS = SEQS * SPAN
MIB = 1024 * 1024

epsilon = 1e-05


def rms_rows(rows, gain):
    values_f = rows.astype(jnp.float32)
    factor = lax.rsqrt(jnp.mean(values_f * values_f, axis=-1, keepdims=True) + epsilon)
    return values_f * factor * gain.astype(jnp.float32)


def rope_tables(positions):
    half_width = HD // 2
    frequency = 500000.0 ** (-jnp.arange(half_width, dtype=jnp.float32) / half_width)
    angles = positions.astype(jnp.float32)[:, None] * frequency[None, :]
    return jnp.cos(angles), jnp.sin(angles)


def rotate(vectors, positions):
    half_width = vectors.shape[-1] // 2
    cosine, sine = rope_tables(positions)
    cosine, sine = cosine[:, None, :], sine[:, None, :]
    first_half = vectors[..., :half_width]
    second_half = vectors[..., half_width:]
    return jnp.concatenate(
        [first_half * cosine - second_half * sine, second_half * cosine + first_half * sine],
        axis=-1,
    )


CHIPS = 8
RING = (0, 2, 4, 6, 7, 5, 3, 1)
ONWARD = [(2 * RING[i], 2 * RING[(i + 1) % CHIPS]) for i in range(CHIPS)] + [
    (2 * RING[i] + 1, 2 * RING[i - 1] + 1) for i in range(CHIPS)
]
ENTER = [(2 * RING[i], 2 * RING[i - 1] + 1) for i in range(CHIPS)] + [
    (2 * RING[i] + 1, 2 * RING[(i + 1) % CHIPS]) for i in range(CHIPS)
]
LEAVE = [(2 * RING[i], 2 * RING[(i + 1) % CHIPS] + 1) for i in range(CHIPS)] + [
    (2 * RING[i] + 1, 2 * RING[i - 1]) for i in range(CHIPS)
]
SWAP = [(t, t ^ 1) for t in range(2 * CHIPS)]
FRESH = [(k, 2 * k) for k in range(KVH)] + [(KVH + k, 2 * k + 1) for k in range(KVH)]
VMEM = pl.BlockSpec(memory_space=pltpu.VMEM)
SMEM = pl.BlockSpec(memory_space=pltpu.SMEM)
HBM = pl.BlockSpec(memory_space=pltpu.HBM)


def ring_place(rank):
    chip = rank // 2
    return jnp.where(chip % 2 == 0, chip // 2, CHIPS - 1 - chip // 2)


def chip_at(place):
    place = place % CHIPS
    return jnp.where(place < CHIPS // 2, 2 * place, 2 * CHIPS - 1 - 2 * place)


def send(array, pairs):
    return lax.ppermute(array, "tp", pairs)


def xor(bits):
    return [(t, t ^ bits) for t in range(2 * CHIPS)]


def after(array, *others):
    return lax.optimization_barrier((array, others))[0]


def ring_gather(own, ready=None, direct=False):
    straight, swapped = own, None if direct else send(own, SWAP)
    crossed = own if direct else swapped
    mine = [own]
    for step in range(1, 5):
        if step == 4 and ready is not None:
            straight = after(straight, ready)
        straight = send(straight, ONWARD)
        mine.append(straight)
        if step < 4:
            crossed = send(crossed, ENTER if direct and step == 1 else ONWARD)
            mine.append(crossed)
    theirs = [send(own, SWAP) if direct else swapped]
    return mine, theirs + [send(block, SWAP) for block in mine[1:]]


def gathered_ids(rank):
    place = ring_place(rank)
    ids = []
    for side in range(2):
        device = rank ^ side
        core = device % 2
        ids.append(device)
        for step in range(1, 5):
            chip = 2 * chip_at(place + (2 * core - 1) * step)
            ids += [chip + core, chip + 1 - core] if step < 4 else [chip + core]
    return jnp.stack(ids).astype(jnp.int32)


SHARES = ((4, 0), (3, 1), (3, 0), (2, 1), (2, 0), (1, 1), (1, 0), (0, 0))


def share_ids(rank):
    place, core = ring_place(rank), rank % 2
    return jnp.stack(
        [2 * chip_at(place + (1 - 2 * core) * d) + (core + other) % 2 for d, other in SHARES]
    ).astype(jnp.int32)


def ring_sum(shares):
    straight, crossed = shares[4, 0], shares[3, 1]
    for step in range(1, 5):
        straight = send(straight, ONWARD)
        if step < 4:
            crossed = send(crossed, LEAVE if step == 3 else ONWARD)
            straight = add_share(straight, shares[4 - step, 0])
        if step < 3:
            crossed = add_share(crossed, shares[3 - step, 1])
    return straight, crossed


def add_share(part, share):
    return (part.astype(jnp.float32) + share).astype(jnp.bfloat16)


def split_cache(key_cache, value_cache, rank, rank_id):
    core = rank % 2
    give = jnp.stack(
        [lax.dynamic_index_in_dim(c, 1 - core, 0, keepdims=False) for c in (key_cache, value_cache)]
    )
    return pack(rank_id, key_cache, value_cache, send(give, SWAP))


def move_cache(parts, *when):
    keep, give = parts
    came = send(give, xor(2))
    pieces = [jnp.stack([keep[m], came[m]]) for m in range(1, 4)]
    return [keep, came] + [send(piece, xor(4 * m)) for m, piece in zip(range(1, 4), pieces)]


def pack_kernel(rank, keys, values, theirs, keep, give, sems):
    me = rank[0]
    copies = []
    for m in range(4):
        for j, out in enumerate((keep, give)):
            chip = (me ^ (4 * m + 2 * j)) // 2
            head = pl.ds(pl.multiple_of(chip * HD, HD), HD)
            for k, cache in enumerate((keys, values)):
                copies.append(
                    pltpu.make_async_copy(
                        cache.at[me % 2, :, head], out.at[m, 0, k], sems.at[m, j, k]
                    )
                )
                copies[-1].start()
            out[m, 1, 0] = theirs[0, :, head]
            out[m, 1, 1] = theirs[1, :, head]
    for copy in copies:
        copy.wait()


def pack(rank_id, key_cache, value_cache, theirs):
    return pl.pallas_call(
        pack_kernel,
        out_shape=[jax.ShapeDtypeStruct((4, 2, 2, CTX_DEV, HD), jnp.bfloat16)] * 2,
        in_specs=[SMEM] + [HBM] * 2 + [VMEM],
        out_specs=[VMEM] * 2,
        scratch_shapes=[pltpu.SemaphoreType.DMA((4, 2, 2))],
        compiler_params=pltpu.CompilerParams(vmem_limit_bytes=8 * MIB),
        cost_estimate=pl.CostEstimate(flops=0, bytes_accessed=MIB, transcendentals=0),
        name="pack_cache",
    )(rank_id, in_hbm(key_cache), in_hbm(value_cache), theirs)


def lanes(block, j):
    return block[:, 128 * j : 128 * j + 128].astype(jnp.float32)


def square_sums(blocks, total):
    for block in blocks:
        for j in range(block.shape[1] // 128):
            v = lanes(block, j)
            total = total + v * v
    return total


def row_factors(squares, features):
    mean = jnp.sum(squares, axis=1, keepdims=True) * (1.0 / features)
    return lax.rsqrt(mean + epsilon)


def normed_block(block, factors, gain_row):
    return jnp.concatenate(
        [
            (lanes(block, j) * factors * gain_row[:, 128 * j : 128 * j + 128]).astype(jnp.bfloat16)
            for j in range(block.shape[1] // 128)
        ],
        axis=1,
    )


def in_hbm(array):
    return pltpu.with_memory_space_constraint(array, pltpu.HBM)


def load_kernel(ids, wq, wkv, out, sems):
    count, width, _ = out.shape
    copies = []
    for i in range(count):
        rows = pl.ds(pl.multiple_of(ids[i] * width, width), width)
        for j, weight in enumerate((wq, wkv)):
            copies.append(
                pltpu.make_async_copy(
                    weight.at[rows, :], out.at[i, :, pl.ds(j * HD, HD)], sems.at[j, i]
                )
            )
            copies[-1].start()
    for copy in copies:
        copy.wait()


def load_weights(ids, wq, wkv, width):
    return pl.pallas_call(
        load_kernel,
        out_shape=jax.ShapeDtypeStruct((16, width, 2 * HD), jnp.bfloat16),
        in_specs=[SMEM] + [HBM] * 2,
        out_specs=VMEM,
        scratch_shapes=[pltpu.SemaphoreType.DMA((2, 16))],
        compiler_params=pltpu.CompilerParams(vmem_limit_bytes=16 * MIB),
        cost_estimate=pl.CostEstimate(flops=0, bytes_accessed=16 * MIB, transcendentals=0),
        name="load_weights",
    )(ids, in_hbm(wq), in_hbm(wkv))


def all_factors(blocks):
    total = square_sums(blocks, jnp.zeros((TOKENS, 128), jnp.float32))
    return row_factors(total, 16 * blocks[0].shape[1])


def project_kernel(ids, *refs):
    blocks, refs = refs[:16], refs[16:]
    gain, weights, cosine, sine, kv_cos, kv_sin = refs[:6]
    q_keep, q_send, fresh = refs[6:]
    factors = all_factors(blocks)
    total = jnp.zeros((TOKENS, 2 * HD), jnp.float32)
    for i in range(16):
        normed = normed_block(blocks[i], factors, gain[ids[i]])
        total = total + jnp.dot(normed, weights[i], preferred_element_type=jnp.float32)
    q, kv = total[:, :HD], total[:, HD:]
    q = (q * cosine[...] + pltpu.roll(q, HD // 2, 1) * sine[...]).astype(jnp.bfloat16)
    kv = (kv * kv_cos[...] + pltpu.roll(kv, HD // 2, 1) * kv_sin[...]).astype(jnp.bfloat16)
    core_one = ids[0] % 2 == 1
    q_keep[...] = jnp.where(core_one, q[SPAN:], q[:SPAN])
    q_send[...] = jnp.where(core_one, q[:SPAN], q[SPAN:])
    fresh[...] = kv


def project(ids, arrays, gain, weights, tables):
    return pl.pallas_call(
        project_kernel,
        out_shape=[jax.ShapeDtypeStruct((SPAN, HD), jnp.bfloat16)] * 2
        + [jax.ShapeDtypeStruct((TOKENS, HD), jnp.bfloat16)],
        in_specs=[SMEM] + [VMEM] * (len(arrays) + 6),
        out_specs=[VMEM] * 3,
        compiler_params=pltpu.CompilerParams(vmem_limit_bytes=24 * MIB),
        cost_estimate=pl.CostEstimate(
            flops=2 * TOKENS * weights.size, bytes_accessed=12 * MIB, transcendentals=0
        ),
        name="norm_project",
    )(ids, *arrays, gain, weights, *tables)


def share_copies(to, first, weight, weight_other, out, sems):
    count, _, width = out.shape
    copies = []
    for i in range(count):
        columns = pl.ds(pl.multiple_of(to[first + i] * width, width), width)
        pair = [
            pltpu.make_async_copy(part.at[:, columns], out.at[i, pl.ds(j * HD, HD), :], sems.at[j, i])
            for j, part in enumerate((weight, weight_other))
        ]
        for copy in pair:
            copy.start()
        copies.append(pair)
    return copies


def cache_rows(cache, which):
    keep, came, rest = cache[0], cache[1], cache[2:]
    groups = [part[0, c, which] for part in (keep, came) for c in range(2)]
    groups += [part[x, c, which] for part in rest for x in range(2) for c in range(2)]
    return jnp.concatenate(groups, axis=0)


CONTRACT = (((1,), (1,)), ((), ()))


def scores_kernel(info, to, q, q_other, *refs):
    cache, weight, weight_other, scores, weights, sems = refs[:5], *refs[5:]
    copies = share_copies(to, 0, weight, weight_other, weights, sems)
    core, rank = info[SEQS], info[SEQS + 1]
    queries = jnp.concatenate([q[...], q_other[...]], axis=0)
    old = lax.dot_general(
        queries, cache_rows(cache, 0), CONTRACT, preferred_element_type=jnp.float32
    )
    lane = lax.broadcasted_iota(jnp.int32, old.shape, 1)
    position = (rank ^ (lane // CTX_DEV)) * CTX_DEV + lane % CTX_DEV
    scores[...] = jnp.where(position < info[core], old * HD ** (-0.5), -1e30)
    for pair in copies:
        for copy in pair:
            copy.wait()


def cache_scores(info, to, q, q_other, cache, weight, weight_other, ahead):
    width = weight.shape[1] // 16
    return pl.pallas_call(
        scores_kernel,
        out_shape=[
            jax.ShapeDtypeStruct((TOKENS, 16 * CTX_DEV), jnp.float32),
            jax.ShapeDtypeStruct((ahead, 2 * HD, width), jnp.bfloat16),
        ],
        in_specs=[SMEM] * 2 + [VMEM] * 7 + [HBM] * 2,
        out_specs=[VMEM] * 2,
        scratch_shapes=[pltpu.SemaphoreType.DMA((2, ahead))],
        compiler_params=pltpu.CompilerParams(vmem_limit_bytes=16 * MIB),
        cost_estimate=pl.CostEstimate(
            flops=32 * MIB, bytes_accessed=3 * MIB, transcendentals=0
        ),
        name="cache_scores",
    )(info, to, q, q_other, *cache, in_hbm(weight), weight_other)


def attend_kernel(info, q, q_other, fresh_own, fresh_other, scores, *refs):
    cache, out = refs[:5], refs[5]
    core = info[SEQS]
    came = fresh_other[...]
    fresh_keys = jnp.where(core == 0, fresh_own[:SPAN, :], came)
    fresh_values = jnp.where(core == 0, came, fresh_own[SPAN:, :])
    queries = jnp.concatenate([q[...], q_other[...]], axis=0)
    old = scores[...]
    valid = old > -1e29
    fresh = lax.dot_general(
        queries, fresh_keys, CONTRACT, preferred_element_type=jnp.float32
    ) * HD ** (-0.5)
    place = lax.broadcasted_iota(jnp.int32, fresh.shape, 0) % SPAN
    causal = place >= lax.broadcasted_iota(jnp.int32, fresh.shape, 1)
    fresh = jnp.where(causal, fresh, -1e30)
    most = jnp.maximum(jnp.max(old, axis=1, keepdims=True), jnp.max(fresh, axis=1, keepdims=True))
    old_weights = jnp.where(valid, jnp.exp(old - most), 0.0)
    fresh_weights = jnp.where(causal, jnp.exp(fresh - most), 0.0)
    totals = jnp.sum(old_weights, axis=1, keepdims=True) + jnp.sum(
        fresh_weights, axis=1, keepdims=True
    )
    summed = jnp.dot(
        old_weights.astype(jnp.bfloat16), cache_rows(cache, 1), preferred_element_type=jnp.float32
    ) + jnp.dot(
        fresh_weights.astype(jnp.bfloat16), fresh_values, preferred_element_type=jnp.float32
    )
    attn = (summed / totals).astype(jnp.bfloat16)
    out[:, :HD] = attn[:SPAN]
    out[:, HD:] = attn[SPAN:]


def attend(info, q, q_other, fresh_own, fresh_other, scores, cache):
    return pl.pallas_call(
        attend_kernel,
        out_shape=jax.ShapeDtypeStruct((SPAN, 2 * HD), jnp.bfloat16),
        in_specs=[SMEM] + [VMEM] * 10,
        out_specs=VMEM,
        compiler_params=pltpu.CompilerParams(vmem_limit_bytes=16 * MIB),
        cost_estimate=pl.CostEstimate(
            flops=48 * MIB, bytes_accessed=2 * MIB, transcendentals=TOKENS * 1088
        ),
        name="attend",
    )(info, q, q_other, fresh_own, fresh_other, scores, *cache)


def both_heads(core, attn, attn_other):
    mine = attn[...]
    theirs = jnp.concatenate([attn_other[:, HD:], attn_other[:, :HD]], axis=1)
    core_one = core[0] == 1
    return jnp.concatenate(
        [jnp.where(core_one, theirs, mine), jnp.where(core_one, mine, theirs)], axis=0
    )


def first_shares_kernel(core, attn, attn_other, weights, *outs):
    rows = both_heads(core, attn, attn_other)
    for i, out in enumerate(outs):
        out[...] = jnp.dot(rows, weights[i], preferred_element_type=jnp.float32).astype(out.dtype)


def first_shares(shares, core, attn, attn_other, weights):
    count, _, width = weights.shape
    out_shape = [jax.ShapeDtypeStruct((TOKENS, width), jnp.bfloat16)] * count
    arrays = pl.pallas_call(
        first_shares_kernel,
        out_shape=out_shape,
        in_specs=[SMEM] + [VMEM] * 3,
        out_specs=[VMEM] * len(out_shape),
        compiler_params=pltpu.CompilerParams(vmem_limit_bytes=16 * MIB),
        cost_estimate=pl.CostEstimate(
            flops=2 * TOKENS * weights.size, bytes_accessed=count * MIB, transcendentals=0
        ),
        name="first_shares",
    )(core, attn, attn_other, weights)
    return dict(zip(shares, arrays))


def more_shares_kernel(first, core, to, attn, attn_other, weight, weight_other, *refs):
    outs, (weights, sems) = refs[:-2], refs[-2:]
    copies = share_copies(to, first, weight, weight_other, weights, sems)
    rows = both_heads(core, attn, attn_other)
    for i, out in enumerate(outs):
        for copy in copies[i]:
            copy.wait()
        out[...] = jnp.dot(rows, weights[i], preferred_element_type=jnp.float32)


def more_shares(core, to, attn, attn_other, weight, weight_other, first, last):
    count, width = last - first, weight.shape[1] // 16
    out_shape = [jax.ShapeDtypeStruct((TOKENS, width), jnp.float32)] * count
    arrays = pl.pallas_call(
        functools.partial(more_shares_kernel, first),
        out_shape=out_shape,
        in_specs=[SMEM] * 2 + [VMEM] * 2 + [HBM] * 2,
        out_specs=[VMEM] * len(out_shape),
        scratch_shapes=[
            pltpu.VMEM((count, 2 * HD, width), jnp.bfloat16),
            pltpu.SemaphoreType.DMA((2, count)),
        ],
        compiler_params=pltpu.CompilerParams(vmem_limit_bytes=16 * MIB),
        cost_estimate=pl.CostEstimate(
            flops=4 * TOKENS * HD * width * count,
            bytes_accessed=count * MIB,
            transcendentals=0,
        ),
        name="shares_%d" % first,
    )(core, to, attn, attn_other, in_hbm(weight), weight_other)
    return dict(zip(SHARES[first:last], arrays))


def squares_kernel(*refs):
    refs[-1][...] = square_sums(refs[:-1], jnp.zeros((TOKENS, 128), jnp.float32))


def squares_of(blocks):
    return pl.pallas_call(
        squares_kernel,
        out_shape=jax.ShapeDtypeStruct((TOKENS, 128), jnp.float32),
        in_specs=[VMEM] * len(blocks),
        out_specs=VMEM,
        compiler_params=pltpu.CompilerParams(vmem_limit_bytes=16 * MIB),
        cost_estimate=pl.CostEstimate(
            flops=4 * MIB, bytes_accessed=len(blocks) * MIB // 4, transcendentals=0
        ),
        name="squares",
    )(*blocks)


def final_kernel(ids, *refs):
    blocks, refs = refs[:16], refs[16:]
    squares, gain, out, staged, sems = refs
    width = staged.shape[2]
    factors = row_factors(square_sums(blocks[15:], squares[...]), 16 * width)
    copies = []
    for i in range(16):
        staged[i] = normed_block(blocks[i], factors, gain[ids[i]])
        copy = pltpu.make_async_copy(
            staged.at[i],
            out.at[:, pl.ds(pl.multiple_of(ids[i] * width, width), width)],
            sems.at[i],
        )
        copy.start()
        copies.append(copy)
    for copy in copies:
        copy.wait()


def final_norm(ids, arrays, squares, gain):
    width = arrays[0].shape[1]
    return pl.pallas_call(
        final_kernel,
        out_shape=jax.ShapeDtypeStruct((TOKENS, 16 * width), jnp.bfloat16),
        in_specs=[SMEM] + [VMEM] * (len(arrays) + 2),
        out_specs=HBM,
        scratch_shapes=[
            pltpu.VMEM((16, TOKENS, width), jnp.bfloat16),
            pltpu.SemaphoreType.DMA((16,)),
        ],
        compiler_params=pltpu.CompilerParams(vmem_limit_bytes=24 * MIB),
        cost_estimate=pl.CostEstimate(
            flops=16 * MIB, bytes_accessed=12 * MIB, transcendentals=0
        ),
        name="final_norm",
    )(ids, *arrays, squares, gain)


def per_device_ring(
    residual, attn_gain, ffn_gain, q_weight, kv_weight, o_weight, key_cache, value_cache, prefix
):
    rank = lax.axis_index("tp")
    core = rank % 2
    width = residual.shape[1]
    ids = gathered_ids(rank)
    to = share_ids(rank)
    core_id, rank_id = core[None].astype(jnp.int32), rank[None].astype(jnp.int32)
    info = jnp.concatenate([prefix, core_id, rank_id])

    weight_other = send(o_weight, SWAP)
    parts = split_cache(key_cache, value_cache, rank, rank_id)
    mine, theirs = ring_gather(residual, weight_other, direct=True)
    weights = load_weights(ids, q_weight, kv_weight, width)
    cache = move_cache(parts)

    positions = (prefix[:, None] + jnp.arange(SPAN, dtype=jnp.int32)[None, :]).reshape(-1)
    cosine, sine = rope_tables(positions)
    cosine = jnp.concatenate([cosine, cosine], axis=1)
    sine = jnp.concatenate([-sine, sine], axis=1)
    holds_keys = rank < KVH
    tables = (cosine, sine, jnp.where(holds_keys, cosine, 1.0), jnp.where(holds_keys, sine, 0.0))

    gain = attn_gain.reshape(16, 1, width).astype(jnp.float32)
    mine[0] = after(mine[0], cache[1])
    q_keep, q_send, fresh = project(ids, mine + theirs, gain, weights, tables)
    q_other = send(q_send, SWAP)
    fresh_own = send(fresh, FRESH)
    fresh_other = send(jnp.where(core == 0, fresh_own[SPAN:], fresh_own[:SPAN]), SWAP)
    scores, first_weights = cache_scores(
        info, to, q_keep, q_other, cache, o_weight, weight_other, 2
    )
    attn = attend(info, q_keep, q_other, fresh_own, fresh_other, scores, cache)
    attn_other = send(attn, SWAP)

    shares = first_shares(SHARES[:2], core_id, attn, attn_other, first_weights)
    shares.update(
        more_shares(core_id, to, attn, attn_other, o_weight, weight_other, 2, len(SHARES))
    )
    one_way, other_way = ring_sum(shares)
    projected = shares[0, 0] + one_way.astype(jnp.float32) + other_way.astype(jnp.float32)
    hidden = (residual.astype(jnp.float32) + projected).astype(jnp.bfloat16)

    mine, theirs = ring_gather(hidden)
    gain = ffn_gain.reshape(16, 1, width).astype(jnp.float32)
    return final_norm(ids, mine + theirs, squares_of((mine + theirs)[:15]), gain)


def per_device(
    residual, attn_gain, ffn_gain, q_weight, kv_weight, o_weight, key_cache, value_cache, prefix
):
    tp_count = lax.axis_size("tp")
    tp_rank = lax.axis_index("tp")
    heads_all = HQ_DEV * tp_count
    group_size = heads_all // KVH
    token_count = SEQS * SPAN
    score_scale = HD ** (-0.5)
    whole_rows = lax.all_gather(residual, "tp", axis=1, tiled=True)
    normed = rms_rows(whole_rows, attn_gain).astype(jnp.bfloat16)
    positions = (prefix[:, None] + jnp.arange(SPAN, dtype=jnp.int32)[None, :]).reshape(-1)
    queries = jnp.dot(normed, q_weight, preferred_element_type=jnp.float32).reshape(
        token_count, HQ_DEV, HD
    )
    queries = rotate(queries, positions).astype(jnp.bfloat16)
    kv_part = jnp.dot(normed, kv_weight, preferred_element_type=jnp.float32)
    kv_whole = lax.all_gather(kv_part, "tp", axis=1, tiled=True)
    new_keys = rotate(kv_whole[:, : KVH * HD].reshape(token_count, KVH, HD), positions).astype(
        jnp.bfloat16
    )
    new_values = kv_whole[:, KVH * HD :].reshape(token_count, KVH, HD).astype(jnp.bfloat16)
    head_ids = tp_rank * HQ_DEV + jnp.arange(HQ_DEV, dtype=jnp.int32)
    own_kv = head_ids // group_size
    own_keys = jnp.take(new_keys, own_kv, axis=1).reshape(SEQS, SPAN, HQ_DEV, HD)
    own_values = jnp.take(new_values, own_kv, axis=1).reshape(SEQS, SPAN, HQ_DEV, HD)
    own_queries = queries.reshape(SEQS, SPAN, HQ_DEV, HD)
    causal = (jnp.arange(SPAN)[:, None] >= jnp.arange(SPAN)[None, :])[None, None]
    fresh_scores = (
        jnp.einsum("schd,skhd->shck", own_queries, own_keys, preferred_element_type=jnp.float32)
        * score_scale
    )
    fresh_scores = jnp.where(causal, fresh_scores, -1e30)
    fresh_max = fresh_scores.max(-1)
    gathered = lax.all_gather(queries.reshape(token_count, HQ_DEV * HD), "tp", axis=1, tiled=True)
    queries_all = gathered.reshape(SEQS, SPAN, KVH, group_size, HD)
    keys_local = key_cache.reshape(SEQS, CTX_DEV, KVH, HD)
    values_local = value_cache.reshape(SEQS, CTX_DEV, KVH, HD)
    local_scores = (
        jnp.einsum("sckgd,sjkd->skgcj", queries_all, keys_local, preferred_element_type=jnp.float32)
        * score_scale
    )
    first_slot = tp_rank * CTX_DEV
    is_valid = ((first_slot + jnp.arange(CTX_DEV, dtype=jnp.int32))[None, :] < prefix[:, None])[
        :, None, None, None, :
    ]
    local_scores = jnp.where(is_valid, local_scores, -1e30)
    local_max = local_scores.max(-1)
    local_weights = jnp.where(is_valid, jnp.exp(local_scores - local_max[..., None]), 0.0)
    local_total = local_weights.sum(-1)
    local_sum = jnp.einsum(
        "skgcj,sjkd->skgcd",
        local_weights.astype(jnp.bfloat16),
        values_local,
        preferred_element_type=jnp.float32,
    )
    sums_in, maxes_in, totals_in = (
        lax.all_to_all(
            local_sum.reshape(1, SEQS, heads_all, SPAN, HD),
            "tp",
            split_axis=2,
            concat_axis=0,
            tiled=True,
        ),
        lax.all_to_all(
            local_max.reshape(1, SEQS, heads_all, SPAN),
            "tp",
            split_axis=2,
            concat_axis=0,
            tiled=True,
        ),
        lax.all_to_all(
            local_total.reshape(1, SEQS, heads_all, SPAN),
            "tp",
            split_axis=2,
            concat_axis=0,
            tiled=True,
        ),
    )
    running_max = jnp.maximum(maxes_in.max(0), fresh_max)
    factors = jnp.exp(maxes_in - running_max[None])
    fresh_weights = jnp.where(causal, jnp.exp(fresh_scores - running_max[..., None]), 0.0)
    totals = (factors * totals_in).sum(0) + fresh_weights.sum(-1)
    summed = (factors[..., None] * sums_in).sum(0)
    summed = summed + jnp.einsum(
        "shck,skhd->shcd",
        fresh_weights.astype(jnp.bfloat16),
        own_values,
        preferred_element_type=jnp.float32,
    )
    attn = (summed / totals[..., None]).astype(jnp.bfloat16)
    attn = jnp.transpose(attn, (0, 2, 1, 3)).reshape(token_count, HQ_DEV * HD)
    share_part = lax.psum_scatter(
        lax.dot_general(
            o_weight, attn, (((0,), (1,)), ((), ())), preferred_element_type=jnp.float32
        ),
        "tp",
        scatter_dimension=0,
        tiled=True,
    )
    hidden = (residual.astype(jnp.float32) + share_part.T).astype(jnp.bfloat16)
    stream = lax.all_gather(hidden, "tp", axis=1, tiled=True)
    return rms_rows(stream, ffn_gain).astype(jnp.bfloat16)


def solution(mesh):
    return jax.shard_map(
        per_device_ring if mesh.shape["tp"] == 2 * CHIPS else per_device,
        mesh=mesh,
        in_specs=(
            P("replica", "tp"),
            P(),
            P(),
            P(None, "tp"),
            P(None, "tp"),
            P("tp", None),
            P("replica", "tp", None),
            P("replica", "tp", None),
            P("replica"),
        ),
        out_specs=P("replica", None),
        check_vma=False,
    )
```

```python
import functools

import jax
import jax.numpy as jnp
from jax import lax
from jax.experimental import pallas as pl
from jax.experimental.pallas import tpu as pltpu
from jax.sharding import PartitionSpec as P

HD = 128
KVH = 8
HQ_DEV = 1
SPAN = 64
SEQS = 2
CTX_DEV = 64
TOKENS = SEQS * SPAN
MIB = 1024 * 1024

epsilon = 1e-05


def rms_rows(rows, gain):
    values_f = rows.astype(jnp.float32)
    factor = lax.rsqrt(jnp.mean(values_f * values_f, axis=-1, keepdims=True) + epsilon)
    return values_f * factor * gain.astype(jnp.float32)


def rope_tables(positions):
    half_width = HD // 2
    frequency = 500000.0 ** (-jnp.arange(half_width, dtype=jnp.float32) / half_width)
    angles = positions.astype(jnp.float32)[:, None] * frequency[None, :]
    return jnp.cos(angles), jnp.sin(angles)


def rotate(vectors, positions):
    half_width = vectors.shape[-1] // 2
    cosine, sine = rope_tables(positions)
    cosine, sine = cosine[:, None, :], sine[:, None, :]
    first_half = vectors[..., :half_width]
    second_half = vectors[..., half_width:]
    return jnp.concatenate(
        [first_half * cosine - second_half * sine, second_half * cosine + first_half * sine],
        axis=-1,
    )


CHIPS = 8
RING = (0, 2, 4, 6, 7, 5, 3, 1)
ONWARD = [(2 * RING[i], 2 * RING[(i + 1) % CHIPS]) for i in range(CHIPS)] + [
    (2 * RING[i] + 1, 2 * RING[i - 1] + 1) for i in range(CHIPS)
]
ENTER = [(2 * RING[i], 2 * RING[i - 1] + 1) for i in range(CHIPS)] + [
    (2 * RING[i] + 1, 2 * RING[(i + 1) % CHIPS]) for i in range(CHIPS)
]
LEAVE = [(2 * RING[i], 2 * RING[(i + 1) % CHIPS] + 1) for i in range(CHIPS)] + [
    (2 * RING[i] + 1, 2 * RING[i - 1]) for i in range(CHIPS)
]
SWAP = [(t, t ^ 1) for t in range(2 * CHIPS)]
FRESH = [(k, 2 * k) for k in range(KVH)] + [(KVH + k, 2 * k + 1) for k in range(KVH)]
VMEM = pl.BlockSpec(memory_space=pltpu.VMEM)
SMEM = pl.BlockSpec(memory_space=pltpu.SMEM)
HBM = pl.BlockSpec(memory_space=pltpu.HBM)


def ring_place(rank):
    chip = rank // 2
    return jnp.where(chip % 2 == 0, chip // 2, CHIPS - 1 - chip // 2)


def chip_at(place):
    place = place % CHIPS
    return jnp.where(place < CHIPS // 2, 2 * place, 2 * CHIPS - 1 - 2 * place)


def send(array, pairs):
    return lax.ppermute(array, "tp", pairs)


def xor(bits):
    return [(t, t ^ bits) for t in range(2 * CHIPS)]


def after(array, *others):
    return lax.optimization_barrier((array, others))[0]


def ring_gather(own, ready=None, direct=False):
    straight, swapped = own, None if direct else send(own, SWAP)
    crossed = own if direct else swapped
    mine = [own]
    for step in range(1, 5):
        if step == 4 and ready is not None:
            straight = after(straight, ready)
        straight = send(straight, ONWARD)
        mine.append(straight)
        if step < 4:
            crossed = send(crossed, ENTER if direct and step == 1 else ONWARD)
            mine.append(crossed)
    theirs = [send(own, SWAP) if direct else swapped]
    return mine, theirs + [send(block, SWAP) for block in mine[1:]]


def gathered_ids(rank):
    place = ring_place(rank)
    ids = []
    for side in range(2):
        device = rank ^ side
        core = device % 2
        ids.append(device)
        for step in range(1, 5):
            chip = 2 * chip_at(place + (2 * core - 1) * step)
            ids += [chip + core, chip + 1 - core] if step < 4 else [chip + core]
    return jnp.stack(ids).astype(jnp.int32)


SHARES = ((4, 0), (3, 1), (3, 0), (2, 1), (2, 0), (1, 1), (1, 0), (0, 0))


def share_ids(rank):
    place, core = ring_place(rank), rank % 2
    return jnp.stack(
        [2 * chip_at(place + (1 - 2 * core) * d) + (core + other) % 2 for d, other in SHARES]
    ).astype(jnp.int32)


def ring_sum(shares):
    straight, crossed = shares[4, 0], shares[3, 1]
    for step in range(1, 5):
        straight = send(straight, ONWARD)
        if step < 4:
            crossed = send(crossed, LEAVE if step == 3 else ONWARD)
            straight = add_share(straight, shares[4 - step, 0])
        if step < 3:
            crossed = add_share(crossed, shares[3 - step, 1])
    return straight, crossed


def add_share(part, share):
    return (part.astype(jnp.float32) + share).astype(jnp.bfloat16)


def split_cache(key_cache, value_cache, rank, rank_id):
    core = rank % 2
    give = jnp.stack(
        [lax.dynamic_index_in_dim(c, 1 - core, 0, keepdims=False) for c in (key_cache, value_cache)]
    )
    return pack(rank_id, key_cache, value_cache, send(give, SWAP))


def move_cache(parts, *when):
    keep, give = parts
    came = send(give, xor(2))
    pieces = [jnp.stack([keep[m], came[m]]) for m in range(1, 4)]
    return [keep, came] + [send(piece, xor(4 * m)) for m, piece in zip(range(1, 4), pieces)]


def pack_kernel(rank, keys, values, theirs, keep, give, sems):
    me = rank[0]
    copies = []
    for m in range(4):
        for j, out in enumerate((keep, give)):
            chip = (me ^ (4 * m + 2 * j)) // 2
            head = pl.ds(pl.multiple_of(chip * HD, HD), HD)
            for k, cache in enumerate((keys, values)):
                copies.append(
                    pltpu.make_async_copy(
                        cache.at[me % 2, :, head], out.at[m, 0, k], sems.at[m, j, k]
                    )
                )
                copies[-1].start()
            out[m, 1, 0] = theirs[0, :, head]
            out[m, 1, 1] = theirs[1, :, head]
    for copy in copies:
        copy.wait()


def pack(rank_id, key_cache, value_cache, theirs):
    return pl.pallas_call(
        pack_kernel,
        out_shape=[jax.ShapeDtypeStruct((4, 2, 2, CTX_DEV, HD), jnp.bfloat16)] * 2,
        in_specs=[SMEM] + [HBM] * 2 + [VMEM],
        out_specs=[VMEM] * 2,
        scratch_shapes=[pltpu.SemaphoreType.DMA((4, 2, 2))],
        compiler_params=pltpu.CompilerParams(vmem_limit_bytes=8 * MIB),
        cost_estimate=pl.CostEstimate(flops=0, bytes_accessed=MIB, transcendentals=0),
        name="pack_cache",
    )(rank_id, in_hbm(key_cache), in_hbm(value_cache), theirs)


def lanes(block, j):
    return block[:, 128 * j : 128 * j + 128].astype(jnp.float32)


def square_sums(blocks, total):
    for block in blocks:
        for j in range(block.shape[1] // 128):
            v = lanes(block, j)
            total = total + v * v
    return total


def row_factors(squares, features):
    mean = jnp.sum(squares, axis=1, keepdims=True) * (1.0 / features)
    return lax.rsqrt(mean + epsilon)


def normed_block(block, factors, gain_row):
    return jnp.concatenate(
        [
            (lanes(block, j) * factors * gain_row[:, 128 * j : 128 * j + 128]).astype(jnp.bfloat16)
            for j in range(block.shape[1] // 128)
        ],
        axis=1,
    )


def in_hbm(array):
    return pltpu.with_memory_space_constraint(array, pltpu.HBM)


def load_kernel(ids, wq, wkv, out, sems):
    count, width, _ = out.shape
    copies = []
    for i in range(count):
        rows = pl.ds(pl.multiple_of(ids[i] * width, width), width)
        for j, weight in enumerate((wq, wkv)):
            copies.append(
                pltpu.make_async_copy(
                    weight.at[rows, :], out.at[i, :, pl.ds(j * HD, HD)], sems.at[j, i]
                )
            )
            copies[-1].start()
    for copy in copies:
        copy.wait()


def load_weights(ids, wq, wkv, width):
    return pl.pallas_call(
        load_kernel,
        out_shape=jax.ShapeDtypeStruct((16, width, 2 * HD), jnp.bfloat16),
        in_specs=[SMEM] + [HBM] * 2,
        out_specs=VMEM,
        scratch_shapes=[pltpu.SemaphoreType.DMA((2, 16))],
        compiler_params=pltpu.CompilerParams(vmem_limit_bytes=16 * MIB),
        cost_estimate=pl.CostEstimate(flops=0, bytes_accessed=16 * MIB, transcendentals=0),
        name="load_weights",
    )(ids, in_hbm(wq), in_hbm(wkv))


def all_factors(blocks):
    total = square_sums(blocks, jnp.zeros((TOKENS, 128), jnp.float32))
    return row_factors(total, 16 * blocks[0].shape[1])


def project_kernel(ids, *refs):
    blocks, refs = refs[:16], refs[16:]
    gain, weights, cosine, sine, kv_cos, kv_sin = refs[:6]
    q_keep, q_send, fresh = refs[6:]
    factors = all_factors(blocks)
    total = jnp.zeros((TOKENS, 2 * HD), jnp.float32)
    for i in range(16):
        normed = normed_block(blocks[i], factors, gain[ids[i]])
        total = total + jnp.dot(normed, weights[i], preferred_element_type=jnp.float32)
    q, kv = total[:, :HD], total[:, HD:]
    q = (q * cosine[...] + pltpu.roll(q, HD // 2, 1) * sine[...]).astype(jnp.bfloat16)
    kv = (kv * kv_cos[...] + pltpu.roll(kv, HD // 2, 1) * kv_sin[...]).astype(jnp.bfloat16)
    core_one = ids[0] % 2 == 1
    q_keep[...] = jnp.where(core_one, q[SPAN:], q[:SPAN])
    q_send[...] = jnp.where(core_one, q[:SPAN], q[SPAN:])
    fresh[...] = kv


def project(ids, arrays, gain, weights, tables):
    return pl.pallas_call(
        project_kernel,
        out_shape=[jax.ShapeDtypeStruct((SPAN, HD), jnp.bfloat16)] * 2
        + [jax.ShapeDtypeStruct((TOKENS, HD), jnp.bfloat16)],
        in_specs=[SMEM] + [VMEM] * (len(arrays) + 6),
        out_specs=[VMEM] * 3,
        compiler_params=pltpu.CompilerParams(vmem_limit_bytes=24 * MIB),
        cost_estimate=pl.CostEstimate(
            flops=2 * TOKENS * weights.size, bytes_accessed=12 * MIB, transcendentals=0
        ),
        name="norm_project",
    )(ids, *arrays, gain, weights, *tables)


def share_copies(to, first, weight, weight_other, out, sems):
    count, _, width = out.shape
    copies = []
    for i in range(count):
        columns = pl.ds(pl.multiple_of(to[first + i] * width, width), width)
        pair = [
            pltpu.make_async_copy(part.at[:, columns], out.at[i, pl.ds(j * HD, HD), :], sems.at[j, i])
            for j, part in enumerate((weight, weight_other))
        ]
        for copy in pair:
            copy.start()
        copies.append(pair)
    return copies


def cache_rows(cache, which):
    keep, came, rest = cache[0], cache[1], cache[2:]
    groups = [part[0, c, which] for part in (keep, came) for c in range(2)]
    groups += [part[x, c, which] for part in rest for x in range(2) for c in range(2)]
    return jnp.concatenate(groups, axis=0)


CONTRACT = (((1,), (1,)), ((), ()))


def first_weights_kernel(to, weight, weight_other, out, sems):
    for pair in share_copies(to, 0, weight, weight_other, out, sems):
        for copy in pair:
            copy.wait()


def load_first(to, weight, weight_other, count):
    return pl.pallas_call(
        first_weights_kernel,
        out_shape=jax.ShapeDtypeStruct((count, 2 * HD, weight.shape[1] // 16), jnp.bfloat16),
        in_specs=[SMEM] + [HBM] * 2,
        out_specs=VMEM,
        scratch_shapes=[pltpu.SemaphoreType.DMA((2, count))],
        compiler_params=pltpu.CompilerParams(vmem_limit_bytes=8 * MIB),
        cost_estimate=pl.CostEstimate(flops=0, bytes_accessed=2 * MIB, transcendentals=0),
        name="load_first",
    )(to, in_hbm(weight), weight_other)


def scores_kernel(info, q, q_other, *refs):
    cache, scores = refs[:5], refs[5]
    core, rank = info[SEQS], info[SEQS + 1]
    queries = jnp.concatenate([q[...], q_other[...]], axis=0)
    old = lax.dot_general(
        queries, cache_rows(cache, 0), CONTRACT, preferred_element_type=jnp.float32
    )
    lane = lax.broadcasted_iota(jnp.int32, old.shape, 1)
    position = (rank ^ (lane // CTX_DEV)) * CTX_DEV + lane % CTX_DEV
    scores[...] = jnp.where(position < info[core], old * HD ** (-0.5), -1e30)


def cache_scores(info, q, q_other, cache):
    return pl.pallas_call(
        scores_kernel,
        out_shape=jax.ShapeDtypeStruct((TOKENS, 16 * CTX_DEV), jnp.float32),
        in_specs=[SMEM] + [VMEM] * 7,
        out_specs=VMEM,
        compiler_params=pltpu.CompilerParams(vmem_limit_bytes=16 * MIB),
        cost_estimate=pl.CostEstimate(flops=32 * MIB, bytes_accessed=MIB, transcendentals=0),
        name="cache_scores",
    )(info, q, q_other, *cache)


def attend_kernel(info, q, q_other, fresh_own, fresh_other, scores, *refs):
    cache, out = refs[:5], refs[5]
    core = info[SEQS]
    came = fresh_other[...]
    fresh_keys = jnp.where(core == 0, fresh_own[:SPAN, :], came)
    fresh_values = jnp.where(core == 0, came, fresh_own[SPAN:, :])
    queries = jnp.concatenate([q[...], q_other[...]], axis=0)
    old = scores[...]
    valid = old > -1e29
    fresh = lax.dot_general(
        queries, fresh_keys, CONTRACT, preferred_element_type=jnp.float32
    ) * HD ** (-0.5)
    place = lax.broadcasted_iota(jnp.int32, fresh.shape, 0) % SPAN
    causal = place >= lax.broadcasted_iota(jnp.int32, fresh.shape, 1)
    fresh = jnp.where(causal, fresh, -1e30)
    most = jnp.maximum(jnp.max(old, axis=1, keepdims=True), jnp.max(fresh, axis=1, keepdims=True))
    old_weights = jnp.where(valid, jnp.exp(old - most), 0.0)
    fresh_weights = jnp.where(causal, jnp.exp(fresh - most), 0.0)
    totals = jnp.sum(old_weights, axis=1, keepdims=True) + jnp.sum(
        fresh_weights, axis=1, keepdims=True
    )
    summed = jnp.dot(
        old_weights.astype(jnp.bfloat16), cache_rows(cache, 1), preferred_element_type=jnp.float32
    ) + jnp.dot(
        fresh_weights.astype(jnp.bfloat16), fresh_values, preferred_element_type=jnp.float32
    )
    attn = (summed / totals).astype(jnp.bfloat16)
    out[:, :HD] = attn[:SPAN]
    out[:, HD:] = attn[SPAN:]


def attend(info, q, q_other, fresh_own, fresh_other, scores, cache):
    return pl.pallas_call(
        attend_kernel,
        out_shape=jax.ShapeDtypeStruct((SPAN, 2 * HD), jnp.bfloat16),
        in_specs=[SMEM] + [VMEM] * 10,
        out_specs=VMEM,
        compiler_params=pltpu.CompilerParams(vmem_limit_bytes=16 * MIB),
        cost_estimate=pl.CostEstimate(
            flops=48 * MIB, bytes_accessed=2 * MIB, transcendentals=TOKENS * 1088
        ),
        name="attend",
    )(info, q, q_other, fresh_own, fresh_other, scores, *cache)


def both_heads(core, attn, attn_other):
    mine = attn[...]
    theirs = jnp.concatenate([attn_other[:, HD:], attn_other[:, :HD]], axis=1)
    core_one = core[0] == 1
    return jnp.concatenate(
        [jnp.where(core_one, theirs, mine), jnp.where(core_one, mine, theirs)], axis=0
    )


def first_shares_kernel(core, attn, attn_other, weights, *outs):
    rows = both_heads(core, attn, attn_other)
    for i, out in enumerate(outs):
        out[...] = jnp.dot(rows, weights[i], preferred_element_type=jnp.float32).astype(out.dtype)


def first_shares(shares, core, attn, attn_other, weights):
    count, _, width = weights.shape
    out_shape = [jax.ShapeDtypeStruct((TOKENS, width), jnp.bfloat16)] * count
    arrays = pl.pallas_call(
        first_shares_kernel,
        out_shape=out_shape,
        in_specs=[SMEM] + [VMEM] * 3,
        out_specs=[VMEM] * len(out_shape),
        compiler_params=pltpu.CompilerParams(vmem_limit_bytes=16 * MIB),
        cost_estimate=pl.CostEstimate(
            flops=2 * TOKENS * weights.size, bytes_accessed=count * MIB, transcendentals=0
        ),
        name="first_shares",
    )(core, attn, attn_other, weights)
    return dict(zip(shares, arrays))


def more_shares_kernel(first, core, to, attn, attn_other, weight, weight_other, *refs):
    outs, (weights, sems) = refs[:-2], refs[-2:]
    copies = share_copies(to, first, weight, weight_other, weights, sems)
    rows = both_heads(core, attn, attn_other)
    for i, out in enumerate(outs):
        for copy in copies[i]:
            copy.wait()
        out[...] = jnp.dot(rows, weights[i], preferred_element_type=jnp.float32)


def more_shares(core, to, attn, attn_other, weight, weight_other, first, last):
    count, width = last - first, weight.shape[1] // 16
    out_shape = [jax.ShapeDtypeStruct((TOKENS, width), jnp.float32)] * count
    arrays = pl.pallas_call(
        functools.partial(more_shares_kernel, first),
        out_shape=out_shape,
        in_specs=[SMEM] * 2 + [VMEM] * 2 + [HBM] * 2,
        out_specs=[VMEM] * len(out_shape),
        scratch_shapes=[
            pltpu.VMEM((count, 2 * HD, width), jnp.bfloat16),
            pltpu.SemaphoreType.DMA((2, count)),
        ],
        compiler_params=pltpu.CompilerParams(vmem_limit_bytes=16 * MIB),
        cost_estimate=pl.CostEstimate(
            flops=4 * TOKENS * HD * width * count,
            bytes_accessed=count * MIB,
            transcendentals=0,
        ),
        name="shares_%d" % first,
    )(core, to, attn, attn_other, in_hbm(weight), weight_other)
    return dict(zip(SHARES[first:last], arrays))


def squares_kernel(*refs):
    refs[-1][...] = square_sums(refs[:-1], jnp.zeros((TOKENS, 128), jnp.float32))


def squares_of(blocks):
    return pl.pallas_call(
        squares_kernel,
        out_shape=jax.ShapeDtypeStruct((TOKENS, 128), jnp.float32),
        in_specs=[VMEM] * len(blocks),
        out_specs=VMEM,
        compiler_params=pltpu.CompilerParams(vmem_limit_bytes=16 * MIB),
        cost_estimate=pl.CostEstimate(
            flops=4 * MIB, bytes_accessed=len(blocks) * MIB // 4, transcendentals=0
        ),
        name="squares",
    )(*blocks)


def final_kernel(ids, *refs):
    blocks, refs = refs[:16], refs[16:]
    squares, gain, out, staged, sems = refs
    width = staged.shape[2]
    factors = row_factors(square_sums(blocks[15:], squares[...]), 16 * width)
    copies = []
    for i in range(16):
        staged[i] = normed_block(blocks[i], factors, gain[ids[i]])
        copy = pltpu.make_async_copy(
            staged.at[i],
            out.at[:, pl.ds(pl.multiple_of(ids[i] * width, width), width)],
            sems.at[i],
        )
        copy.start()
        copies.append(copy)
    for copy in copies:
        copy.wait()


def final_norm(ids, arrays, squares, gain):
    width = arrays[0].shape[1]
    return pl.pallas_call(
        final_kernel,
        out_shape=jax.ShapeDtypeStruct((TOKENS, 16 * width), jnp.bfloat16),
        in_specs=[SMEM] + [VMEM] * (len(arrays) + 2),
        out_specs=HBM,
        scratch_shapes=[
            pltpu.VMEM((16, TOKENS, width), jnp.bfloat16),
            pltpu.SemaphoreType.DMA((16,)),
        ],
        compiler_params=pltpu.CompilerParams(vmem_limit_bytes=24 * MIB),
        cost_estimate=pl.CostEstimate(
            flops=16 * MIB, bytes_accessed=12 * MIB, transcendentals=0
        ),
        name="final_norm",
    )(ids, *arrays, squares, gain)


def per_device_ring(
    residual, attn_gain, ffn_gain, q_weight, kv_weight, o_weight, key_cache, value_cache, prefix
):
    rank = lax.axis_index("tp")
    core = rank % 2
    width = residual.shape[1]
    ids = gathered_ids(rank)
    to = share_ids(rank)
    core_id, rank_id = core[None].astype(jnp.int32), rank[None].astype(jnp.int32)
    info = jnp.concatenate([prefix, core_id, rank_id])

    weight_other = send(o_weight, SWAP)
    parts = split_cache(key_cache, value_cache, rank, rank_id)
    mine, theirs = ring_gather(residual, weight_other, direct=True)
    weights = load_weights(ids, q_weight, kv_weight, width)
    cache = move_cache(parts)

    positions = (prefix[:, None] + jnp.arange(SPAN, dtype=jnp.int32)[None, :]).reshape(-1)
    cosine, sine = rope_tables(positions)
    cosine = jnp.concatenate([cosine, cosine], axis=1)
    sine = jnp.concatenate([-sine, sine], axis=1)
    holds_keys = rank < KVH
    tables = (cosine, sine, jnp.where(holds_keys, cosine, 1.0), jnp.where(holds_keys, sine, 0.0))

    gain = attn_gain.reshape(16, 1, width).astype(jnp.float32)
    mine[0] = after(mine[0], cache[1])
    q_keep, q_send, fresh = project(ids, mine + theirs, gain, weights, tables)
    q_other = send(q_send, SWAP)
    fresh_own = send(fresh, FRESH)
    fresh_other = send(jnp.where(core == 0, fresh_own[SPAN:], fresh_own[:SPAN]), SWAP)
    first_weights = load_first(after(to, fresh), o_weight, weight_other, 2)
    scores = cache_scores(info, after(q_keep, first_weights), q_other, cache)
    attn = attend(info, q_keep, q_other, fresh_own, fresh_other, scores, cache)
    attn_other = send(attn, SWAP)

    shares = first_shares(SHARES[:2], core_id, attn, attn_other, first_weights)
    shares.update(
        more_shares(core_id, to, attn, attn_other, o_weight, weight_other, 2, len(SHARES))
    )
    one_way, other_way = ring_sum(shares)
    projected = shares[0, 0] + one_way.astype(jnp.float32) + other_way.astype(jnp.float32)
    hidden = (residual.astype(jnp.float32) + projected).astype(jnp.bfloat16)

    mine, theirs = ring_gather(hidden)
    gain = ffn_gain.reshape(16, 1, width).astype(jnp.float32)
    return final_norm(ids, mine + theirs, squares_of((mine + theirs)[:15]), gain)


def per_device(
    residual, attn_gain, ffn_gain, q_weight, kv_weight, o_weight, key_cache, value_cache, prefix
):
    tp_count = lax.axis_size("tp")
    tp_rank = lax.axis_index("tp")
    heads_all = HQ_DEV * tp_count
    group_size = heads_all // KVH
    token_count = SEQS * SPAN
    score_scale = HD ** (-0.5)
    whole_rows = lax.all_gather(residual, "tp", axis=1, tiled=True)
    normed = rms_rows(whole_rows, attn_gain).astype(jnp.bfloat16)
    positions = (prefix[:, None] + jnp.arange(SPAN, dtype=jnp.int32)[None, :]).reshape(-1)
    queries = jnp.dot(normed, q_weight, preferred_element_type=jnp.float32).reshape(
        token_count, HQ_DEV, HD
    )
    queries = rotate(queries, positions).astype(jnp.bfloat16)
    kv_part = jnp.dot(normed, kv_weight, preferred_element_type=jnp.float32)
    kv_whole = lax.all_gather(kv_part, "tp", axis=1, tiled=True)
    new_keys = rotate(kv_whole[:, : KVH * HD].reshape(token_count, KVH, HD), positions).astype(
        jnp.bfloat16
    )
    new_values = kv_whole[:, KVH * HD :].reshape(token_count, KVH, HD).astype(jnp.bfloat16)
    head_ids = tp_rank * HQ_DEV + jnp.arange(HQ_DEV, dtype=jnp.int32)
    own_kv = head_ids // group_size
    own_keys = jnp.take(new_keys, own_kv, axis=1).reshape(SEQS, SPAN, HQ_DEV, HD)
    own_values = jnp.take(new_values, own_kv, axis=1).reshape(SEQS, SPAN, HQ_DEV, HD)
    own_queries = queries.reshape(SEQS, SPAN, HQ_DEV, HD)
    causal = (jnp.arange(SPAN)[:, None] >= jnp.arange(SPAN)[None, :])[None, None]
    fresh_scores = (
        jnp.einsum("schd,skhd->shck", own_queries, own_keys, preferred_element_type=jnp.float32)
        * score_scale
    )
    fresh_scores = jnp.where(causal, fresh_scores, -1e30)
    fresh_max = fresh_scores.max(-1)
    gathered = lax.all_gather(queries.reshape(token_count, HQ_DEV * HD), "tp", axis=1, tiled=True)
    queries_all = gathered.reshape(SEQS, SPAN, KVH, group_size, HD)
    keys_local = key_cache.reshape(SEQS, CTX_DEV, KVH, HD)
    values_local = value_cache.reshape(SEQS, CTX_DEV, KVH, HD)
    local_scores = (
        jnp.einsum("sckgd,sjkd->skgcj", queries_all, keys_local, preferred_element_type=jnp.float32)
        * score_scale
    )
    first_slot = tp_rank * CTX_DEV
    is_valid = ((first_slot + jnp.arange(CTX_DEV, dtype=jnp.int32))[None, :] < prefix[:, None])[
        :, None, None, None, :
    ]
    local_scores = jnp.where(is_valid, local_scores, -1e30)
    local_max = local_scores.max(-1)
    local_weights = jnp.where(is_valid, jnp.exp(local_scores - local_max[..., None]), 0.0)
    local_total = local_weights.sum(-1)
    local_sum = jnp.einsum(
        "skgcj,sjkd->skgcd",
        local_weights.astype(jnp.bfloat16),
        values_local,
        preferred_element_type=jnp.float32,
    )
    sums_in, maxes_in, totals_in = (
        lax.all_to_all(
            local_sum.reshape(1, SEQS, heads_all, SPAN, HD),
            "tp",
            split_axis=2,
            concat_axis=0,
            tiled=True,
        ),
        lax.all_to_all(
            local_max.reshape(1, SEQS, heads_all, SPAN),
            "tp",
            split_axis=2,
            concat_axis=0,
            tiled=True,
        ),
        lax.all_to_all(
            local_total.reshape(1, SEQS, heads_all, SPAN),
            "tp",
            split_axis=2,
            concat_axis=0,
            tiled=True,
        ),
    )
    running_max = jnp.maximum(maxes_in.max(0), fresh_max)
    factors = jnp.exp(maxes_in - running_max[None])
    fresh_weights = jnp.where(causal, jnp.exp(fresh_scores - running_max[..., None]), 0.0)
    totals = (factors * totals_in).sum(0) + fresh_weights.sum(-1)
    summed = (factors[..., None] * sums_in).sum(0)
    summed = summed + jnp.einsum(
        "shck,skhd->shcd",
        fresh_weights.astype(jnp.bfloat16),
        own_values,
        preferred_element_type=jnp.float32,
    )
    attn = (summed / totals[..., None]).astype(jnp.bfloat16)
    attn = jnp.transpose(attn, (0, 2, 1, 3)).reshape(token_count, HQ_DEV * HD)
    share_part = lax.psum_scatter(
        lax.dot_general(
            o_weight, attn, (((0,), (1,)), ((), ())), preferred_element_type=jnp.float32
        ),
        "tp",
        scatter_dimension=0,
        tiled=True,
    )
    hidden = (residual.astype(jnp.float32) + share_part.T).astype(jnp.bfloat16)
    stream = lax.all_gather(hidden, "tp", axis=1, tiled=True)
    return rms_rows(stream, ffn_gain).astype(jnp.bfloat16)


def solution(mesh):
    return jax.shard_map(
        per_device_ring if mesh.shape["tp"] == 2 * CHIPS else per_device,
        mesh=mesh,
        in_specs=(
            P("replica", "tp"),
            P(),
            P(),
            P(None, "tp"),
            P(None, "tp"),
            P("tp", None),
            P("replica", "tp", None),
            P("replica", "tp", None),
            P("replica"),
        ),
        out_specs=P("replica", None),
        check_vma=False,
    )
```
